32 devices in a mesh: expert: 8 (over y, x, core), tensor: 4 (over z).
Axes of the slice: x: 2, y: 2, z: 4, core: 2. Of those that a mesh axis runs over, the one named last changes fastest.
Arguments:
- layer_in: bfloat16 [4096, 1024], P('expert'), may hold values from -6 to 6
- seq_lengths: int32 [8, 3], P('expert'), may hold values from 1 to 384, 512 in all within a row
- routes: int32 [4096, 2], P('expert'), may hold values from 0 to 7, all different within a row; in each aligned block of 512 rows (0 to 511, 512 to 1023, ...) at most 256 rows name the same one
- gain_attn: float32 [1024], replicated, may hold values from 0.5 to 1.5
- w_qkv: bfloat16 [1024, 8, 256], P(None, 'tensor'), may hold values from -0.25 to 0.25
- w_output: bfloat16 [1024, 1024], P('tensor'), may hold values from -0.5 to 0.5
- gain_ffn: float32 [1024], replicated, may hold values from 0.5 to 1.5
- w_router: bfloat16 [1024, 8], replicated, may hold values from -0.09375 to 0.09375
- w_in: bfloat16 [8, 2, 512, 1024], P('expert', None, 'tensor'), may hold values from -0.1875 to 0.1875
- w_out: bfloat16 [8, 512, 1024], P('expert', 'tensor'), may hold values from -1.5 to 1.5
- out_grad: bfloat16 [4096, 1024], P('expert'), may hold values from -6 to 6
Outputs:
- layer_out: bfloat16 [4096, 1024], P('expert')
- in_grad: bfloat16 [4096, 1024], P('expert')
- gain_attn_grad: float32 [1024], replicated
- w_qkv_grad: float32 [1024, 8, 256], P(None, 'tensor')
- w_output_grad: float32 [1024, 1024], P('tensor')
- gain_ffn_grad: float32 [1024], replicated
- w_router_grad: float32 [1024, 8], replicated
- w_in_grad: float32 [8, 2, 512, 1024], P('expert', None, 'tensor')
- w_out_grad: float32 [8, 512, 1024], P('expert', 'tensor')
The draws below stay inside these ranges and needn't reach their ends.
Inputs may be any that keep to these rules, and one draw needn't show every extreme that they name: `seq_lengths`: each row lists the sequence lengths of one device group in order; they sum to 512 and the longest of each row is 384. `routes`: each token names 2 different experts; among the tokens of one device group no expert is named by more than 256 tokens, and some expert reaches 256.
All inputs are finite; a program needn't handle non-finite values.
Results may differ from the reference program's by a relative error of at most 0.025.
Values may be sent and summed in bfloat16 or wider, within the bound.
No kernel may reach another device: no remote copies, remote signals or barrier semaphores. Data moves between devices by JAX's collectives and lax.ppermute only.
A program may use at most 192 MiB of HBM per device.

```python
import math
import jax
import jax.numpy as jnp
import numpy as np
from jax import lax

D = 1024
HEADS = 16
KV_HEADS = 8
HEAD_DIM = 64
FF_E = 512
TOK_DEV = 512
SEQS = 3
EXPERTS = 8
TOP = 2
CAP = 256
MOST_LEN = 384
GROUPS = 8
TOKENS = 4096


def level_of(stream_key, shape, pieces, smallest, top_value):
    level = 1.0
    for dim, shards_of in pieces:
        heights = jax.random.uniform(jax.random.fold_in(jax.random.fold_in(stream_key, 6), dim), (shards_of,), jnp.float32, smallest / len(pieces), top_value / len(pieces))
        level = level * jnp.repeat(jnp.exp(heights), shape[dim] // shards_of).reshape((-1,) + (1,) * (len(shape) - 1 - dim))
    return level


def split_up(amount, total, bound, skew):
    loads = [(1 << 20) // math.isqrt(rank ** skew) + 1 for rank in range(2, amount + 1)]
    surplus, counts = total - bound - (amount - 1), [1] * (amount - 1)
    while surplus > 0:
        candidates = [i for i in range(amount - 1) if counts[i] < bound]
        mass, budget = sum([loads[i] for i in candidates]), surplus
        for i in candidates:
            extra = min(bound - counts[i], max(1, budget * loads[i] // mass), surplus)
            counts[i] = counts[i] + extra
            surplus = surplus - extra
    return np.array([bound] + counts)


def uneven(rng, number_of, total, bound, lean):
    if number_of == 2:
        one = jax.random.randint(rng, (), max(1, total - bound), min(bound, total - 1) + 1)
        return jnp.stack([one, total - one])
    sizes = jnp.asarray(split_up(number_of, total, bound, lean), jnp.int32)
    twos = (number_of - 1) // 2
    source_of, taker = sizes[1:1 + 2 * twos:2], sizes[2:2 + 2 * twos:2]
    room = jnp.minimum(source_of - 1, bound - taker)
    passed = jax.random.randint(jax.random.fold_in(rng, 1), (twos,), 0, 1 << 20) % (room + 1)
    sizes = sizes.at[1:1 + 2 * twos:2].set(source_of - passed).at[2:2 + 2 * twos:2].set(taker + passed)
    return sizes[jax.random.permutation(jax.random.fold_in(rng, 2), number_of)]


def assign_block(stream_key, own, number, rows, amount, top, bound, slope):
    sequence = jax.random.permutation(stream_key, amount)
    crowded, usual = load_shares(amount, rows * top, bound, slope, True), load_shares(amount, rows * top, bound, slope, False)
    places = jnp.arange(amount)

    def named(sizes, turn):
        used = int((sizes > 0).sum())
        fixed = max(1, used // 4)
        passed = fixed + (places - fixed + turn * (used - fixed)) % max(1, amount - fixed)
        return jnp.zeros((amount,), jnp.int32).at[sequence[jnp.where(places < fixed, places, passed)]].set(jnp.asarray(sizes, jnp.int32))

    sizes = jnp.where(number % 4 == 0, named(crowded, number // 4), named(usual, number - number // 4 - 1))
    mixed = jax.random.permutation(jax.random.fold_in(own, 3), amount)
    source_of, sink = mixed[0:amount // 2 * 2:2], mixed[1:amount // 2 * 2:2]
    slack = jnp.minimum(sizes[source_of] - 1, bound - sizes[sink]) // 2
    slack = jnp.where((source_of == sequence[0]) | (sink == sequence[0]) | (sizes[sink] == 0), 0, jnp.maximum(slack, 0))
    passed = jax.random.randint(jax.random.fold_in(own, 4), (amount // 2,), 0, 1 << 20) % (slack + 1)
    sizes = sizes.at[source_of].add(-passed).at[sink].add(passed)
    members = jnp.searchsorted(jnp.cumsum(sizes), jnp.arange(rows * top), side="right").astype(jnp.int32)
    table = members.reshape(top, rows).T
    table = table[jax.random.permutation(jax.random.fold_in(own, 1), rows)]
    turn = jax.random.randint(jax.random.fold_in(own, 2), (rows, 1), 0, top)
    return jnp.take_along_axis(table, (jnp.arange(top)[None, :] + turn) % top, axis=1)


def load_shares(count, total, limit, lean, full):
    weights = [(1 << 20) // math.isqrt(standing ** lean) + 1 for standing in range(1, count + 1)]
    largest = limit if full else min(limit, max(-(-total // count), total * weights[0] // sum(weights)))
    least = 1 if total - largest >= count - 1 else 0
    holding, rest = [largest] + [least] * (count - 1), total - largest - least * (count - 1)
    while rest > 0:
        free = [i for i in range(1, count) if holding[i] < largest] or [i for i in range(1, count) if holding[i] < limit]
        whole, budget = sum([weights[i] for i in free]), rest
        for i in free:
            extra = min(limit - holding[i], max(1, budget * weights[i] // whole), rest)
            holding[i] = holding[i] + extra
            rest = rest - extra
    return np.array(holding)


def scatter_about(rng, extent, width, bound, shards=(), held_as=jnp.bfloat16):
    result = width * jax.random.normal(rng, extent, jnp.float32)
    if shards:
        result = result * level_of(rng, extent, shards, -0.22, 0.18)
    return jnp.clip(result, -bound, bound).astype(held_as)


def setup_inputs(seed: int = 0) -> dict:
    streams_of = jax.random.split(jax.random.key(seed), 12)
    layer_in = scatter_about(streams_of[0], (TOKENS, D), 1.0, 6.0, ((0, 8),))
    seq_lengths = jax.vmap(lambda own: uneven(own, SEQS, TOK_DEV, MOST_LEN, 1))(jax.random.split(streams_of[1], GROUPS)).reshape((GROUPS, SEQS)).astype(jnp.int32)
    routes_keys = jax.random.split(jax.random.fold_in(streams_of[2], 1), TOKENS // TOK_DEV)
    routes_turns = jax.random.permutation(jax.random.fold_in(streams_of[2], 3), TOKENS // TOK_DEV)
    routes = jax.vmap(lambda own, number: assign_block(jax.random.fold_in(streams_of[2], 2), own, number, TOK_DEV, EXPERTS, TOP, CAP, 1))(routes_keys, routes_turns).reshape((TOKENS, TOP))
    gain_attn = jnp.clip(1.0 + 0.1 * jax.random.normal(streams_of[3], (D,), jnp.float32), 0.5, 1.5)
    w_qkv = scatter_about(streams_of[4], (D, KV_HEADS, (HEADS // KV_HEADS + 2) * HEAD_DIM), (D // 2) ** -0.5, 0.25, ((1, 4),))
    w_output = scatter_about(streams_of[5], (HEADS * HEAD_DIM, D), (HEADS * HEAD_DIM // 8) ** -0.5, 0.5, ((0, 4),))
    gain_ffn = jnp.clip(1.0 + 0.1 * jax.random.normal(streams_of[6], (D,), jnp.float32), 0.5, 1.5)
    w_router = scatter_about(streams_of[7], (D, EXPERTS), (4 * D) ** -0.5, 0.09375)
    w_in = scatter_about(streams_of[8], (EXPERTS, 2, FF_E, D), D ** -0.5, 0.1875, ((0, 8), (2, 4)))
    w_out = scatter_about(streams_of[9], (EXPERTS, FF_E, D), (FF_E // 32) ** -0.5, 1.5, ((0, 8), (1, 4)))
    out_grad = scatter_about(streams_of[10], (TOKENS, D), 1.0, 6.0, ((0, 8),))
    return {"layer_in": layer_in, "seq_lengths": seq_lengths, "routes": routes, "gain_attn": gain_attn, "w_qkv": w_qkv, "w_output": w_output, "gain_ffn": gain_ffn, "w_router": w_router, "w_in": w_in, "w_out": w_out, "out_grad": out_grad}


epsilon = 1e-06
rope_base = 10000.0
masked_out = -1e+30
precise = lax.Precision.HIGHEST

@jax.custom_vjp
def low(v):
    return lax.optimization_barrier(v.astype(jnp.bfloat16)).astype(jnp.float32)

@jax.custom_vjp
def low_back(v):
    return v

def low_keep(v):
    return (low(v), None)

def low_pass(kept, grad):
    return (grad,)

def back_keep(v):
    return (v, None)

def back_low(kept, grad):
    return (low(grad),)
low.defvjp(low_keep, low_pass)
low_back.defvjp(back_keep, back_low)

def rms_norm(values, gain_vec):
    inverse = lax.rsqrt(lax.optimization_barrier(jnp.mean(values * values, axis=-1, keepdims=True)) + epsilon)
    return values * inverse * gain_vec

def positions(lengths, token_count):
    seq_ends = jnp.cumsum(lengths, dtype=jnp.int32)
    row_index = jnp.arange(token_count, dtype=jnp.int32)
    segment = lax.optimization_barrier(jnp.sum((row_index[:, None] >= seq_ends[None, :]).astype(jnp.int32), axis=1, dtype=jnp.int32))
    seq_ids = jnp.arange(lengths.shape[0], dtype=jnp.int32)
    seq_start = lax.optimization_barrier(jnp.sum(jnp.where(segment[:, None] == seq_ids[None, :], (seq_ends - lengths)[None, :], 0), axis=1, dtype=jnp.int32))
    return (segment, row_index - seq_start)

def rope_tables(position, head_dim):
    half_dim = head_dim // 2
    inverse_freq = jnp.exp(jnp.arange(half_dim, dtype=jnp.float32) * (-2.0 * math.log(rope_base) / head_dim))
    angles = position.astype(jnp.float32)[:, None] * inverse_freq[None, :]
    cosine = jnp.cos(angles)
    sine_tab = jnp.sin(angles)
    return (jnp.concatenate([cosine, cosine], 1), jnp.concatenate([sine_tab, sine_tab], 1))

def rotate(values, cosine, sine_tab):
    half_dim = values.shape[-1] // 2
    turned = jnp.concatenate([-values[..., half_dim:], values[..., :half_dim]], -1)
    return values * cosine + turned * sine_tab

def slot_table(routes_part, experts_all, capacity):
    flat_routes = routes_part.reshape(-1)
    hot_table = (flat_routes[:, None] == jnp.arange(experts_all, dtype=jnp.int32)[None, :]).astype(jnp.int32)
    earlier = jnp.cumsum(hot_table, axis=0, dtype=jnp.int32) - hot_table
    slot_of = lax.optimization_barrier(jnp.sum(earlier * hot_table, axis=1, dtype=jnp.int32))
    assign_ids = jnp.arange(flat_routes.shape[0], dtype=jnp.int32)
    return jnp.full((experts_all, capacity), -1, jnp.int32).at[flat_routes, slot_of].set(assign_ids)

def attend_group(rows_in, lengths, gain_one, qkv_weight, output_weight):
    token_count = rows_in.shape[0]
    group_size = HEADS // KV_HEADS
    segment, position = positions(lengths, token_count)
    cosine, sine_tab = rope_tables(position, HEAD_DIM)
    normed = low(rms_norm(rows_in, gain_one))
    projected = low_back(jnp.dot(normed, qkv_weight.reshape(D, -1), precision=precise))
    projected = projected.reshape(token_count, KV_HEADS, group_size + 2, HEAD_DIM)
    queries = low(rotate(jnp.transpose(projected[:, :, :group_size], (1, 2, 0, 3)), cosine, sine_tab))
    key_rows = low(rotate(jnp.transpose(projected[:, :, group_size], (1, 0, 2)), cosine, sine_tab))
    values = low(jnp.transpose(projected[:, :, group_size + 1], (1, 0, 2)))
    scores = low_back(jnp.einsum('kgtd,ksd->kgts', queries, key_rows, precision=precise) * (1.0 / math.sqrt(HEAD_DIM)))
    row_index = jnp.arange(token_count, dtype=jnp.int32)
    allowed = (segment[:, None] == segment[None, :]) & (row_index[None, :] <= row_index[:, None])
    scores = jnp.where(allowed[None, None], scores, masked_out)
    probs = low(jax.nn.softmax(scores, axis=-1))
    attended = low_back(low(jnp.einsum('kgts,ksd->kgtd', probs, values, precision=precise)))
    heads_out = jnp.transpose(attended, (2, 0, 1, 3)).reshape(token_count, -1)
    return rows_in + low_back(jnp.dot(heads_out, output_weight, precision=precise))

def mix_experts(residual, routes, gain_two, router_weight, in_weight, out_weight):
    normed = low(rms_norm(residual, gain_two))
    logits = low_back(jnp.dot(normed, router_weight, precision=precise))
    picked = routes[:, :, None] == jnp.arange(EXPERTS, dtype=jnp.int32)[None, None, :]
    chosen = lax.optimization_barrier(jnp.sum(jnp.where(picked, logits[:, None, :], 0.0), -1))
    flat_gates = jax.nn.softmax(chosen, axis=-1).reshape(-1)
    local_tables = jax.vmap(lambda part_routes: slot_table(part_routes, EXPERTS, CAP))(routes.reshape(GROUPS, TOK_DEV * TOP))
    offsets = (jnp.arange(GROUPS, dtype=jnp.int32) * (TOK_DEV * TOP))[:, None, None]
    tables = jnp.where(local_tables >= 0, local_tables + offsets, -1)
    tables = jnp.transpose(tables, (1, 0, 2)).reshape(EXPERTS, GROUPS * CAP)

    def expert_step(running, packed):
        in_one, out_one, table_one = packed
        filled = table_one >= 0
        assign = jnp.where(filled, table_one, 0)
        token_of = assign // TOP
        copied = low_back(normed[token_of])
        hidden = low_back(jnp.dot(copied, in_one.reshape(2 * FF_E, D).T, precision=precise))
        active = low(jax.nn.silu(hidden[:, :FF_E]) * hidden[:, FF_E:])
        output = low_back(low(jnp.dot(active, out_one, precision=precise)))
        weight_col = jnp.where(filled, flat_gates[assign], 0.0)
        return (running + jax.ops.segment_sum(output * weight_col[:, None], token_of, num_segments=TOKENS), None)
    return lax.scan(jax.checkpoint(expert_step), jnp.zeros_like(residual), (in_weight, out_weight, tables))[0]

def reference(layer_in, seq_lengths, routes, gain_attn, w_qkv, w_output, gain_ffn, w_router, w_in, w_out, out_grad):

    def forward(inputs, gain_one, qkv_weight, output_weight, gain_two, router_weight, in_weight, out_weight):
        grouped = inputs.reshape(GROUPS, TOK_DEV, D)

        def group_attention(packed):
            return attend_group(packed[0], packed[1], gain_one, qkv_weight, output_weight)
        residual = lax.map(jax.checkpoint(group_attention), (grouped, seq_lengths)).reshape(TOKENS, D)
        return residual + mix_experts(residual, routes, gain_two, router_weight, in_weight, out_weight)
    floats = tuple((member.astype(jnp.float32) for member in (layer_in, gain_attn, w_qkv, w_output, gain_ffn, w_router, w_in, w_out)))
    layer_out, pullback = jax.vjp(forward, *floats)
    gradients = pullback(out_grad.astype(jnp.float32))
    return (layer_out.astype(jnp.bfloat16), gradients[0].astype(jnp.bfloat16), gradients[1], gradients[2], gradients[3], gradients[4], gradients[5], gradients[6], gradients[7])
```

```python
import math

import jax
import jax.numpy as jnp
from jax import lax
from jax.sharding import PartitionSpec as P

HEADS = 16
KV_HEADS = 8
HEAD_DIM = 64


epsilon = 1e-06
rope_base = 10000.0
masked_out = -1e30


def rms_forward(values, gain_vec):
    inverse = lax.rsqrt(jnp.mean(values * values, axis=-1, keepdims=True) + epsilon)
    return (values * inverse * gain_vec, inverse)


def rms_backward(values, inverse, gain_vec, upstream):
    normal = values * inverse
    scaled = upstream * gain_vec
    inner_mean = jnp.mean(scaled * normal, axis=-1, keepdims=True)
    return inverse * (scaled - normal * inner_mean)


def positions(lengths, token_count):
    seq_ends = jnp.cumsum(lengths, dtype=jnp.int32)
    row_index = jnp.arange(token_count, dtype=jnp.int32)
    segment = jnp.sum(
        (row_index[:, None] >= seq_ends[None, :]).astype(jnp.int32), axis=1, dtype=jnp.int32
    )
    seq_ids = jnp.arange(lengths.shape[0], dtype=jnp.int32)
    seq_start = jnp.sum(
        jnp.where(segment[:, None] == seq_ids[None, :], (seq_ends - lengths)[None, :], 0),
        axis=1,
        dtype=jnp.int32,
    )
    return (segment, row_index - seq_start)


def rope_tables(position, head_dim):
    half_dim = head_dim // 2
    inverse_freq = jnp.exp(
        jnp.arange(half_dim, dtype=jnp.float32) * (-2.0 * math.log(rope_base) / head_dim)
    )
    angles = position.astype(jnp.float32)[:, None] * inverse_freq[None, :]
    cosine = jnp.cos(angles)
    sine_tab = jnp.sin(angles)
    return (jnp.concatenate([cosine, cosine], 1), jnp.concatenate([sine_tab, sine_tab], 1))


def rotate(values, cosine, sine_tab):
    half_dim = values.shape[-1] // 2
    turned = jnp.concatenate([-values[..., half_dim:], values[..., :half_dim]], -1)
    return values * cosine + turned * sine_tab


def split_blocks(array_in, axis_at, block_count):
    dims_now = array_in.shape
    regrouped = array_in.reshape(
        dims_now[:axis_at]
        + (block_count, dims_now[axis_at] // block_count)
        + dims_now[axis_at + 1 :]
    )
    return jnp.moveaxis(regrouped, axis_at, 0)


def join_blocks(array_in, axis_at):
    regrouped = jnp.moveaxis(array_in, 0, axis_at)
    dims_now = regrouped.shape
    return regrouped.reshape(
        dims_now[:axis_at] + (dims_now[axis_at] * dims_now[axis_at + 1],) + dims_now[axis_at + 2 :]
    )


def block_scores(query_block, key_rows, segment_rows, row_start, segment, scaling):
    block_rows = query_block.shape[2]
    scores_raw = (
        jnp.einsum("kgbd,ksd->kgbs", query_block, key_rows, preferred_element_type=jnp.float32)
        * scaling
    )
    query_index = row_start + jnp.arange(block_rows, dtype=jnp.int32)
    key_index = jnp.arange(key_rows.shape[1], dtype=jnp.int32)
    allowed = (segment_rows[:, None] == segment[None, :]) & (
        key_index[None, :] <= query_index[:, None]
    )
    return jnp.where(allowed[None, None], scores_raw, masked_out)


def attention_forward(queries, key_rows, values, segment, scaling, block_size):
    block_count = queries.shape[2] // block_size
    starts_all = jnp.arange(block_count, dtype=jnp.int32) * block_size

    def one_block(packed):
        query_block, segment_rows, row_start = packed
        scores = block_scores(query_block, key_rows, segment_rows, row_start, segment, scaling)
        top_score = jnp.max(scores, -1)
        exponent = jnp.exp(scores - top_score[..., None])
        row_total = jnp.sum(exponent, -1)
        probs = (exponent / row_total[..., None]).astype(jnp.bfloat16)
        output = jnp.einsum("kgbs,ksd->kgbd", probs, values, preferred_element_type=jnp.float32)
        return (output.astype(jnp.bfloat16), top_score, row_total)

    outputs, top_blocks, total_blocks = lax.map(
        one_block,
        (
            split_blocks(queries, 2, block_count),
            segment.reshape(block_count, block_size),
            starts_all,
        ),
    )
    return (join_blocks(outputs, 2), join_blocks(top_blocks, 2), join_blocks(total_blocks, 2))


def attention_backward(
    queries, key_rows, values, heads_grad, segment, top_kept, total_kept, scaling, block_size
):
    block_count = queries.shape[2] // block_size
    starts_all = jnp.arange(block_count, dtype=jnp.int32) * block_size

    def one_block(running, packed):
        key_acc, value_acc = running
        query_block, grad_block, segment_rows, row_start, top_block, total_block = packed
        scores = block_scores(query_block, key_rows, segment_rows, row_start, segment, scaling)
        probs = jnp.exp(scores - top_block[..., None]) / total_block[..., None]
        probs_low = probs.astype(jnp.bfloat16)
        value_acc = value_acc + jnp.einsum(
            "kgbs,kgbd->ksd", probs_low, grad_block, preferred_element_type=jnp.float32
        )
        prob_grad = jnp.einsum(
            "kgbd,ksd->kgbs", grad_block, values, preferred_element_type=jnp.float32
        )
        inner_sum = jnp.sum(probs * prob_grad, -1, keepdims=True)
        score_grad = (probs * (prob_grad - inner_sum)).astype(jnp.bfloat16)
        query_grad = (
            jnp.einsum("kgbs,ksd->kgbd", score_grad, key_rows, preferred_element_type=jnp.float32)
            * scaling
        )
        key_acc = (
            key_acc
            + jnp.einsum(
                "kgbs,kgbd->ksd", score_grad, query_block, preferred_element_type=jnp.float32
            )
            * scaling
        )
        return ((key_acc, value_acc), query_grad)

    empty = jnp.zeros(key_rows.shape, jnp.float32)
    packed_all = (
        split_blocks(queries, 2, block_count),
        split_blocks(heads_grad, 2, block_count),
        segment.reshape(block_count, block_size),
        starts_all,
        split_blocks(top_kept, 2, block_count),
        split_blocks(total_kept, 2, block_count),
    )
    (key_grad, value_grad), query_blocks = lax.scan(one_block, (empty, empty), packed_all)
    return (join_blocks(query_blocks, 2), key_grad, value_grad)


def on_device(
    layer_in,
    seq_lengths,
    routes,
    gain_attn,
    w_qkv,
    w_output,
    gain_ffn,
    w_router,
    w_in,
    w_out,
    out_grad,
):
    token_count, model_width = layer_in.shape
    kv_here = w_qkv.shape[1]
    group_size = HEADS // KV_HEADS
    scaling = 1.0 / math.sqrt(HEAD_DIM)
    block_size = min(512, token_count)
    w_output_all = lax.all_gather(w_output, "tensor", axis=0, tiled=True)
    w_gate_all = lax.all_gather(w_in[0, 0], "expert", axis=0, tiled=True)
    w_up_all = lax.all_gather(w_in[0, 1], "expert", axis=0, tiled=True)
    w_out_all = lax.all_gather(w_out[0], "expert", axis=0, tiled=True)
    segment, position = positions(seq_lengths[0], token_count)
    cosine, sine_tab = rope_tables(position, HEAD_DIM)
    inputs = layer_in.astype(jnp.float32)
    normed_one, inverse_one = rms_forward(inputs, gain_attn)
    normed_one_low = normed_one.astype(jnp.bfloat16)
    qkv_flat = w_qkv.reshape(model_width, -1)
    projected = jnp.dot(normed_one_low, qkv_flat, preferred_element_type=jnp.float32)
    projected = projected.reshape(token_count, kv_here, group_size + 2, HEAD_DIM)
    queries = rotate(
        jnp.transpose(projected[:, :, :group_size], (1, 2, 0, 3)), cosine, sine_tab
    ).astype(jnp.bfloat16)
    key_rows = rotate(
        jnp.transpose(projected[:, :, group_size], (1, 0, 2)), cosine, sine_tab
    ).astype(jnp.bfloat16)
    values = jnp.transpose(projected[:, :, group_size + 1], (1, 0, 2)).astype(jnp.bfloat16)
    attended, top_kept, total_kept = attention_forward(
        queries, key_rows, values, segment, scaling, block_size
    )
    heads_out = jnp.transpose(attended, (2, 0, 1, 3)).reshape(token_count, -1)
    heads_all = lax.all_gather(heads_out, "tensor", axis=1, tiled=True)
    branch_here = jnp.dot(heads_all, w_output_all, preferred_element_type=jnp.float32)
    residual = inputs + branch_here
    normed_two, inverse_two = rms_forward(residual, gain_ffn)
    normed_low = normed_two.astype(jnp.bfloat16)
    experts_all = w_router.shape[1]
    unit_count = w_out.shape[1]
    logits = jnp.dot(normed_low, w_router, preferred_element_type=jnp.float32)
    expert_ids = jnp.arange(experts_all, dtype=jnp.int32)
    picked = jnp.any(routes[:, :, None] == expert_ids[None, None, :], axis=1)
    picked_logits = jnp.where(picked, logits, masked_out)
    top_logit = jnp.max(picked_logits, -1, keepdims=True)
    weight = jnp.where(picked, jnp.exp(picked_logits - top_logit), 0.0)
    gates = weight / jnp.sum(weight, -1, keepdims=True)

    def by_unit(per_expert):
        return jnp.broadcast_to(
            per_expert[:, :, None], (token_count, experts_all, unit_count)
        ).reshape(token_count, -1)

    def over_units(per_unit):
        return jnp.sum(per_unit.reshape(token_count, experts_all, unit_count), -1)

    def times_transposed(left, right):
        return lax.dot_general(
            left, right, (((1,), (1,)), ((), ())), preferred_element_type=jnp.float32
        )

    def transposed_times(left, right):
        return lax.dot_general(
            left, right, (((0,), (0,)), ((), ())), preferred_element_type=jnp.float32
        )

    gates_wide = by_unit(gates)
    gate_vals = times_transposed(normed_low, w_gate_all)
    up_vals = times_transposed(normed_low, w_up_all)
    plain_grad = times_transposed(out_grad, w_out_all)
    sig_vals = jax.nn.sigmoid(gate_vals)
    silu_vals = gate_vals * sig_vals
    active = silu_vals * up_vals
    scaled_active = (active * gates_wide).astype(jnp.bfloat16)
    active_grad = plain_grad * gates_wide
    gate_pre = (
        active_grad * up_vals * (sig_vals * (1.0 + gate_vals * (1.0 - sig_vals)))
    ).astype(jnp.bfloat16)
    up_pre = (active_grad * silu_vals).astype(jnp.bfloat16)
    gate_grad_part = over_units(active * plain_grad)
    logit_part = (
        gates * (gate_grad_part - jnp.sum(gates * gate_grad_part, -1, keepdims=True))
    ).astype(jnp.bfloat16)
    normed_two_part = (
        jnp.dot(gate_pre, w_gate_all, preferred_element_type=jnp.float32)
        + jnp.dot(up_pre, w_up_all, preferred_element_type=jnp.float32)
        + times_transposed(logit_part, w_router)
    )
    normed_two_grad = lax.psum(normed_two_part.astype(jnp.bfloat16), "tensor").astype(jnp.float32)
    mixture_part = jnp.dot(scaled_active, w_out_all, preferred_element_type=jnp.float32)
    mixture = lax.psum(mixture_part.astype(jnp.bfloat16), "tensor").astype(jnp.float32)
    layer_here = (residual + mixture).astype(jnp.bfloat16)

    def to_owner(partial):
        return lax.psum_scatter(
            partial.astype(jnp.bfloat16), "expert", scatter_dimension=0, tiled=True
        ).astype(jnp.float32)

    w_gate_grad = to_owner(transposed_times(gate_pre, normed_low))
    w_up_grad = to_owner(transposed_times(up_pre, normed_low))
    w_in_grad = jnp.stack([w_gate_grad, w_up_grad])[None]
    w_out_grad = to_owner(transposed_times(scaled_active, out_grad))[None]
    router_part = transposed_times(logit_part, normed_low)
    normal_two = residual * inverse_two
    gain_ffn_part = jnp.sum(normed_two_part * normal_two, axis=0)
    upstream = out_grad.astype(jnp.float32)
    residual_part = rms_backward(residual, inverse_two, gain_ffn, normed_two_grad)
    residual_grad = upstream + residual_part
    branch_here_grad = residual_grad.astype(jnp.bfloat16)
    w_output_grad = lax.dot_general(
        heads_out, branch_here_grad, (((0,), (0,)), ((), ())), preferred_element_type=jnp.float32
    )
    heads_flat = lax.dot_general(
        branch_here_grad, w_output, (((1,), (1,)), ((), ())), preferred_element_type=jnp.float32
    ).astype(jnp.bfloat16)
    heads_grad = jnp.transpose(
        heads_flat.reshape(token_count, kv_here, group_size, HEAD_DIM), (1, 2, 0, 3)
    )
    query_grad, key_grad, value_grad = attention_backward(
        queries, key_rows, values, heads_grad, segment, top_kept, total_kept, scaling, block_size
    )
    query_grad = rotate(query_grad, cosine, -sine_tab)
    key_grad = rotate(key_grad, cosine, -sine_tab)
    projected_grad = jnp.concatenate(
        [
            jnp.transpose(query_grad, (2, 0, 1, 3)),
            jnp.transpose(key_grad, (1, 0, 2))[:, :, None],
            jnp.transpose(value_grad, (1, 0, 2))[:, :, None],
        ],
        2,
    )
    projected_grad = projected_grad.reshape(token_count, -1).astype(jnp.bfloat16)
    w_qkv_grad = lax.dot_general(
        normed_one_low, projected_grad, (((0,), (0,)), ((), ())), preferred_element_type=jnp.float32
    ).reshape(w_qkv.shape)
    normed_one_part = lax.dot_general(
        projected_grad, qkv_flat, (((1,), (1,)), ((), ())), preferred_element_type=jnp.float32
    )
    gain_attn_part = jnp.sum(normed_one_part * (inputs * inverse_one), axis=0)
    normed_one_grad = lax.psum(normed_one_part.astype(jnp.bfloat16), "tensor").astype(jnp.float32)
    input_part = rms_backward(inputs, inverse_one, gain_attn, normed_one_grad)
    in_here = (residual_grad + input_part).astype(jnp.bfloat16)
    qkv_summed = lax.psum(w_qkv_grad.astype(jnp.bfloat16), "expert").astype(jnp.float32)
    output_summed = lax.psum(w_output_grad.astype(jnp.bfloat16), "expert").astype(jnp.float32)
    small = jnp.concatenate([router_part, gain_ffn_part[None], gain_attn_part[None]])
    small = lax.psum(small, ("expert", "tensor"))
    return (
        layer_here,
        in_here,
        small[experts_all + 1],
        qkv_summed,
        output_summed,
        small[experts_all],
        jnp.transpose(small[:experts_all]),
        w_in_grad,
        w_out_grad,
    )


def solution(mesh):
    placed = (
        P("expert", None),
        P("expert", None),
        P("expert", None),
        P(),
        P(None, "tensor", None),
        P("tensor", None),
        P(),
        P(),
        P("expert", None, "tensor", None),
        P("expert", "tensor", None),
        P("expert", None),
    )
    return jax.shard_map(
        on_device,
        mesh=mesh,
        in_specs=placed,
        out_specs=(
            P("expert", None),
            P("expert", None),
            P(),
            P(None, "tensor", None),
            P("tensor", None),
            P(),
            P(),
            P("expert", None, "tensor", None),
            P("expert", "tensor", None),
        ),
        check_vma=False,
    )
```

```python
import math

import jax
import jax.numpy as jnp
from jax import lax
from jax.sharding import PartitionSpec as P

HEADS = 16
KV_HEADS = 8
HEAD_DIM = 64


epsilon = 1e-06
rope_base = 10000.0
masked_out = -1e30


def rms_forward(values, gain_vec):
    inverse = lax.rsqrt(jnp.mean(values * values, axis=-1, keepdims=True) + epsilon)
    return (values * inverse * gain_vec, inverse)


def rms_backward(values, inverse, gain_vec, upstream):
    normal = values * inverse
    scaled = upstream * gain_vec
    inner_mean = jnp.mean(scaled * normal, axis=-1, keepdims=True)
    return inverse * (scaled - normal * inner_mean)


def positions(lengths, token_count):
    seq_ends = jnp.cumsum(lengths, dtype=jnp.int32)
    row_index = jnp.arange(token_count, dtype=jnp.int32)
    segment = jnp.sum(
        (row_index[:, None] >= seq_ends[None, :]).astype(jnp.int32), axis=1, dtype=jnp.int32
    )
    seq_ids = jnp.arange(lengths.shape[0], dtype=jnp.int32)
    seq_start = jnp.sum(
        jnp.where(segment[:, None] == seq_ids[None, :], (seq_ends - lengths)[None, :], 0),
        axis=1,
        dtype=jnp.int32,
    )
    return (segment, row_index - seq_start)


def rope_tables(position, head_dim):
    half_dim = head_dim // 2
    inverse_freq = jnp.exp(
        jnp.arange(half_dim, dtype=jnp.float32) * (-2.0 * math.log(rope_base) / head_dim)
    )
    angles = position.astype(jnp.float32)[:, None] * inverse_freq[None, :]
    cosine = jnp.cos(angles)
    sine_tab = jnp.sin(angles)
    return (jnp.concatenate([cosine, cosine], 1), jnp.concatenate([sine_tab, sine_tab], 1))


def rotate(values, cosine, sine_tab):
    half_dim = values.shape[-1] // 2
    turned = jnp.concatenate([-values[..., half_dim:], values[..., :half_dim]], -1)
    return values * cosine + turned * sine_tab


def split_blocks(array_in, axis_at, block_count):
    dims_now = array_in.shape
    regrouped = array_in.reshape(
        dims_now[:axis_at]
        + (block_count, dims_now[axis_at] // block_count)
        + dims_now[axis_at + 1 :]
    )
    return jnp.moveaxis(regrouped, axis_at, 0)


def join_blocks(array_in, axis_at):
    regrouped = jnp.moveaxis(array_in, 0, axis_at)
    dims_now = regrouped.shape
    return regrouped.reshape(
        dims_now[:axis_at] + (dims_now[axis_at] * dims_now[axis_at + 1],) + dims_now[axis_at + 2 :]
    )


def block_scores(query_block, key_rows, segment_rows, row_start, segment, scaling):
    block_rows = query_block.shape[2]
    scores_raw = (
        jnp.einsum("kgbd,ksd->kgbs", query_block, key_rows, preferred_element_type=jnp.float32)
        * scaling
    )
    query_index = row_start + jnp.arange(block_rows, dtype=jnp.int32)
    key_index = jnp.arange(key_rows.shape[1], dtype=jnp.int32)
    allowed = (segment_rows[:, None] == segment[None, :]) & (
        key_index[None, :] <= query_index[:, None]
    )
    return jnp.where(allowed[None, None], scores_raw, masked_out)


def attention_forward(queries, key_rows, values, segment, scaling, block_size):
    block_count = queries.shape[2] // block_size
    starts_all = jnp.arange(block_count, dtype=jnp.int32) * block_size

    def one_block(packed):
        query_block, segment_rows, row_start = packed
        scores = block_scores(query_block, key_rows, segment_rows, row_start, segment, scaling)
        top_score = jnp.max(scores, -1)
        exponent = jnp.exp(scores - top_score[..., None])
        row_total = jnp.sum(exponent, -1)
        probs = (exponent / row_total[..., None]).astype(jnp.bfloat16)
        output = jnp.einsum("kgbs,ksd->kgbd", probs, values, preferred_element_type=jnp.float32)
        return (output.astype(jnp.bfloat16), top_score, row_total)

    outputs, top_blocks, total_blocks = lax.map(
        one_block,
        (
            split_blocks(queries, 2, block_count),
            segment.reshape(block_count, block_size),
            starts_all,
        ),
    )
    return (join_blocks(outputs, 2), join_blocks(top_blocks, 2), join_blocks(total_blocks, 2))


def attention_backward(
    queries, key_rows, values, heads_grad, segment, top_kept, total_kept, scaling, block_size
):
    block_count = queries.shape[2] // block_size
    starts_all = jnp.arange(block_count, dtype=jnp.int32) * block_size

    def one_block(running, packed):
        key_acc, value_acc = running
        query_block, grad_block, segment_rows, row_start, top_block, total_block = packed
        scores = block_scores(query_block, key_rows, segment_rows, row_start, segment, scaling)
        probs = jnp.exp(scores - top_block[..., None]) / total_block[..., None]
        probs_low = probs.astype(jnp.bfloat16)
        value_acc = value_acc + jnp.einsum(
            "kgbs,kgbd->ksd", probs_low, grad_block, preferred_element_type=jnp.float32
        )
        prob_grad = jnp.einsum(
            "kgbd,ksd->kgbs", grad_block, values, preferred_element_type=jnp.float32
        )
        inner_sum = jnp.sum(probs * prob_grad, -1, keepdims=True)
        score_grad = (probs * (prob_grad - inner_sum)).astype(jnp.bfloat16)
        query_grad = (
            jnp.einsum("kgbs,ksd->kgbd", score_grad, key_rows, preferred_element_type=jnp.float32)
            * scaling
        )
        key_acc = (
            key_acc
            + jnp.einsum(
                "kgbs,kgbd->ksd", score_grad, query_block, preferred_element_type=jnp.float32
            )
            * scaling
        )
        return ((key_acc, value_acc), query_grad)

    empty = jnp.zeros(key_rows.shape, jnp.float32)
    packed_all = (
        split_blocks(queries, 2, block_count),
        split_blocks(heads_grad, 2, block_count),
        segment.reshape(block_count, block_size),
        starts_all,
        split_blocks(top_kept, 2, block_count),
        split_blocks(total_kept, 2, block_count),
    )
    (key_grad, value_grad), query_blocks = lax.scan(one_block, (empty, empty), packed_all)
    return (join_blocks(query_blocks, 2), key_grad, value_grad)


def exchange(array_in, axis_name, bits):
    count = lax.axis_size(axis_name)
    return lax.ppermute(array_in, axis_name, [(i, i ^ bits) for i in range(count)])


def gather_blocks(own, axis_name):
    count = lax.axis_size(axis_name)
    blocks = {0: own}
    bit = count // 2
    while bit:
        for d in sorted(blocks):
            blocks[d ^ bit] = exchange(blocks[d], axis_name, bit)
        bit //= 2
    return [blocks[d] for d in range(count)]


def scatter_sums(parts, axis_name):
    count = lax.axis_size(axis_name)
    sums = dict(enumerate(parts))
    bit = 1
    while bit < count:
        for d in sorted((d for d in sums if d & bit), reverse=True):
            arrived = exchange(sums.pop(d).astype(jnp.bfloat16), axis_name, bit)
            sums[d ^ bit] = sums[d ^ bit].astype(jnp.float32) + arrived.astype(jnp.float32)
        bit *= 2
    return sums[0]


def gather_experts(own, high_first):
    count = lax.axis_size("expert")
    blocks = {0: own}
    for d in range(2, count, 2):
        highest = 1 << (d.bit_length() - 1)
        lowest = d & -d
        bit = highest if high_first else lowest
        blocks[d] = exchange(blocks[d ^ bit], "expert", bit)
    for d in range(0, count, 2):
        blocks[d + 1] = exchange(blocks[d], "expert", 1)
    return [blocks[d] for d in range(count)]


def scatter_experts(parts, high_first):
    count = lax.axis_size("expert")
    sums = {}
    for d in range(0, count, 2):
        arrived = exchange(parts[d + 1].astype(jnp.bfloat16), "expert", 1)
        sums[d] = parts[d] + arrived.astype(jnp.float32)
    for d in range(count - 2, 0, -2):
        highest = 1 << (d.bit_length() - 1)
        lowest = d & -d
        bit = highest if high_first else lowest
        arrived = exchange(sums.pop(d).astype(jnp.bfloat16), "expert", bit)
        sums[d ^ bit] = sums[d ^ bit] + arrived.astype(jnp.float32)
    return sums[0]


def sum_experts(array_in):
    core = lax.axis_index("expert") & 1
    rows = array_in.shape[0] // 2
    top, bottom = array_in[:rows], array_in[rows:]
    keep = jnp.where(core == 0, top, bottom)
    give = jnp.where(core == 0, bottom, top).astype(jnp.bfloat16)
    half = keep + exchange(give, "expert", 1).astype(jnp.float32)
    count = lax.axis_size("expert")
    chip_bits = [1 << i for i in range(1, count.bit_length() - 1)]
    pieces = []
    for piece, bits in (
        (half[: rows // 2], chip_bits),
        (half[rows // 2 :], chip_bits[::-1]),
    ):
        piece = piece.astype(jnp.bfloat16)
        for bit in bits:
            arrived = exchange(piece, "expert", bit)
            piece = (piece.astype(jnp.float32) + arrived.astype(jnp.float32)).astype(jnp.bfloat16)
        pieces.append(piece)
    half = jnp.concatenate(pieces)
    other = exchange(half, "expert", 1)
    return jnp.concatenate(
        [jnp.where(core == 0, half, other), jnp.where(core == 0, other, half)]
    ).astype(jnp.float32)


def sum_all(array_in):
    for axis_name in ("tensor", "expert"):
        bit = 1
        while bit < lax.axis_size(axis_name):
            array_in = array_in + exchange(array_in, axis_name, bit)
            bit *= 2
    return array_in


def on_device(
    layer_in,
    seq_lengths,
    routes,
    gain_attn,
    w_qkv,
    w_output,
    gain_ffn,
    w_router,
    w_in,
    w_out,
    out_grad,
):
    token_count, model_width = layer_in.shape
    kv_here = w_qkv.shape[1]
    group_size = HEADS // KV_HEADS
    scaling = 1.0 / math.sqrt(HEAD_DIM)
    block_size = min(512, token_count)
    tensor_count = lax.axis_size("tensor")
    tensor_here = lax.axis_index("tensor")
    expert_here = lax.axis_index("expert")
    span = token_count // tensor_count
    w_output_all = gather_blocks(w_output, "tensor")
    w_in_all = gather_experts(w_in[0], True)
    w_out_all = jnp.concatenate(gather_experts(w_out[0], False))
    w_gate_all = jnp.concatenate([block[0] for block in w_in_all])
    w_up_all = jnp.concatenate([block[1] for block in w_in_all])

    def token_block(array_in, place):
        return lax.dynamic_slice_in_dim(array_in, (tensor_here ^ place) * span, span, 0)

    def token_blocks(array_in):
        return [token_block(array_in, place) for place in range(tensor_count)]

    def in_order(blocks):
        joined = jnp.zeros((token_count,) + blocks[0].shape[1:], blocks[0].dtype)
        for place, block in enumerate(blocks):
            joined = lax.dynamic_update_slice_in_dim(
                joined, block, (tensor_here ^ place) * span, 0
            )
        return joined

    segment, position = positions(seq_lengths[0], token_count)
    cosine, sine_tab = rope_tables(position, HEAD_DIM)
    inputs = layer_in.astype(jnp.float32)
    normed_one, inverse_one = rms_forward(inputs, gain_attn)
    normed_one_low = normed_one.astype(jnp.bfloat16)
    qkv_flat = w_qkv.reshape(model_width, -1)
    projected = jnp.dot(normed_one_low, qkv_flat, preferred_element_type=jnp.float32)
    projected = projected.reshape(token_count, kv_here, group_size + 2, HEAD_DIM)
    queries = rotate(
        jnp.transpose(projected[:, :, :group_size], (1, 2, 0, 3)), cosine, sine_tab
    ).astype(jnp.bfloat16)
    key_rows = rotate(
        jnp.transpose(projected[:, :, group_size], (1, 0, 2)), cosine, sine_tab
    ).astype(jnp.bfloat16)
    values = jnp.transpose(projected[:, :, group_size + 1], (1, 0, 2)).astype(jnp.bfloat16)
    attended, top_kept, total_kept = attention_forward(
        queries, key_rows, values, segment, scaling, block_size
    )
    heads_out = jnp.transpose(attended, (2, 0, 1, 3)).reshape(token_count, -1)
    residual = inputs
    for heads_block, output_block in zip(gather_blocks(heads_out, "tensor"), w_output_all):
        residual = residual + jnp.dot(
            heads_block, output_block, preferred_element_type=jnp.float32
        )
    normed_two, inverse_two = rms_forward(residual, gain_ffn)
    normed_low = normed_two.astype(jnp.bfloat16)
    experts_all = w_router.shape[1]
    unit_count = w_out.shape[1]
    expert_ids = jnp.arange(experts_all, dtype=jnp.int32) ^ expert_here
    w_router = w_router[:, expert_ids]
    logits = jnp.dot(normed_low, w_router, preferred_element_type=jnp.float32)
    picked = jnp.any(routes[:, :, None] == expert_ids[None, None, :], axis=1)
    picked_logits = jnp.where(picked, logits, masked_out)
    top_logit = jnp.max(picked_logits, -1, keepdims=True)
    weight = jnp.where(picked, jnp.exp(picked_logits - top_logit), 0.0)
    gates = weight / jnp.sum(weight, -1, keepdims=True)

    def by_unit(per_expert):
        return jnp.broadcast_to(
            per_expert[:, :, None], (token_count, experts_all, unit_count)
        ).reshape(token_count, -1)

    def over_units(per_unit):
        return jnp.sum(per_unit.reshape(token_count, experts_all, unit_count), -1)

    def times_transposed(left, right):
        return lax.dot_general(
            left, right, (((1,), (1,)), ((), ())), preferred_element_type=jnp.float32
        )

    def transposed_times(left, right):
        return lax.dot_general(
            left, right, (((0,), (0,)), ((), ())), preferred_element_type=jnp.float32
        )

    gates_wide = by_unit(gates)
    gate_vals = times_transposed(normed_low, w_gate_all)
    up_vals = times_transposed(normed_low, w_up_all)
    plain_grad = times_transposed(out_grad, w_out_all)
    sig_vals = jax.nn.sigmoid(gate_vals)
    silu_vals = gate_vals * sig_vals
    active = silu_vals * up_vals
    scaled_active = (active * gates_wide).astype(jnp.bfloat16)
    active_grad = plain_grad * gates_wide
    gate_pre = (
        active_grad * up_vals * (sig_vals * (1.0 + gate_vals * (1.0 - sig_vals)))
    ).astype(jnp.bfloat16)
    up_pre = (active_grad * silu_vals).astype(jnp.bfloat16)
    gate_grad_part = over_units(active * plain_grad)
    logit_part = (
        gates * (gate_grad_part - jnp.sum(gates * gate_grad_part, -1, keepdims=True))
    ).astype(jnp.bfloat16)
    normed_two_part = (
        jnp.dot(gate_pre, w_gate_all, preferred_element_type=jnp.float32)
        + jnp.dot(up_pre, w_up_all, preferred_element_type=jnp.float32)
        + times_transposed(logit_part, w_router)
    )
    upstream = token_block(out_grad, 0).astype(jnp.float32)
    residual_block = token_block(residual, 0)
    normed_two_grad = scatter_sums(token_blocks(normed_two_part), "tensor")
    residual_part = rms_backward(
        residual_block, token_block(inverse_two, 0), gain_ffn, normed_two_grad
    )
    residual_grad = upstream + residual_part
    branch_here_grad = in_order(gather_blocks(residual_grad.astype(jnp.bfloat16), "tensor"))
    mixture_part = jnp.dot(scaled_active, w_out_all, preferred_element_type=jnp.float32)
    mixture = scatter_sums(token_blocks(mixture_part), "tensor")
    layer_here = in_order(
        gather_blocks((residual_block + mixture).astype(jnp.bfloat16), "tensor")
    )

    def to_owner(left, right, high_first):
        return scatter_experts(
            split_blocks(transposed_times(left, right), 0, experts_all), high_first
        )

    w_in_grad = jnp.stack(
        [to_owner(gate_pre, normed_low, True), to_owner(up_pre, normed_low, True)]
    )[None]
    w_out_grad = to_owner(scaled_active, out_grad, False)[None]
    router_part = transposed_times(logit_part, normed_low)
    normal_two = residual * inverse_two
    gain_ffn_part = jnp.sum(normed_two_part * normal_two, axis=0)
    w_output_grad = lax.dot_general(
        heads_out, branch_here_grad, (((0,), (0,)), ((), ())), preferred_element_type=jnp.float32
    )
    heads_flat = lax.dot_general(
        branch_here_grad, w_output, (((1,), (1,)), ((), ())), preferred_element_type=jnp.float32
    ).astype(jnp.bfloat16)
    heads_grad = jnp.transpose(
        heads_flat.reshape(token_count, kv_here, group_size, HEAD_DIM), (1, 2, 0, 3)
    )
    query_grad, key_grad, value_grad = attention_backward(
        queries, key_rows, values, heads_grad, segment, top_kept, total_kept, scaling, block_size
    )
    query_grad = rotate(query_grad, cosine, -sine_tab)
    key_grad = rotate(key_grad, cosine, -sine_tab)
    projected_grad = jnp.concatenate(
        [
            jnp.transpose(query_grad, (2, 0, 1, 3)),
            jnp.transpose(key_grad, (1, 0, 2))[:, :, None],
            jnp.transpose(value_grad, (1, 0, 2))[:, :, None],
        ],
        2,
    )
    projected_grad = projected_grad.reshape(token_count, -1).astype(jnp.bfloat16)
    w_qkv_grad = lax.dot_general(
        normed_one_low, projected_grad, (((0,), (0,)), ((), ())), preferred_element_type=jnp.float32
    ).reshape(w_qkv.shape)
    normed_one_part = lax.dot_general(
        projected_grad, qkv_flat, (((1,), (1,)), ((), ())), preferred_element_type=jnp.float32
    )
    gain_attn_part = jnp.sum(normed_one_part * (inputs * inverse_one), axis=0)
    normed_one_grad = scatter_sums(token_blocks(normed_one_part), "tensor")
    input_part = rms_backward(
        token_block(inputs, 0), token_block(inverse_one, 0), gain_attn, normed_one_grad
    )
    in_here = in_order(
        gather_blocks((residual_grad + input_part).astype(jnp.bfloat16), "tensor")
    )
    qkv_summed = sum_experts(w_qkv_grad.reshape(model_width, -1)).reshape(w_qkv.shape)
    output_summed = sum_experts(w_output_grad)
    router_part = router_part[expert_ids]
    small = jnp.concatenate([router_part, gain_ffn_part[None], gain_attn_part[None]])
    small = sum_all(small)
    return (
        layer_here,
        in_here,
        small[experts_all + 1],
        qkv_summed,
        output_summed,
        small[experts_all],
        jnp.transpose(small[:experts_all]),
        w_in_grad,
        w_out_grad,
    )


def solution(mesh):
    placed = (
        P("expert", None),
        P("expert", None),
        P("expert", None),
        P(),
        P(None, "tensor", None),
        P("tensor", None),
        P(),
        P(),
        P("expert", None, "tensor", None),
        P("expert", "tensor", None),
        P("expert", None),
    )
    return jax.shard_map(
        on_device,
        mesh=mesh,
        in_specs=placed,
        out_specs=(
            P("expert", None),
            P("expert", None),
            P(),
            P(None, "tensor", None),
            P("tensor", None),
            P(),
            P(),
            P("expert", None, "tensor", None),
            P("expert", "tensor", None),
        ),
        check_vma=False,
    )
```

```python
import functools
import math

import jax
import jax.numpy as jnp
import numpy as np
from jax import lax
from jax.experimental import pallas as pl
from jax.experimental.pallas import tpu as pltpu
from jax.sharding import PartitionSpec as P

HEADS = 16
KV_HEADS = 8
HEAD_DIM = 64


epsilon = 1e-06
rope_base = 10000.0
masked_out = -1e30


def rms_forward(values, gain_vec):
    inverse = lax.rsqrt(jnp.mean(values * values, axis=-1, keepdims=True) + epsilon)
    return (values * inverse * gain_vec, inverse)


def rms_backward(values, inverse, gain_vec, upstream):
    normal = values * inverse
    scaled = upstream * gain_vec
    inner_mean = jnp.mean(scaled * normal, axis=-1, keepdims=True)
    return inverse * (scaled - normal * inner_mean)


def positions(lengths, token_count):
    seq_ends = jnp.cumsum(lengths, dtype=jnp.int32)
    row_index = jnp.arange(token_count, dtype=jnp.int32)
    segment = jnp.sum(
        (row_index[:, None] >= seq_ends[None, :]).astype(jnp.int32), axis=1, dtype=jnp.int32
    )
    seq_ids = jnp.arange(lengths.shape[0], dtype=jnp.int32)
    seq_start = jnp.sum(
        jnp.where(segment[:, None] == seq_ids[None, :], (seq_ends - lengths)[None, :], 0),
        axis=1,
        dtype=jnp.int32,
    )
    return (segment, row_index - seq_start)


def rope_tables(position, head_dim):
    half_dim = head_dim // 2
    inverse_freq = jnp.exp(
        jnp.arange(half_dim, dtype=jnp.float32) * (-2.0 * math.log(rope_base) / head_dim)
    )
    angles = position.astype(jnp.float32)[:, None] * inverse_freq[None, :]
    cosine = jnp.cos(angles)
    sine_tab = jnp.sin(angles)
    return (jnp.concatenate([cosine, cosine], 1), jnp.concatenate([sine_tab, sine_tab], 1))


def rotate(values, cosine, sine_tab):
    half_dim = values.shape[-1] // 2
    turned = jnp.concatenate([-values[..., half_dim:], values[..., :half_dim]], -1)
    return values * cosine + turned * sine_tab


def split_blocks(array_in, axis_at, block_count):
    dims_now = array_in.shape
    regrouped = array_in.reshape(
        dims_now[:axis_at]
        + (block_count, dims_now[axis_at] // block_count)
        + dims_now[axis_at + 1 :]
    )
    return jnp.moveaxis(regrouped, axis_at, 0)


def join_blocks(array_in, axis_at):
    regrouped = jnp.moveaxis(array_in, 0, axis_at)
    dims_now = regrouped.shape
    return regrouped.reshape(
        dims_now[:axis_at] + (dims_now[axis_at] * dims_now[axis_at + 1],) + dims_now[axis_at + 2 :]
    )


def block_scores(query_block, key_rows, segment_rows, row_start, segment, scaling):
    block_rows = query_block.shape[2]
    scores_raw = (
        jnp.einsum("kgbd,ksd->kgbs", query_block, key_rows, preferred_element_type=jnp.float32)
        * scaling
    )
    query_index = row_start + jnp.arange(block_rows, dtype=jnp.int32)
    key_index = jnp.arange(key_rows.shape[1], dtype=jnp.int32)
    allowed = (segment_rows[:, None] == segment[None, :]) & (
        key_index[None, :] <= query_index[:, None]
    )
    return jnp.where(allowed[None, None], scores_raw, masked_out)


def attention_forward(queries, key_rows, values, segment, scaling, block_size):
    block_count = queries.shape[2] // block_size
    starts_all = jnp.arange(block_count, dtype=jnp.int32) * block_size

    def one_block(packed):
        query_block, segment_rows, row_start = packed
        scores = block_scores(query_block, key_rows, segment_rows, row_start, segment, scaling)
        top_score = jnp.max(scores, -1)
        exponent = jnp.exp(scores - top_score[..., None])
        row_total = jnp.sum(exponent, -1)
        probs = (exponent / row_total[..., None]).astype(jnp.bfloat16)
        output = jnp.einsum("kgbs,ksd->kgbd", probs, values, preferred_element_type=jnp.float32)
        return (output.astype(jnp.bfloat16), top_score, row_total)

    outputs, top_blocks, total_blocks = lax.map(
        one_block,
        (
            split_blocks(queries, 2, block_count),
            segment.reshape(block_count, block_size),
            starts_all,
        ),
    )
    return (join_blocks(outputs, 2), join_blocks(top_blocks, 2), join_blocks(total_blocks, 2))


def attention_backward(
    queries, key_rows, values, heads_grad, segment, top_kept, total_kept, scaling, block_size
):
    block_count = queries.shape[2] // block_size
    starts_all = jnp.arange(block_count, dtype=jnp.int32) * block_size

    def one_block(running, packed):
        key_acc, value_acc = running
        query_block, grad_block, segment_rows, row_start, top_block, total_block = packed
        scores = block_scores(query_block, key_rows, segment_rows, row_start, segment, scaling)
        probs = jnp.exp(scores - top_block[..., None]) / total_block[..., None]
        probs_low = probs.astype(jnp.bfloat16)
        value_acc = value_acc + jnp.einsum(
            "kgbs,kgbd->ksd", probs_low, grad_block, preferred_element_type=jnp.float32
        )
        prob_grad = jnp.einsum(
            "kgbd,ksd->kgbs", grad_block, values, preferred_element_type=jnp.float32
        )
        inner_sum = jnp.sum(probs * prob_grad, -1, keepdims=True)
        score_grad = (probs * (prob_grad - inner_sum)).astype(jnp.bfloat16)
        query_grad = (
            jnp.einsum("kgbs,ksd->kgbd", score_grad, key_rows, preferred_element_type=jnp.float32)
            * scaling
        )
        key_acc = (
            key_acc
            + jnp.einsum(
                "kgbs,kgbd->ksd", score_grad, query_block, preferred_element_type=jnp.float32
            )
            * scaling
        )
        return ((key_acc, value_acc), query_grad)

    empty = jnp.zeros(key_rows.shape, jnp.float32)
    packed_all = (
        split_blocks(queries, 2, block_count),
        split_blocks(heads_grad, 2, block_count),
        segment.reshape(block_count, block_size),
        starts_all,
        split_blocks(top_kept, 2, block_count),
        split_blocks(total_kept, 2, block_count),
    )
    (key_grad, value_grad), query_blocks = lax.scan(one_block, (empty, empty), packed_all)
    return (join_blocks(query_blocks, 2), key_grad, value_grad)


def on_device_general(
    layer_in,
    seq_lengths,
    routes,
    gain_attn,
    w_qkv,
    w_output,
    gain_ffn,
    w_router,
    w_in,
    w_out,
    out_grad,
):
    token_count, model_width = layer_in.shape
    kv_here = w_qkv.shape[1]
    group_size = HEADS // KV_HEADS
    scaling = 1.0 / math.sqrt(HEAD_DIM)
    block_size = min(512, token_count)
    w_output_all = lax.all_gather(w_output, "tensor", axis=0, tiled=True)
    w_gate_all = lax.all_gather(w_in[0, 0], "expert", axis=0, tiled=True)
    w_up_all = lax.all_gather(w_in[0, 1], "expert", axis=0, tiled=True)
    w_out_all = lax.all_gather(w_out[0], "expert", axis=0, tiled=True)
    segment, position = positions(seq_lengths[0], token_count)
    cosine, sine_tab = rope_tables(position, HEAD_DIM)
    inputs = layer_in.astype(jnp.float32)
    normed_one, inverse_one = rms_forward(inputs, gain_attn)
    normed_one_low = normed_one.astype(jnp.bfloat16)
    qkv_flat = w_qkv.reshape(model_width, -1)
    projected = jnp.dot(normed_one_low, qkv_flat, preferred_element_type=jnp.float32)
    projected = projected.reshape(token_count, kv_here, group_size + 2, HEAD_DIM)
    queries = rotate(
        jnp.transpose(projected[:, :, :group_size], (1, 2, 0, 3)), cosine, sine_tab
    ).astype(jnp.bfloat16)
    key_rows = rotate(
        jnp.transpose(projected[:, :, group_size], (1, 0, 2)), cosine, sine_tab
    ).astype(jnp.bfloat16)
    values = jnp.transpose(projected[:, :, group_size + 1], (1, 0, 2)).astype(jnp.bfloat16)
    attended, top_kept, total_kept = attention_forward(
        queries, key_rows, values, segment, scaling, block_size
    )
    heads_out = jnp.transpose(attended, (2, 0, 1, 3)).reshape(token_count, -1)
    heads_all = lax.all_gather(heads_out, "tensor", axis=1, tiled=True)
    branch_here = jnp.dot(heads_all, w_output_all, preferred_element_type=jnp.float32)
    residual = inputs + branch_here
    normed_two, inverse_two = rms_forward(residual, gain_ffn)
    normed_low = normed_two.astype(jnp.bfloat16)
    experts_all = w_router.shape[1]
    unit_count = w_out.shape[1]
    logits = jnp.dot(normed_low, w_router, preferred_element_type=jnp.float32)
    expert_ids = jnp.arange(experts_all, dtype=jnp.int32)
    picked = jnp.any(routes[:, :, None] == expert_ids[None, None, :], axis=1)
    picked_logits = jnp.where(picked, logits, masked_out)
    top_logit = jnp.max(picked_logits, -1, keepdims=True)
    weight = jnp.where(picked, jnp.exp(picked_logits - top_logit), 0.0)
    gates = weight / jnp.sum(weight, -1, keepdims=True)

    def by_unit(per_expert):
        return jnp.broadcast_to(
            per_expert[:, :, None], (token_count, experts_all, unit_count)
        ).reshape(token_count, -1)

    def over_units(per_unit):
        return jnp.sum(per_unit.reshape(token_count, experts_all, unit_count), -1)

    def times_transposed(left, right):
        return lax.dot_general(
            left, right, (((1,), (1,)), ((), ())), preferred_element_type=jnp.float32
        )

    def transposed_times(left, right):
        return lax.dot_general(
            left, right, (((0,), (0,)), ((), ())), preferred_element_type=jnp.float32
        )

    gates_wide = by_unit(gates)
    gate_vals = times_transposed(normed_low, w_gate_all)
    up_vals = times_transposed(normed_low, w_up_all)
    plain_grad = times_transposed(out_grad, w_out_all)
    sig_vals = jax.nn.sigmoid(gate_vals)
    silu_vals = gate_vals * sig_vals
    active = silu_vals * up_vals
    scaled_active = (active * gates_wide).astype(jnp.bfloat16)
    active_grad = plain_grad * gates_wide
    gate_pre = (
        active_grad * up_vals * (sig_vals * (1.0 + gate_vals * (1.0 - sig_vals)))
    ).astype(jnp.bfloat16)
    up_pre = (active_grad * silu_vals).astype(jnp.bfloat16)
    gate_grad_part = over_units(active * plain_grad)
    logit_part = (
        gates * (gate_grad_part - jnp.sum(gates * gate_grad_part, -1, keepdims=True))
    ).astype(jnp.bfloat16)
    normed_two_part = (
        jnp.dot(gate_pre, w_gate_all, preferred_element_type=jnp.float32)
        + jnp.dot(up_pre, w_up_all, preferred_element_type=jnp.float32)
        + times_transposed(logit_part, w_router)
    )
    normed_two_grad = lax.psum(normed_two_part.astype(jnp.bfloat16), "tensor").astype(jnp.float32)
    mixture_part = jnp.dot(scaled_active, w_out_all, preferred_element_type=jnp.float32)
    mixture = lax.psum(mixture_part.astype(jnp.bfloat16), "tensor").astype(jnp.float32)
    layer_here = (residual + mixture).astype(jnp.bfloat16)

    def to_owner(partial):
        return lax.psum_scatter(
            partial.astype(jnp.bfloat16), "expert", scatter_dimension=0, tiled=True
        ).astype(jnp.float32)

    w_gate_grad = to_owner(transposed_times(gate_pre, normed_low))
    w_up_grad = to_owner(transposed_times(up_pre, normed_low))
    w_in_grad = jnp.stack([w_gate_grad, w_up_grad])[None]
    w_out_grad = to_owner(transposed_times(scaled_active, out_grad))[None]
    router_part = transposed_times(logit_part, normed_low)
    normal_two = residual * inverse_two
    gain_ffn_part = jnp.sum(normed_two_part * normal_two, axis=0)
    upstream = out_grad.astype(jnp.float32)
    residual_part = rms_backward(residual, inverse_two, gain_ffn, normed_two_grad)
    residual_grad = upstream + residual_part
    branch_here_grad = residual_grad.astype(jnp.bfloat16)
    w_output_grad = lax.dot_general(
        heads_out, branch_here_grad, (((0,), (0,)), ((), ())), preferred_element_type=jnp.float32
    )
    heads_flat = lax.dot_general(
        branch_here_grad, w_output, (((1,), (1,)), ((), ())), preferred_element_type=jnp.float32
    ).astype(jnp.bfloat16)
    heads_grad = jnp.transpose(
        heads_flat.reshape(token_count, kv_here, group_size, HEAD_DIM), (1, 2, 0, 3)
    )
    query_grad, key_grad, value_grad = attention_backward(
        queries, key_rows, values, heads_grad, segment, top_kept, total_kept, scaling, block_size
    )
    query_grad = rotate(query_grad, cosine, -sine_tab)
    key_grad = rotate(key_grad, cosine, -sine_tab)
    projected_grad = jnp.concatenate(
        [
            jnp.transpose(query_grad, (2, 0, 1, 3)),
            jnp.transpose(key_grad, (1, 0, 2))[:, :, None],
            jnp.transpose(value_grad, (1, 0, 2))[:, :, None],
        ],
        2,
    )
    projected_grad = projected_grad.reshape(token_count, -1).astype(jnp.bfloat16)
    w_qkv_grad = lax.dot_general(
        normed_one_low, projected_grad, (((0,), (0,)), ((), ())), preferred_element_type=jnp.float32
    ).reshape(w_qkv.shape)
    normed_one_part = lax.dot_general(
        projected_grad, qkv_flat, (((1,), (1,)), ((), ())), preferred_element_type=jnp.float32
    )
    gain_attn_part = jnp.sum(normed_one_part * (inputs * inverse_one), axis=0)
    normed_one_grad = lax.psum(normed_one_part.astype(jnp.bfloat16), "tensor").astype(jnp.float32)
    input_part = rms_backward(inputs, inverse_one, gain_attn, normed_one_grad)
    in_here = (residual_grad + input_part).astype(jnp.bfloat16)
    qkv_summed = lax.psum(w_qkv_grad.astype(jnp.bfloat16), "expert").astype(jnp.float32)
    output_summed = lax.psum(w_output_grad.astype(jnp.bfloat16), "expert").astype(jnp.float32)
    small = jnp.concatenate([router_part, gain_ffn_part[None], gain_attn_part[None]])
    small = lax.psum(small, ("expert", "tensor"))
    return (
        layer_here,
        in_here,
        small[experts_all + 1],
        qkv_summed,
        output_summed,
        small[experts_all],
        jnp.transpose(small[:experts_all]),
        w_in_grad,
        w_out_grad,
    )


LANES = 128
ROWS = 128


def exchange(array_in, axis_name, bits):
    count = lax.axis_size(axis_name)
    return lax.ppermute(array_in, axis_name, [(i, i ^ bits) for i in range(count)])


def gather_blocks(own):
    far = exchange(own, "tensor", 2)
    near = exchange(own, "tensor", 1)
    return [own, near, far, exchange(far, "tensor", 1)]


def scatter_sums(parts):
    relayed = exchange(parts[3], "tensor", 1)
    far = (parts[2].astype(jnp.float32) + relayed.astype(jnp.float32)).astype(jnp.bfloat16)
    far = exchange(far, "tensor", 2)
    near = exchange(parts[1], "tensor", 1)
    return parts[0] + near.astype(jnp.float32) + far.astype(jnp.float32)


def gather_experts(own, high_first):
    near = exchange(own, "expert", 2)
    far = exchange(own, "expert", 4)
    both = exchange(near, "expert", 4) if high_first else exchange(far, "expert", 2)
    chips = [own, near, far, both]
    return chips + [exchange(block, "expert", 1) for block in chips]


def scatter_experts(even, odd):
    summed = even + exchange(odd.astype(jnp.bfloat16), "expert", 1).astype(jnp.float32)
    chips = split_blocks(summed, 0, 4)
    total = chips[0]
    for place in (3, 1, 2):
        total = total + exchange(
            chips[place].astype(jnp.bfloat16), "expert", 2 * place
        ).astype(jnp.float32)
    return total


def sum_experts(array_in, bits):
    core = lax.axis_index("expert") & 1
    rows = array_in.shape[0] // 2
    top, bottom = array_in[:rows], array_in[rows:]
    keep = jnp.where(core == 0, top, bottom)
    give = jnp.where(core == 0, bottom, top).astype(jnp.bfloat16)
    half = keep + exchange(give, "expert", 1).astype(jnp.float32)
    half = half.astype(jnp.bfloat16)
    for bit in bits:
        arrived = exchange(half, "expert", bit)
        half = (half.astype(jnp.float32) + arrived.astype(jnp.float32)).astype(jnp.bfloat16)
    other = exchange(half, "expert", 1)
    return jnp.concatenate(
        [jnp.where(core == 0, half, other), jnp.where(core == 0, other, half)]
    ).astype(jnp.float32)


def sum_all(array_in):
    for axis_name in ("tensor", "expert"):
        bit = 1
        while bit < lax.axis_size(axis_name):
            array_in = array_in + exchange(array_in, axis_name, bit)
            bit *= 2
    return array_in


def dot_plain(left, right):
    return jnp.dot(left, right, preferred_element_type=jnp.float32)


def dot_transposed(left, right):
    return lax.dot_general(
        left, right, (((1,), (1,)), ((), ())), preferred_element_type=jnp.float32
    )


def transposed_dot(left, right):
    return lax.dot_general(
        left, right, (((0,), (0,)), ((), ())), preferred_element_type=jnp.float32
    )


def lane_index(shape):
    return lax.broadcasted_iota(jnp.int32, shape, 1)


def turn(values):
    low_half = (lane_index(values.shape) & (HEAD_DIM - 1)) < HEAD_DIM // 2
    return jnp.where(
        low_half,
        -pltpu.roll(values, LANES - HEAD_DIM // 2, 1),
        pltpu.roll(values, HEAD_DIM // 2, 1),
    )


def swap_heads(values):
    return pltpu.roll(values, HEAD_DIM, 1)


def first_head(shape):
    return lane_index(shape) < HEAD_DIM


def angle_tables(token_count):
    half_dim = HEAD_DIM // 2
    inverse_freq = np.exp(np.arange(half_dim) * (-2.0 * math.log(rope_base) / HEAD_DIM))
    angles = np.arange(token_count)[:, None] * inverse_freq[None, :]
    tile = LANES // half_dim
    return (
        np.tile(np.cos(angles), (1, tile)).astype(np.float32),
        np.tile(np.sin(angles), (1, tile)).astype(np.float32),
    )


def attend_kernel(
    lengths, layer_in, gain, w_qkv, cosine, sine, normed, inverse, queries, pairs, probs, attended
):
    token_count = layer_in.shape[0]
    kv_here = pairs.shape[0]
    for row in range(0, token_count, ROWS):
        rows = pl.ds(row, ROWS)
        values = layer_in[rows, :].astype(jnp.float32)
        scale = lax.rsqrt(jnp.mean(values * values, axis=-1, keepdims=True) + epsilon)
        inverse[rows, :] = scale
        normed[rows, :] = (values * scale * gain[...]).astype(jnp.bfloat16)
    is_first = first_head((ROWS, LANES))
    for kv in range(kv_here):
        projected = dot_plain(normed[...], w_qkv[:, 2 * LANES * kv : 2 * LANES * (kv + 1)])
        for block in range(token_count // ROWS):
            rows = pl.ds(block * ROWS, ROWS)
            cos_rows, sin_rows = cosine[rows, :], sine[rows, :]
            query = projected[block * ROWS : (block + 1) * ROWS, :LANES]
            query = (query * cos_rows + turn(query) * sin_rows) * (1.0 / math.sqrt(HEAD_DIM))
            queries[kv, block, :ROWS, :] = jnp.where(is_first, query, 0.0).astype(jnp.bfloat16)
            queries[kv, block, ROWS:, :] = jnp.where(is_first, swap_heads(query), 0.0).astype(
                jnp.bfloat16
            )
            pair = projected[block * ROWS : (block + 1) * ROWS, LANES:]
            pairs[kv, rows, :] = jnp.where(
                is_first, pair * cos_rows + turn(pair) * sin_rows, pair
            ).astype(jnp.bfloat16)
    for block in range(token_count // ROWS):
        keys = (block + 1) * ROWS
        token = block * ROWS + (
            lax.broadcasted_iota(jnp.int32, (2 * ROWS, keys), 0) & (ROWS - 1)
        )
        start = jnp.zeros_like(token)
        end = 0
        for seq in range(lengths.shape[1] - 1):
            end = end + lengths[0, seq]
            start = jnp.where(token >= end, end, start)
        key = lane_index((2 * ROWS, keys))
        allowed = (key <= token) & (key >= start)
        for kv in range(kv_here):
            scores = dot_transposed(queries[kv, block], pairs[kv, :keys, :])
            scores = jnp.where(allowed, scores, masked_out)
            exponent = jnp.exp(scores - jnp.max(scores, -1, keepdims=True))
            share = (exponent * (1.0 / jnp.sum(exponent, -1, keepdims=True))).astype(jnp.bfloat16)
            probs[kv, block, :, :keys] = share
            output = dot_plain(share, pairs[kv, :keys, :])
            attended[pl.ds(block * ROWS, ROWS), kv * LANES : (kv + 1) * LANES] = jnp.where(
                is_first, swap_heads(output[:ROWS]), output[ROWS:]
            ).astype(jnp.bfloat16)


def write_parts(place, total, parts, span):
    for number, part in enumerate(parts):
        row = pl.multiple_of((place[0] ^ number) * span, span)
        part[...] = total[pl.ds(row, span), :].astype(part.dtype)


def middle_kernel(tensor_count, experts_all, *refs):
    place, gain, router, routes, layer_in, out_grad = refs[:6]
    refs = refs[6:]
    heads, refs = refs[:tensor_count], refs[tensor_count:]
    outputs_w, refs = refs[:tensor_count], refs[tensor_count:]
    w_ins, refs = refs[:experts_all], refs[experts_all:]
    w_outs, refs = refs[:experts_all], refs[experts_all:]
    parts, refs = refs[:tensor_count], refs[tensor_count:]
    (residual_block, inverse_block, normed, active_out, pre_out, gain_part, router_part) = refs[:7]
    (w_in, w_out, residual, inverse, gates, gate_grad, hidden, plain, total, sems) = refs[7:]
    token_count, model_width = layer_in.shape
    units = w_outs[0].shape[0]
    span = token_count // tensor_count
    copies = []
    for number in range(experts_all):
        copies.append(
            pltpu.make_async_copy(
                w_ins[number], w_in.at[pl.ds(number * 2 * units, 2 * units)], sems.at[0, number]
            )
        )
        copies.append(
            pltpu.make_async_copy(
                w_outs[number], w_out.at[pl.ds(number * units, units)], sems.at[1, number]
            )
        )
    for copy in copies:
        copy.start()
    lane = lane_index((ROWS, LANES))
    for row in range(0, token_count, ROWS):
        rows = pl.ds(row, ROWS)
        values = layer_in[rows, :].astype(jnp.float32)
        for head, output in zip(heads, outputs_w):
            values = values + dot_plain(head[rows, :], output[...])
        residual[rows, :] = values
        scale = lax.rsqrt(jnp.mean(values * values, axis=-1, keepdims=True) + epsilon)
        inverse[rows, :] = scale
        normed_low = (values * scale * gain[...]).astype(jnp.bfloat16)
        normed[rows, :] = normed_low
        logits = dot_transposed(normed_low, router[...])
        picked = routes[rows, 0:1] == lane
        for top in range(1, routes.shape[1]):
            picked = picked | (routes[rows, top : top + 1] == lane)
        logits = jnp.where(picked, logits, masked_out)
        weight = jnp.where(picked, jnp.exp(logits - jnp.max(logits, -1, keepdims=True)), 0.0)
        gates[rows, :] = weight / jnp.sum(weight, -1, keepdims=True)
    gate_grad[...] = jnp.zeros_like(gate_grad)
    for copy in copies:
        copy.wait()

    def expert_step(number, carry):
        twice = 2 * number
        name = place[1] ^ jnp.where(twice < experts_all, twice, twice - experts_all + 1)
        in_rows = pl.ds(pl.multiple_of(number * 2 * units, 2 * units), 2 * units)
        out_rows = pl.ds(pl.multiple_of(number * units, units), units)
        gate_lanes = pl.ds(pl.multiple_of(number * 2 * units, units), units)
        up_lanes = pl.ds(pl.multiple_of(number * 2 * units + units, units), units)
        hidden[...] = dot_transposed(normed[...], w_in[in_rows, :])
        plain[...] = dot_transposed(out_grad[...], w_out[out_rows, :])
        for row in range(0, token_count, ROWS):
            rows = pl.ds(row, ROWS)
            gate = jnp.sum(jnp.where(lane == name, gates[rows, :], 0.0), -1, keepdims=True)
            gate_vals, up_vals = hidden[rows, :units], hidden[rows, units:]
            sig_vals = 1.0 / (1.0 + jnp.exp(-gate_vals))
            silu_vals = gate_vals * sig_vals
            active = silu_vals * up_vals
            grad = plain[rows, :]
            gate_grad[rows, :] = gate_grad[rows, :] + jnp.where(
                lane == name, jnp.sum(active * grad, -1, keepdims=True), 0.0
            )
            active_grad = grad * gate
            active_out[rows, out_rows] = (active * gate).astype(jnp.bfloat16)
            pre_out[rows, gate_lanes] = (
                active_grad * up_vals * (sig_vals * (1.0 + gate_vals * (1.0 - sig_vals)))
            ).astype(jnp.bfloat16)
            pre_out[rows, up_lanes] = (active_grad * silu_vals).astype(jnp.bfloat16)
        return carry

    lax.fori_loop(0, experts_all, expert_step, 0)
    gate_all, grad_all = gates[...], gate_grad[...]
    logit_part = (
        gate_all * (grad_all - jnp.sum(gate_all * grad_all, -1, keepdims=True))
    ).astype(jnp.bfloat16)
    router_part[...] = transposed_dot(logit_part, normed[...])[:experts_all]

    def column_step(number, carry):
        columns = pl.ds(pl.multiple_of(number * 2 * LANES, 2 * LANES), 2 * LANES)
        total[:, columns] = dot_plain(pre_out[...], w_in[:, columns]) + dot_plain(
            logit_part, router[:, columns]
        )
        return carry

    lax.fori_loop(0, model_width // (2 * LANES), column_step, 0)
    write_parts(place, total, parts, span)
    row = pl.ds(pl.multiple_of(place[0] * span, span), span)
    residual_block[...] = residual[row, :]
    inverse_block[...] = inverse[row, :]
    gain_sum = jnp.zeros((1, model_width), jnp.float32)
    for row in range(0, token_count, ROWS):
        rows = pl.ds(row, ROWS)
        gain_sum = gain_sum + jnp.sum(
            total[rows, :] * (residual[rows, :] * inverse[rows, :]), 0, keepdims=True
        )
    gain_part[...] = gain_sum


def attend_back_kernel(tensor_count, *refs):
    place, w_output, queries, pairs, probs, cosine, sine, w_qkv, layer_in, inverse = refs[:10]
    refs = refs[10:]
    blocks, refs = refs[:tensor_count], refs[tensor_count:]
    parts, refs = refs[:tensor_count], refs[tensor_count:]
    branch_grad, projected_grad, gain_part, heads_grad, pair_grad, total = refs
    token_count, model_width = layer_in.shape
    span = token_count // tensor_count
    for number, block in enumerate(blocks):
        row = pl.multiple_of((place[0] ^ number) * span, span)
        branch_grad[pl.ds(row, span), :] = block[...]
    heads_grad[...] = dot_transposed(branch_grad[...], w_output[...])
    is_first = first_head((ROWS, LANES))
    for kv in range(pairs.shape[0]):
        pair_grad[...] = jnp.zeros_like(pair_grad)
        for block in range(token_count // ROWS):
            keys = (block + 1) * ROWS
            rows = pl.ds(block * ROWS, ROWS)
            upper = heads_grad[rows, kv * LANES : (kv + 1) * LANES]
            upper = jnp.concatenate(
                [
                    jnp.where(is_first, 0.0, swap_heads(upper)),
                    jnp.where(is_first, 0.0, upper),
                ]
            ).astype(jnp.bfloat16)
            share_low = probs[kv, block, :, :keys]
            share = share_low.astype(jnp.float32)
            prob_grad = dot_transposed(upper, pairs[kv, :keys, :])
            inner = jnp.sum(share * prob_grad, -1, keepdims=True)
            score_grad = (share * (prob_grad - inner)).astype(jnp.bfloat16)
            query_grad = dot_plain(score_grad, pairs[kv, :keys, :])
            query_grad = jnp.where(
                is_first, query_grad[:ROWS], swap_heads(query_grad[ROWS:])
            ) * (1.0 / math.sqrt(HEAD_DIM))
            projected_grad[rows, 2 * kv * LANES : (2 * kv + 1) * LANES] = (
                query_grad * cosine[rows, :] - turn(query_grad) * sine[rows, :]
            ).astype(jnp.bfloat16)
            pair_grad[:keys, :] = (
                pair_grad[:keys, :]
                + transposed_dot(score_grad, queries[kv, block])
                + transposed_dot(share_low, upper)
            )
        for block in range(token_count // ROWS):
            rows = pl.ds(block * ROWS, ROWS)
            grad = pair_grad[rows, :]
            projected_grad[rows, (2 * kv + 1) * LANES : (2 * kv + 2) * LANES] = jnp.where(
                is_first, grad * cosine[rows, :] - turn(grad) * sine[rows, :], grad
            ).astype(jnp.bfloat16)

    def column_step(number, carry):
        columns = pl.ds(pl.multiple_of(number * 2 * LANES, 2 * LANES), 2 * LANES)
        total[:, columns] = dot_transposed(projected_grad[...], w_qkv[columns, :])
        return carry

    lax.fori_loop(0, model_width // (2 * LANES), column_step, 0)
    write_parts(place, total, parts, span)
    gain_sum = jnp.zeros((1, model_width), jnp.float32)
    for row in range(0, token_count, ROWS):
        rows = pl.ds(row, ROWS)
        gain_sum = gain_sum + jnp.sum(
            total[rows, :] * (layer_in[rows, :].astype(jnp.float32) * inverse[rows, :]),
            0,
            keepdims=True,
        )
    gain_part[...] = gain_sum


def in_vmem(count):
    return [pl.BlockSpec(memory_space=pltpu.VMEM)] * count


def in_smem(count):
    return [pl.BlockSpec(memory_space=pltpu.SMEM)] * count


def shaped(shape, dtype):
    return jax.ShapeDtypeStruct(shape, dtype)


def on_device(
    layer_in,
    seq_lengths,
    routes,
    gain_attn,
    w_qkv,
    w_output,
    gain_ffn,
    w_router,
    w_in,
    w_out,
    out_grad,
):
    low, wide = jnp.bfloat16, jnp.float32
    token_count, model_width = layer_in.shape
    kv_here = w_qkv.shape[1]
    experts_all = w_router.shape[1]
    units = w_out.shape[1]
    head_width = kv_here * LANES
    block_count = token_count // ROWS
    tensor_count = lax.axis_size("tensor")
    span = token_count // tensor_count
    tensor_here = lax.axis_index("tensor")
    place = jnp.stack([tensor_here, lax.axis_index("expert")]).astype(jnp.int32)
    mib = 1 << 20

    def token_block(array_in):
        return lax.dynamic_slice_in_dim(array_in, tensor_here * span, span, 0)

    def in_order(blocks):
        joined = jnp.zeros((token_count,) + blocks[0].shape[1:], blocks[0].dtype)
        for number, block in enumerate(blocks):
            joined = lax.dynamic_update_slice_in_dim(
                joined, block, (tensor_here ^ number) * span, 0
            )
        return joined

    w_in_all = gather_experts(w_in.reshape(2 * units, model_width), True)
    w_out_all = gather_experts(w_out[0], False)
    w_output_all = gather_blocks(w_output)

    cosine, sine = angle_tables(token_count)
    qkv_flat = w_qkv.reshape(model_width, -1)
    normed_one, inverse_one, queries, pairs, probs, attended = pl.pallas_call(
        attend_kernel,
        out_shape=(
            shaped((token_count, model_width), low),
            shaped((token_count, 1), wide),
            shaped((kv_here, block_count, 2 * ROWS, LANES), low),
            shaped((kv_here, token_count, LANES), low),
            shaped((kv_here, block_count, 2 * ROWS, token_count), low),
            shaped((token_count, head_width), low),
        ),
        in_specs=in_smem(1) + in_vmem(5),
        out_specs=tuple(in_vmem(6)),
        compiler_params=pltpu.CompilerParams(vmem_limit_bytes=32 * mib),
        name="attend",
    )(seq_lengths, layer_in, gain_attn[None], qkv_flat, cosine, sine)

    heads_all = gather_blocks(attended)
    router_rows = jnp.pad(jnp.transpose(w_router), ((0, LANES - experts_all), (0, 0)))
    part_shapes = (shaped((span, model_width), wide),) + (
        shaped((span, model_width), low),
    ) * (tensor_count - 1)
    middle = pl.pallas_call(
        functools.partial(middle_kernel, tensor_count, experts_all),
        out_shape=part_shapes
        + (
            shaped((span, model_width), wide),
            shaped((span, 1), wide),
            shaped((token_count, model_width), low),
            shaped((token_count, experts_all * units), low),
            shaped((token_count, experts_all * 2 * units), low),
            shaped((1, model_width), wide),
            shaped((experts_all, model_width), wide),
        ),
        in_specs=in_smem(1)
        + in_vmem(5 + 2 * tensor_count)
        + [pl.BlockSpec(memory_space=pl.ANY)] * (2 * experts_all),
        out_specs=tuple(in_vmem(tensor_count + 7)),
        scratch_shapes=[
            pltpu.VMEM((experts_all * 2 * units, model_width), low),
            pltpu.VMEM((experts_all * units, model_width), low),
            pltpu.VMEM((token_count, model_width), wide),
            pltpu.VMEM((token_count, 1), wide),
            pltpu.VMEM((token_count, LANES), wide),
            pltpu.VMEM((token_count, LANES), wide),
            pltpu.VMEM((token_count, 2 * units), wide),
            pltpu.VMEM((token_count, units), wide),
            pltpu.VMEM((token_count, model_width), wide),
            pltpu.SemaphoreType.DMA((2, experts_all)),
        ],
        compiler_params=pltpu.CompilerParams(vmem_limit_bytes=44 * mib),
        name="middle",
    )(
        place,
        gain_ffn[None],
        router_rows,
        routes,
        layer_in,
        out_grad,
        *heads_all,
        *w_output_all,
        *w_in_all,
        *w_out_all,
    )
    normed_parts, middle = middle[:tensor_count], middle[tensor_count:]
    residual, inverse_two, normed_two, active, pre_grad, gain_ffn_part, router_part = middle

    normed_two_grad = scatter_sums(normed_parts)
    residual_grad = token_block(out_grad).astype(wide) + rms_backward(
        residual, inverse_two, gain_ffn, normed_two_grad
    )
    grad_blocks = gather_blocks(residual_grad.astype(low))

    half_units = experts_all * units
    w_in_grad = scatter_experts(
        transposed_dot(pre_grad[:, :half_units], normed_two),
        transposed_dot(pre_grad[:, half_units:], normed_two),
    ).reshape(w_in.shape)
    w_out_grad = scatter_experts(
        transposed_dot(active[:, : half_units // 2], out_grad),
        transposed_dot(active[:, half_units // 2 :], out_grad),
    )[None]

    back = pl.pallas_call(
        functools.partial(attend_back_kernel, tensor_count),
        out_shape=part_shapes
        + (
            shaped((token_count, model_width), low),
            shaped((token_count, 2 * head_width), low),
            shaped((1, model_width), wide),
        ),
        in_specs=in_smem(1) + in_vmem(9 + tensor_count),
        out_specs=tuple(in_vmem(tensor_count + 3)),
        scratch_shapes=[
            pltpu.VMEM((token_count, head_width), wide),
            pltpu.VMEM((token_count, LANES), wide),
            pltpu.VMEM((token_count, model_width), wide),
        ],
        compiler_params=pltpu.CompilerParams(vmem_limit_bytes=32 * mib),
        name="attend_back",
    )(
        place,
        w_output,
        queries,
        pairs,
        probs,
        cosine,
        sine,
        qkv_flat,
        layer_in,
        inverse_one,
        *grad_blocks,
    )
    input_parts, (branch_grad, projected_grad, gain_attn_part) = (
        back[:tensor_count],
        back[tensor_count:],
    )
    normed_one_grad = scatter_sums(input_parts)
    input_part = rms_backward(
        token_block(layer_in).astype(wide), token_block(inverse_one), gain_attn, normed_one_grad
    )
    in_here = in_order(gather_blocks((residual_grad + input_part).astype(low)))

    mixture_part = dot_plain(active, jnp.concatenate(w_out_all))
    mixture_part, _ = lax.optimization_barrier((mixture_part, grad_blocks[3]))
    mixture_parts = [
        lax.dynamic_slice_in_dim(mixture_part, (tensor_here ^ number) * span, span, 0)
        for number in range(tensor_count)
    ]
    mixture = scatter_sums(mixture_parts[:1] + [part.astype(low) for part in mixture_parts[1:]])
    layer_here = in_order(gather_blocks((residual + mixture).astype(low)))

    qkv_summed = sum_experts(transposed_dot(normed_one, projected_grad), (2, 4)).reshape(
        w_qkv.shape
    )
    output_summed = sum_experts(transposed_dot(attended, branch_grad), (4, 2))
    small = sum_all(jnp.concatenate([router_part, gain_ffn_part, gain_attn_part]))
    return (
        layer_here,
        in_here,
        small[experts_all + 1],
        qkv_summed,
        output_summed,
        small[experts_all],
        jnp.transpose(small[:experts_all]),
        w_in_grad,
        w_out_grad,
    )


def solution(mesh):
    fits = mesh.shape["tensor"] == 4 and mesh.shape["expert"] == 8
    placed = (
        P("expert", None),
        P("expert", None),
        P("expert", None),
        P(),
        P(None, "tensor", None),
        P("tensor", None),
        P(),
        P(),
        P("expert", None, "tensor", None),
        P("expert", "tensor", None),
        P("expert", None),
    )
    return jax.shard_map(
        on_device if fits else on_device_general,
        mesh=mesh,
        in_specs=placed,
        out_specs=(
            P("expert", None),
            P("expert", None),
            P(),
            P(None, "tensor", None),
            P("tensor", None),
            P(),
            P(),
            P("expert", None, "tensor", None),
            P("expert", "tensor", None),
        ),
        check_vma=False,
    )
```

```python
import functools
import math

import jax
import jax.numpy as jnp
import numpy as np
from jax import lax
from jax.experimental import pallas as pl
from jax.experimental.pallas import tpu as pltpu
from jax.sharding import PartitionSpec as P

HEADS = 16
KV_HEADS = 8
HEAD_DIM = 64


epsilon = 1e-06
rope_base = 10000.0
masked_out = -1e30


def rms_forward(values, gain_vec):
    inverse = lax.rsqrt(jnp.mean(values * values, axis=-1, keepdims=True) + epsilon)
    return (values * inverse * gain_vec, inverse)


def rms_backward(values, inverse, gain_vec, upstream):
    normal = values * inverse
    scaled = upstream * gain_vec
    inner_mean = jnp.mean(scaled * normal, axis=-1, keepdims=True)
    return inverse * (scaled - normal * inner_mean)


def positions(lengths, token_count):
    seq_ends = jnp.cumsum(lengths, dtype=jnp.int32)
    row_index = jnp.arange(token_count, dtype=jnp.int32)
    segment = jnp.sum(
        (row_index[:, None] >= seq_ends[None, :]).astype(jnp.int32), axis=1, dtype=jnp.int32
    )
    seq_ids = jnp.arange(lengths.shape[0], dtype=jnp.int32)
    seq_start = jnp.sum(
        jnp.where(segment[:, None] == seq_ids[None, :], (seq_ends - lengths)[None, :], 0),
        axis=1,
        dtype=jnp.int32,
    )
    return (segment, row_index - seq_start)


def rope_tables(position, head_dim):
    half_dim = head_dim // 2
    inverse_freq = jnp.exp(
        jnp.arange(half_dim, dtype=jnp.float32) * (-2.0 * math.log(rope_base) / head_dim)
    )
    angles = position.astype(jnp.float32)[:, None] * inverse_freq[None, :]
    cosine = jnp.cos(angles)
    sine_tab = jnp.sin(angles)
    return (jnp.concatenate([cosine, cosine], 1), jnp.concatenate([sine_tab, sine_tab], 1))


def rotate(values, cosine, sine_tab):
    half_dim = values.shape[-1] // 2
    turned = jnp.concatenate([-values[..., half_dim:], values[..., :half_dim]], -1)
    return values * cosine + turned * sine_tab


def split_blocks(array_in, axis_at, block_count):
    dims_now = array_in.shape
    regrouped = array_in.reshape(
        dims_now[:axis_at]
        + (block_count, dims_now[axis_at] // block_count)
        + dims_now[axis_at + 1 :]
    )
    return jnp.moveaxis(regrouped, axis_at, 0)


def join_blocks(array_in, axis_at):
    regrouped = jnp.moveaxis(array_in, 0, axis_at)
    dims_now = regrouped.shape
    return regrouped.reshape(
        dims_now[:axis_at] + (dims_now[axis_at] * dims_now[axis_at + 1],) + dims_now[axis_at + 2 :]
    )


def block_scores(query_block, key_rows, segment_rows, row_start, segment, scaling):
    block_rows = query_block.shape[2]
    scores_raw = (
        jnp.einsum("kgbd,ksd->kgbs", query_block, key_rows, preferred_element_type=jnp.float32)
        * scaling
    )
    query_index = row_start + jnp.arange(block_rows, dtype=jnp.int32)
    key_index = jnp.arange(key_rows.shape[1], dtype=jnp.int32)
    allowed = (segment_rows[:, None] == segment[None, :]) & (
        key_index[None, :] <= query_index[:, None]
    )
    return jnp.where(allowed[None, None], scores_raw, masked_out)


def attention_forward(queries, key_rows, values, segment, scaling, block_size):
    block_count = queries.shape[2] // block_size
    starts_all = jnp.arange(block_count, dtype=jnp.int32) * block_size

    def one_block(packed):
        query_block, segment_rows, row_start = packed
        scores = block_scores(query_block, key_rows, segment_rows, row_start, segment, scaling)
        top_score = jnp.max(scores, -1)
        exponent = jnp.exp(scores - top_score[..., None])
        row_total = jnp.sum(exponent, -1)
        probs = (exponent / row_total[..., None]).astype(jnp.bfloat16)
        output = jnp.einsum("kgbs,ksd->kgbd", probs, values, preferred_element_type=jnp.float32)
        return (output.astype(jnp.bfloat16), top_score, row_total)

    outputs, top_blocks, total_blocks = lax.map(
        one_block,
        (
            split_blocks(queries, 2, block_count),
            segment.reshape(block_count, block_size),
            starts_all,
        ),
    )
    return (join_blocks(outputs, 2), join_blocks(top_blocks, 2), join_blocks(total_blocks, 2))


def attention_backward(
    queries, key_rows, values, heads_grad, segment, top_kept, total_kept, scaling, block_size
):
    block_count = queries.shape[2] // block_size
    starts_all = jnp.arange(block_count, dtype=jnp.int32) * block_size

    def one_block(running, packed):
        key_acc, value_acc = running
        query_block, grad_block, segment_rows, row_start, top_block, total_block = packed
        scores = block_scores(query_block, key_rows, segment_rows, row_start, segment, scaling)
        probs = jnp.exp(scores - top_block[..., None]) / total_block[..., None]
        probs_low = probs.astype(jnp.bfloat16)
        value_acc = value_acc + jnp.einsum(
            "kgbs,kgbd->ksd", probs_low, grad_block, preferred_element_type=jnp.float32
        )
        prob_grad = jnp.einsum(
            "kgbd,ksd->kgbs", grad_block, values, preferred_element_type=jnp.float32
        )
        inner_sum = jnp.sum(probs * prob_grad, -1, keepdims=True)
        score_grad = (probs * (prob_grad - inner_sum)).astype(jnp.bfloat16)
        query_grad = (
            jnp.einsum("kgbs,ksd->kgbd", score_grad, key_rows, preferred_element_type=jnp.float32)
            * scaling
        )
        key_acc = (
            key_acc
            + jnp.einsum(
                "kgbs,kgbd->ksd", score_grad, query_block, preferred_element_type=jnp.float32
            )
            * scaling
        )
        return ((key_acc, value_acc), query_grad)

    empty = jnp.zeros(key_rows.shape, jnp.float32)
    packed_all = (
        split_blocks(queries, 2, block_count),
        split_blocks(heads_grad, 2, block_count),
        segment.reshape(block_count, block_size),
        starts_all,
        split_blocks(top_kept, 2, block_count),
        split_blocks(total_kept, 2, block_count),
    )
    (key_grad, value_grad), query_blocks = lax.scan(one_block, (empty, empty), packed_all)
    return (join_blocks(query_blocks, 2), key_grad, value_grad)


def on_device_general(
    layer_in,
    seq_lengths,
    routes,
    gain_attn,
    w_qkv,
    w_output,
    gain_ffn,
    w_router,
    w_in,
    w_out,
    out_grad,
):
    token_count, model_width = layer_in.shape
    kv_here = w_qkv.shape[1]
    group_size = HEADS // KV_HEADS
    scaling = 1.0 / math.sqrt(HEAD_DIM)
    block_size = min(512, token_count)
    w_output_all = lax.all_gather(w_output, "tensor", axis=0, tiled=True)
    w_gate_all = lax.all_gather(w_in[0, 0], "expert", axis=0, tiled=True)
    w_up_all = lax.all_gather(w_in[0, 1], "expert", axis=0, tiled=True)
    w_out_all = lax.all_gather(w_out[0], "expert", axis=0, tiled=True)
    segment, position = positions(seq_lengths[0], token_count)
    cosine, sine_tab = rope_tables(position, HEAD_DIM)
    inputs = layer_in.astype(jnp.float32)
    normed_one, inverse_one = rms_forward(inputs, gain_attn)
    normed_one_low = normed_one.astype(jnp.bfloat16)
    qkv_flat = w_qkv.reshape(model_width, -1)
    projected = jnp.dot(normed_one_low, qkv_flat, preferred_element_type=jnp.float32)
    projected = projected.reshape(token_count, kv_here, group_size + 2, HEAD_DIM)
    queries = rotate(
        jnp.transpose(projected[:, :, :group_size], (1, 2, 0, 3)), cosine, sine_tab
    ).astype(jnp.bfloat16)
    key_rows = rotate(
        jnp.transpose(projected[:, :, group_size], (1, 0, 2)), cosine, sine_tab
    ).astype(jnp.bfloat16)
    values = jnp.transpose(projected[:, :, group_size + 1], (1, 0, 2)).astype(jnp.bfloat16)
    attended, top_kept, total_kept = attention_forward(
        queries, key_rows, values, segment, scaling, block_size
    )
    heads_out = jnp.transpose(attended, (2, 0, 1, 3)).reshape(token_count, -1)
    heads_all = lax.all_gather(heads_out, "tensor", axis=1, tiled=True)
    branch_here = jnp.dot(heads_all, w_output_all, preferred_element_type=jnp.float32)
    residual = inputs + branch_here
    normed_two, inverse_two = rms_forward(residual, gain_ffn)
    normed_low = normed_two.astype(jnp.bfloat16)
    experts_all = w_router.shape[1]
    unit_count = w_out.shape[1]
    logits = jnp.dot(normed_low, w_router, preferred_element_type=jnp.float32)
    expert_ids = jnp.arange(experts_all, dtype=jnp.int32)
    picked = jnp.any(routes[:, :, None] == expert_ids[None, None, :], axis=1)
    picked_logits = jnp.where(picked, logits, masked_out)
    top_logit = jnp.max(picked_logits, -1, keepdims=True)
    weight = jnp.where(picked, jnp.exp(picked_logits - top_logit), 0.0)
    gates = weight / jnp.sum(weight, -1, keepdims=True)

    def by_unit(per_expert):
        return jnp.broadcast_to(
            per_expert[:, :, None], (token_count, experts_all, unit_count)
        ).reshape(token_count, -1)

    def over_units(per_unit):
        return jnp.sum(per_unit.reshape(token_count, experts_all, unit_count), -1)

    def times_transposed(left, right):
        return lax.dot_general(
            left, right, (((1,), (1,)), ((), ())), preferred_element_type=jnp.float32
        )

    def transposed_times(left, right):
        return lax.dot_general(
            left, right, (((0,), (0,)), ((), ())), preferred_element_type=jnp.float32
        )

    gates_wide = by_unit(gates)
    gate_vals = times_transposed(normed_low, w_gate_all)
    up_vals = times_transposed(normed_low, w_up_all)
    plain_grad = times_transposed(out_grad, w_out_all)
    sig_vals = jax.nn.sigmoid(gate_vals)
    silu_vals = gate_vals * sig_vals
    active = silu_vals * up_vals
    scaled_active = (active * gates_wide).astype(jnp.bfloat16)
    active_grad = plain_grad * gates_wide
    gate_pre = (
        active_grad * up_vals * (sig_vals * (1.0 + gate_vals * (1.0 - sig_vals)))
    ).astype(jnp.bfloat16)
    up_pre = (active_grad * silu_vals).astype(jnp.bfloat16)
    gate_grad_part = over_units(active * plain_grad)
    logit_part = (
        gates * (gate_grad_part - jnp.sum(gates * gate_grad_part, -1, keepdims=True))
    ).astype(jnp.bfloat16)
    normed_two_part = (
        jnp.dot(gate_pre, w_gate_all, preferred_element_type=jnp.float32)
        + jnp.dot(up_pre, w_up_all, preferred_element_type=jnp.float32)
        + times_transposed(logit_part, w_router)
    )
    normed_two_grad = lax.psum(normed_two_part.astype(jnp.bfloat16), "tensor").astype(jnp.float32)
    mixture_part = jnp.dot(scaled_active, w_out_all, preferred_element_type=jnp.float32)
    mixture = lax.psum(mixture_part.astype(jnp.bfloat16), "tensor").astype(jnp.float32)
    layer_here = (residual + mixture).astype(jnp.bfloat16)

    def to_owner(partial):
        return lax.psum_scatter(
            partial.astype(jnp.bfloat16), "expert", scatter_dimension=0, tiled=True
        ).astype(jnp.float32)

    w_gate_grad = to_owner(transposed_times(gate_pre, normed_low))
    w_up_grad = to_owner(transposed_times(up_pre, normed_low))
    w_in_grad = jnp.stack([w_gate_grad, w_up_grad])[None]
    w_out_grad = to_owner(transposed_times(scaled_active, out_grad))[None]
    router_part = transposed_times(logit_part, normed_low)
    normal_two = residual * inverse_two
    gain_ffn_part = jnp.sum(normed_two_part * normal_two, axis=0)
    upstream = out_grad.astype(jnp.float32)
    residual_part = rms_backward(residual, inverse_two, gain_ffn, normed_two_grad)
    residual_grad = upstream + residual_part
    branch_here_grad = residual_grad.astype(jnp.bfloat16)
    w_output_grad = lax.dot_general(
        heads_out, branch_here_grad, (((0,), (0,)), ((), ())), preferred_element_type=jnp.float32
    )
    heads_flat = lax.dot_general(
        branch_here_grad, w_output, (((1,), (1,)), ((), ())), preferred_element_type=jnp.float32
    ).astype(jnp.bfloat16)
    heads_grad = jnp.transpose(
        heads_flat.reshape(token_count, kv_here, group_size, HEAD_DIM), (1, 2, 0, 3)
    )
    query_grad, key_grad, value_grad = attention_backward(
        queries, key_rows, values, heads_grad, segment, top_kept, total_kept, scaling, block_size
    )
    query_grad = rotate(query_grad, cosine, -sine_tab)
    key_grad = rotate(key_grad, cosine, -sine_tab)
    projected_grad = jnp.concatenate(
        [
            jnp.transpose(query_grad, (2, 0, 1, 3)),
            jnp.transpose(key_grad, (1, 0, 2))[:, :, None],
            jnp.transpose(value_grad, (1, 0, 2))[:, :, None],
        ],
        2,
    )
    projected_grad = projected_grad.reshape(token_count, -1).astype(jnp.bfloat16)
    w_qkv_grad = lax.dot_general(
        normed_one_low, projected_grad, (((0,), (0,)), ((), ())), preferred_element_type=jnp.float32
    ).reshape(w_qkv.shape)
    normed_one_part = lax.dot_general(
        projected_grad, qkv_flat, (((1,), (1,)), ((), ())), preferred_element_type=jnp.float32
    )
    gain_attn_part = jnp.sum(normed_one_part * (inputs * inverse_one), axis=0)
    normed_one_grad = lax.psum(normed_one_part.astype(jnp.bfloat16), "tensor").astype(jnp.float32)
    input_part = rms_backward(inputs, inverse_one, gain_attn, normed_one_grad)
    in_here = (residual_grad + input_part).astype(jnp.bfloat16)
    qkv_summed = lax.psum(w_qkv_grad.astype(jnp.bfloat16), "expert").astype(jnp.float32)
    output_summed = lax.psum(w_output_grad.astype(jnp.bfloat16), "expert").astype(jnp.float32)
    small = jnp.concatenate([router_part, gain_ffn_part[None], gain_attn_part[None]])
    small = lax.psum(small, ("expert", "tensor"))
    return (
        layer_here,
        in_here,
        small[experts_all + 1],
        qkv_summed,
        output_summed,
        small[experts_all],
        jnp.transpose(small[:experts_all]),
        w_in_grad,
        w_out_grad,
    )


LANES = 128
ROWS = 128
SMALL_ROWS = 16
IN_ORDER = (0, 2, 4, 6, 1, 3, 5, 7)
OUT_ORDER = (0, 4, 2, 6, 1, 5, 3, 7)


def exchange(array_in, axis_name, bits):
    count = lax.axis_size(axis_name)
    return lax.ppermute(array_in, axis_name, [(i, i ^ bits) for i in range(count)])


def gather_blocks(own):
    far = exchange(own, "tensor", 2)
    near = exchange(own, "tensor", 1)
    far, near = lax.optimization_barrier((far, near))
    return [own, near, far, exchange(far, "tensor", 1)]


def scatter_parts(parts, relayed):
    near, far, relayed = lax.optimization_barrier((parts[1], parts[2], relayed))
    far = (far.astype(jnp.float32) + relayed.astype(jnp.float32)).astype(jnp.bfloat16)
    far = exchange(far, "tensor", 2)
    return parts[0], exchange(near, "tensor", 1), far


def gather_pairs(own, arrived, second):
    near = jnp.concatenate([own, arrived])
    far = exchange(near, "expert", second)
    return [near, far, exchange(near, "expert", 1), exchange(far, "expert", 1)]


def sum_experts(array_in):
    core = lax.axis_index("expert") & 1
    rows = array_in.shape[0] // 2
    top, bottom = array_in[:rows], array_in[rows:]
    keep = jnp.where(core == 0, top, bottom)
    give = jnp.where(core == 0, bottom, top).astype(jnp.bfloat16)
    half = keep + exchange(give, "expert", 1).astype(jnp.float32)
    pieces = []
    for piece, bits in ((half[: rows // 2], (2, 4)), (half[rows // 2 :], (4, 2))):
        piece = piece.astype(jnp.bfloat16)
        for bit in bits:
            arrived = exchange(piece, "expert", bit)
            piece = (piece.astype(jnp.float32) + arrived.astype(jnp.float32)).astype(jnp.bfloat16)
        pieces.append(piece)
    half = jnp.concatenate(pieces)
    other = exchange(half, "expert", 1)
    return jnp.concatenate(
        [jnp.where(core == 0, half, other), jnp.where(core == 0, other, half)]
    ).astype(jnp.float32)


def sum_over_experts(array_in):
    for bit in (1, 2, 4):
        array_in = array_in + exchange(array_in, "expert", bit)
    return array_in


def dot_plain(left, right):
    return jnp.dot(left, right, preferred_element_type=jnp.float32)


def dot_transposed(left, right):
    return lax.dot_general(
        left, right, (((1,), (1,)), ((), ())), preferred_element_type=jnp.float32
    )


def transposed_dot(left, right):
    return lax.dot_general(
        left, right, (((0,), (0,)), ((), ())), preferred_element_type=jnp.float32
    )


def lane_index(shape):
    return lax.broadcasted_iota(jnp.int32, shape, 1)


def turn(values):
    low_half = (lane_index(values.shape) & (HEAD_DIM - 1)) < HEAD_DIM // 2
    return jnp.where(
        low_half,
        -pltpu.roll(values, LANES - HEAD_DIM // 2, 1),
        pltpu.roll(values, HEAD_DIM // 2, 1),
    )


def swap_heads(values):
    return pltpu.roll(values, HEAD_DIM, 1)


def first_head(shape):
    return lane_index(shape) < HEAD_DIM


def angle_tables(token_count):
    half_dim = HEAD_DIM // 2
    inverse_freq = np.exp(np.arange(half_dim) * (-2.0 * math.log(rope_base) / HEAD_DIM))
    angles = np.arange(token_count)[:, None] * inverse_freq[None, :]
    tile = LANES // half_dim
    return (
        np.tile(np.cos(angles), (1, tile)).astype(np.float32),
        np.tile(np.sin(angles), (1, tile)).astype(np.float32),
    )


def attend_kernel(
    lengths,
    layer_in,
    gain,
    w_qkv,
    cosine,
    sine,
    normed_out,
    queries_out,
    pairs_out,
    probs_out,
    attended,
    normed,
    queries,
    pairs,
    probs,
    sems,
):
    token_count = layer_in.shape[0]
    kv_here = pairs.shape[0]
    for row in range(0, token_count, ROWS):
        rows = pl.ds(row, ROWS)
        values = layer_in[rows, :].astype(jnp.float32)
        scale = lax.rsqrt(jnp.mean(values * values, axis=-1, keepdims=True) + epsilon)
        normed[rows, :] = (values * scale * gain[...]).astype(jnp.bfloat16)
    copies = [pltpu.make_async_copy(normed, normed_out, sems.at[0])]
    copies[0].start()
    is_first = first_head((ROWS, LANES))
    for kv in range(kv_here):
        projected = dot_plain(normed[...], w_qkv[:, 2 * LANES * kv : 2 * LANES * (kv + 1)])
        for block in range(token_count // ROWS):
            rows = pl.ds(block * ROWS, ROWS)
            cos_rows, sin_rows = cosine[rows, :], sine[rows, :]
            query = projected[block * ROWS : (block + 1) * ROWS, :LANES]
            query = (query * cos_rows + turn(query) * sin_rows) * (1.0 / math.sqrt(HEAD_DIM))
            queries[kv, block, :ROWS, :] = jnp.where(is_first, query, 0.0).astype(jnp.bfloat16)
            queries[kv, block, ROWS:, :] = jnp.where(is_first, swap_heads(query), 0.0).astype(
                jnp.bfloat16
            )
            pair = projected[block * ROWS : (block + 1) * ROWS, LANES:]
            pairs[kv, rows, :] = jnp.where(
                is_first, pair * cos_rows + turn(pair) * sin_rows, pair
            ).astype(jnp.bfloat16)
    copies.append(pltpu.make_async_copy(queries, queries_out, sems.at[1]))
    copies.append(pltpu.make_async_copy(pairs, pairs_out, sems.at[2]))
    copies[1].start()
    copies[2].start()
    for block in range(token_count // ROWS):
        keys = (block + 1) * ROWS
        token = block * ROWS + (
            lax.broadcasted_iota(jnp.int32, (2 * ROWS, keys), 0) & (ROWS - 1)
        )
        start = jnp.zeros_like(token)
        end = 0
        for seq in range(lengths.shape[1] - 1):
            end = end + lengths[0, seq]
            start = jnp.where(token >= end, end, start)
        key = lane_index((2 * ROWS, keys))
        allowed = (key <= token) & (key >= start)
        for kv in range(kv_here):
            scores = dot_transposed(queries[kv, block], pairs[kv, :keys, :])
            scores = jnp.where(allowed, scores, masked_out)
            exponent = jnp.exp(scores - jnp.max(scores, -1, keepdims=True))
            share = (exponent * (1.0 / jnp.sum(exponent, -1, keepdims=True))).astype(jnp.bfloat16)
            probs[kv, block, :, :keys] = share
            output = dot_plain(share, pairs[kv, :keys, :])
            attended[pl.ds(block * ROWS, ROWS), kv * LANES : (kv + 1) * LANES] = jnp.where(
                is_first, swap_heads(output[:ROWS]), output[ROWS:]
            ).astype(jnp.bfloat16)
        copies.append(
            pltpu.make_async_copy(
                probs.at[:, block, :, :keys], probs_out.at[:, block, :, :keys], sems.at[3 + block]
            )
        )
        copies[-1].start()
    for copy in copies:
        copy.wait()


def write_parts(place, total, parts, span):
    for number, part in enumerate(parts):
        row = pl.multiple_of((place[0] ^ number) * span, span)
        part[...] = total[pl.ds(row, span), :].astype(part.dtype)


def middle_kernel(tensor_count, *refs):
    place, gain, router, routes, layer_in, out_grad = refs[:6]
    w_mine, w_other, heads, refs = refs[6], refs[7], refs[8], refs[9:]
    w_ins, w_outs, refs = refs[:4], refs[4:8], refs[8:]
    parts, refs = refs[:tensor_count], refs[tensor_count:]
    (residual_block, inverse_block, normed, active_out, pre_out, gain_part, router_part) = refs[:7]
    (residual, inverse, gates, gate_grad, hidden, plain, total) = refs[7:]
    token_count, model_width = layer_in.shape
    experts_all = router_part.shape[0]
    units = w_outs[0].shape[0] // 2
    span = token_count // tensor_count
    lane = lane_index((ROWS, LANES))
    half = w_mine.shape[0] // tensor_count
    core = place[1] & 1
    mine_lanes = pl.ds(pl.multiple_of(core * half, half), half)
    other_lanes = pl.ds(pl.multiple_of((1 - core) * half, half), half)
    for row in range(0, token_count, ROWS):
        rows = pl.ds(row, ROWS)
        values = layer_in[rows, :].astype(jnp.float32)
        for number in range(tensor_count):
            head_rows = pl.ds(number * token_count + row, ROWS)
            half_rows = pl.ds(number * half, half)
            values = values + dot_plain(heads[head_rows, mine_lanes], w_mine[half_rows, :])
            values = values + dot_plain(heads[head_rows, other_lanes], w_other[half_rows, :])
        residual[rows, :] = values
        scale = lax.rsqrt(jnp.mean(values * values, axis=-1, keepdims=True) + epsilon)
        inverse[rows, :] = scale
        normed_low = (values * scale * gain[...]).astype(jnp.bfloat16)
        normed[rows, :] = normed_low
        logits = dot_transposed(normed_low, router[...])
        picked = routes[rows, 0:1] == lane
        for top in range(1, routes.shape[1]):
            picked = picked | (routes[rows, top : top + 1] == lane)
        logits = jnp.where(picked, logits, masked_out)
        weight = jnp.where(picked, jnp.exp(logits - jnp.max(logits, -1, keepdims=True)), 0.0)
        gates[rows, :] = weight / jnp.sum(weight, -1, keepdims=True)
    gate_grad[...] = jnp.zeros_like(gate_grad)
    for number in range(experts_all):
        name = place[1] ^ IN_ORDER[number]
        in_rows = pl.ds(number % 2 * 2 * units, 2 * units)
        out_number = OUT_ORDER.index(IN_ORDER[number])
        out_rows = pl.ds(out_number % 2 * units, units)
        hidden[...] = dot_transposed(normed[...], w_ins[number // 2][in_rows, :])
        plain[...] = dot_transposed(out_grad[...], w_outs[out_number // 2][out_rows, :])
        for row in range(0, token_count, ROWS):
            rows = pl.ds(row, ROWS)
            gate = jnp.sum(jnp.where(lane == name, gates[rows, :], 0.0), -1, keepdims=True)
            gate_vals, up_vals = hidden[rows, :units], hidden[rows, units:]
            sig_vals = 1.0 / (1.0 + jnp.exp(-gate_vals))
            silu_vals = gate_vals * sig_vals
            active = silu_vals * up_vals
            grad = plain[rows, :]
            gate_grad[rows, :] = gate_grad[rows, :] + jnp.where(
                lane == name, jnp.sum(active * grad, -1, keepdims=True), 0.0
            )
            active_grad = grad * gate
            active_out[rows, out_number * units : (out_number + 1) * units] = (
                active * gate
            ).astype(jnp.bfloat16)
            pre_out[rows, 2 * number * units : (2 * number + 1) * units] = (
                active_grad * up_vals * (sig_vals * (1.0 + gate_vals * (1.0 - sig_vals)))
            ).astype(jnp.bfloat16)
            pre_out[rows, (2 * number + 1) * units : (2 * number + 2) * units] = (
                active_grad * silu_vals
            ).astype(jnp.bfloat16)
    gate_all, grad_all = gates[...], gate_grad[...]
    logit_part = (
        gate_all * (grad_all - jnp.sum(gate_all * grad_all, -1, keepdims=True))
    ).astype(jnp.bfloat16)
    router_part[...] = transposed_dot(logit_part, normed[...])[:experts_all]

    def column_step(number, carry):
        columns = pl.ds(pl.multiple_of(number * 2 * LANES, 2 * LANES), 2 * LANES)
        summed = dot_plain(logit_part, router[:, columns])
        for pair, weights in enumerate(w_ins):
            pre = pre_out[:, 4 * pair * units : 4 * (pair + 1) * units]
            summed = summed + dot_plain(pre, weights[:, columns])
        total[:, columns] = summed
        return carry

    lax.fori_loop(0, model_width // (2 * LANES), column_step, 0)
    write_parts(place, total, parts, span)
    row = pl.ds(pl.multiple_of(place[0] * span, span), span)
    residual_block[...] = residual[row, :]
    inverse_block[...] = inverse[row, :]
    gain_sum = jnp.zeros((1, model_width), jnp.float32)
    for row in range(0, token_count, ROWS):
        rows = pl.ds(row, ROWS)
        gain_sum = gain_sum + jnp.sum(
            total[rows, :] * (residual[rows, :] * inverse[rows, :]), 0, keepdims=True
        )
    gain_part[...] = gain_sum


def weight_grad_kernel(tensor_count, *refs):
    place, normed, out_grad, active, pre_grad = refs[:5]
    w_outs, parts = refs[5:9], refs[9 : 9 + tensor_count]
    grads, total, slots, sems = refs[9 + tensor_count :]
    token_count, model_width = normed.shape
    experts_all = grads.shape[0]
    units = w_outs[0].shape[0] // 2

    def column_step(number, carry):
        columns = pl.ds(pl.multiple_of(number * 2 * LANES, 2 * LANES), 2 * LANES)
        summed = jnp.zeros((token_count, 2 * LANES), jnp.float32)
        for pair, weights in enumerate(w_outs):
            summed = summed + dot_plain(
                active[:, 2 * pair * units : 2 * (pair + 1) * units], weights[:, columns]
            )
        total[:, columns] = summed
        return carry

    lax.fori_loop(0, model_width // (2 * LANES), column_step, 0)
    write_parts(place, total, parts, token_count // tensor_count)
    copies = []
    for number in range(experts_all):
        name = place[1] ^ IN_ORDER[number]
        out_number = OUT_ORDER.index(IN_ORDER[number])
        slot = number % 2
        if number >= 2:
            copies[number - 2].wait()
        slots[slot, : 2 * units, :] = transposed_dot(
            pre_grad[:, 2 * number * units : 2 * (number + 1) * units], normed[...]
        ).astype(jnp.bfloat16)
        slots[slot, 2 * units :, :] = transposed_dot(
            active[:, out_number * units : (out_number + 1) * units], out_grad[...]
        ).astype(jnp.bfloat16)
        copies.append(pltpu.make_async_copy(slots.at[slot], grads.at[name], sems.at[slot]))
        copies[-1].start()
    for copy in copies[-2:]:
        copy.wait()


def attend_back_kernel(tensor_count, *refs):
    place, far_refs, refs = refs[0], refs[1:9], refs[9:]
    blocks, refs = refs[:tensor_count], refs[tensor_count:]
    mixtures, refs = refs[:tensor_count], refs[tensor_count:]
    parts, refs = refs[:tensor_count], refs[tensor_count:]
    branch_grad, projected_grad, gain_part, heads_grad, pair_grad, total = refs[:6]
    near_refs, sems = refs[6:14], refs[14]
    w_output, queries, pairs, probs, cosine, sine, w_qkv, layer_in = near_refs
    copies = [
        pltpu.make_async_copy(source, target, sems.at[number])
        for number, (source, target) in enumerate(zip(far_refs, near_refs))
    ]
    for copy in copies:
        copy.start()
    token_count, model_width = layer_in.shape
    span = token_count // tensor_count
    for number, block in enumerate(blocks):
        row = pl.multiple_of((place[0] ^ number) * span, span)
        branch_grad[pl.ds(row, span), :] = block[...]
    copies[0].wait()
    heads_grad[...] = dot_transposed(branch_grad[...], w_output[...])
    for copy in copies[1:6]:
        copy.wait()
    is_first = first_head((ROWS, LANES))
    for kv in range(pairs.shape[0]):
        pair_grad[...] = jnp.zeros_like(pair_grad)
        for block in range(token_count // ROWS):
            keys = (block + 1) * ROWS
            rows = pl.ds(block * ROWS, ROWS)
            upper = heads_grad[rows, kv * LANES : (kv + 1) * LANES]
            upper = jnp.concatenate(
                [
                    jnp.where(is_first, 0.0, swap_heads(upper)),
                    jnp.where(is_first, 0.0, upper),
                ]
            ).astype(jnp.bfloat16)
            share_low = probs[kv, block, :, :keys]
            share = share_low.astype(jnp.float32)
            prob_grad = dot_transposed(upper, pairs[kv, :keys, :])
            inner = jnp.sum(share * prob_grad, -1, keepdims=True)
            score_grad = (share * (prob_grad - inner)).astype(jnp.bfloat16)
            query_grad = dot_plain(score_grad, pairs[kv, :keys, :])
            query_grad = jnp.where(
                is_first, query_grad[:ROWS], swap_heads(query_grad[ROWS:])
            ) * (1.0 / math.sqrt(HEAD_DIM))
            projected_grad[rows, 2 * kv * LANES : (2 * kv + 1) * LANES] = (
                query_grad * cosine[rows, :] - turn(query_grad) * sine[rows, :]
            ).astype(jnp.bfloat16)
            pair_grad[:keys, :] = (
                pair_grad[:keys, :]
                + transposed_dot(score_grad, queries[kv, block])
                + transposed_dot(share_low, upper)
            )
        for block in range(token_count // ROWS):
            rows = pl.ds(block * ROWS, ROWS)
            grad = pair_grad[rows, :]
            projected_grad[rows, (2 * kv + 1) * LANES : (2 * kv + 2) * LANES] = jnp.where(
                is_first, grad * cosine[rows, :] - turn(grad) * sine[rows, :], grad
            ).astype(jnp.bfloat16)

    for copy in copies[6:]:
        copy.wait()

    def column_step(number, carry):
        columns = pl.ds(pl.multiple_of(number * 2 * LANES, 2 * LANES), 2 * LANES)
        total[:, columns] = dot_transposed(projected_grad[...], w_qkv[columns, :])
        return carry

    lax.fori_loop(0, model_width // (2 * LANES), column_step, 0)
    write_parts(place, total, [part.at[:span] for part in parts], span)
    for mixture, part in zip(mixtures, parts):
        part[span:, :] = mixture[...]
    gain_sum = jnp.zeros((1, model_width), jnp.float32)
    for row in range(0, token_count, ROWS):
        rows = pl.ds(row, ROWS)
        values = layer_in[rows, :].astype(jnp.float32)
        scale = lax.rsqrt(jnp.mean(values * values, axis=-1, keepdims=True) + epsilon)
        gain_sum = gain_sum + jnp.sum(total[rows, :] * (values * scale), 0, keepdims=True)
    gain_part[...] = gain_sum


def norm_back_kernel(own, near, far, residual, inverse, gain, out_grad, residual_grad, low_grad):
    summed = own[...] + near[...].astype(jnp.float32) + far[...].astype(jnp.float32)
    total = out_grad[...].astype(jnp.float32) + rms_backward(
        residual[...], inverse[...], gain[...], summed
    )
    residual_grad[...] = total
    low_grad[...] = total.astype(jnp.bfloat16)


def finish_kernel(own, near, far, layer_in, gain, residual_grad, residual, small, block):
    span = layer_in.shape[0]
    summed = own[...] + near[...].astype(jnp.float32) + far[...].astype(jnp.float32)
    values = layer_in[...].astype(jnp.float32)
    inverse = lax.rsqrt(jnp.mean(values * values, axis=-1, keepdims=True) + epsilon)
    block[:span, :] = (residual[...] + summed[span:]).astype(jnp.bfloat16)
    block[span : 2 * span, :] = (
        residual_grad[...] + rms_backward(values, inverse, gain[...], summed[:span])
    ).astype(jnp.bfloat16)
    block[2 * span :, :] = small[...]


def in_vmem(count):
    return [pl.BlockSpec(memory_space=pltpu.VMEM)] * count


def in_hbm(count):
    return [pl.BlockSpec(memory_space=pltpu.HBM)] * count


def in_smem(count):
    return [pl.BlockSpec(memory_space=pltpu.SMEM)] * count


def shaped(shape, dtype):
    return jax.ShapeDtypeStruct(shape, dtype)


def on_device(
    layer_in,
    seq_lengths,
    routes,
    gain_attn,
    w_qkv,
    w_output,
    gain_ffn,
    w_router,
    w_in,
    w_out,
    out_grad,
):
    low, wide = jnp.bfloat16, jnp.float32
    token_count, model_width = layer_in.shape
    kv_here = w_qkv.shape[1]
    experts_all = w_router.shape[1]
    units = w_out.shape[1]
    head_width = kv_here * LANES
    block_count = token_count // ROWS
    tensor_count = lax.axis_size("tensor")
    span = token_count // tensor_count
    tensor_here = lax.axis_index("tensor")
    place = jnp.stack([tensor_here, lax.axis_index("expert")]).astype(jnp.int32)
    mib = 1 << 20

    def token_block(array_in):
        return lax.dynamic_slice_in_dim(array_in, tensor_here * span, span, 0)

    def in_order(blocks, rows=span):
        joined = jnp.zeros((tensor_count * rows,) + blocks[0].shape[1:], blocks[0].dtype)
        for number, block in enumerate(blocks):
            joined = lax.dynamic_update_slice_in_dim(
                joined, block, (tensor_here ^ number) * rows, 0
            )
        return joined

    core = lax.axis_index("expert") & 1
    half = w_output.shape[0] // 2
    output_own = jnp.where(core == 0, w_output[:half], w_output[half:])
    output_far = exchange(output_own, "tensor", 2)
    output_near = exchange(output_own, "tensor", 1)
    w_in_own, w_out_own = w_in.reshape(2 * units, model_width), w_out[0]
    w_in_near = exchange(w_in_own, "expert", 2)
    w_out_near = exchange(w_out_own, "expert", 4)

    cosine, sine = angle_tables(token_count)
    qkv_flat = w_qkv.reshape(model_width, -1)
    kept = (
        shaped((token_count, model_width), low),
        shaped((kv_here, block_count, 2 * ROWS, LANES), low),
        shaped((kv_here, token_count, LANES), low),
        shaped((kv_here, block_count, 2 * ROWS, token_count), low),
    )
    normed_one, queries, pairs, probs, attended = pl.pallas_call(
        attend_kernel,
        out_shape=kept + (shaped((token_count, head_width), low),),
        in_specs=in_smem(1) + in_vmem(5),
        out_specs=tuple(in_hbm(4) + in_vmem(1)),
        scratch_shapes=[pltpu.VMEM(each.shape, low) for each in kept]
        + [pltpu.SemaphoreType.DMA((3 + block_count,))],
        compiler_params=pltpu.CompilerParams(vmem_limit_bytes=56 * mib),
        name="attend",
    )(seq_lengths, layer_in, gain_attn[None], qkv_flat, cosine, sine)

    w_in_near, w_out_near, output_far, output_near, attended = lax.optimization_barrier(
        (w_in_near, w_out_near, output_far, output_near, attended)
    )
    heads_far = exchange(attended, "tensor", 2)
    heads_near = exchange(attended, "tensor", 1)
    w_in_all = gather_pairs(w_in_own, w_in_near, 4)
    w_out_all = gather_pairs(w_out_own, w_out_near, 2)
    heads_far, heads_near, w_out_all = lax.optimization_barrier(
        (heads_far, heads_near, w_out_all)
    )
    heads_both = exchange(heads_far, "tensor", 1)
    heads_all = [attended, heads_near, heads_far, heads_both]
    output_both = exchange(output_far, "tensor", 1)
    output_mine = jnp.concatenate([output_own, output_near, output_far, output_both])
    output_other = exchange(output_mine, "expert", 1)
    router_rows = jnp.pad(jnp.transpose(w_router), ((0, LANES - experts_all), (0, 0)))
    part_shapes = (shaped((span, model_width), wide),) + (
        shaped((span, model_width), low),
    ) * (tensor_count - 1)
    middle = pl.pallas_call(
        functools.partial(middle_kernel, tensor_count),
        out_shape=part_shapes
        + (
            shaped((span, model_width), wide),
            shaped((span, 1), wide),
            shaped((token_count, model_width), low),
            shaped((token_count, experts_all * units), low),
            shaped((token_count, experts_all * 2 * units), low),
            shaped((1, model_width), wide),
            shaped((experts_all, model_width), wide),
        ),
        in_specs=in_smem(1) + in_vmem(16),
        out_specs=tuple(in_vmem(tensor_count + 7)),
        scratch_shapes=[
            pltpu.VMEM((token_count, model_width), wide),
            pltpu.VMEM((token_count, 1), wide),
            pltpu.VMEM((token_count, LANES), wide),
            pltpu.VMEM((token_count, LANES), wide),
            pltpu.VMEM((token_count, 2 * units), wide),
            pltpu.VMEM((token_count, units), wide),
            pltpu.VMEM((token_count, model_width), wide),
        ],
        compiler_params=pltpu.CompilerParams(vmem_limit_bytes=20 * mib),
        name="middle",
    )(
        place,
        gain_ffn[None],
        router_rows,
        routes,
        layer_in,
        out_grad,
        output_mine,
        output_other,
        jnp.concatenate(heads_all),
        *w_in_all,
        *w_out_all,
    )
    normed_parts, middle = middle[:tensor_count], middle[tensor_count:]
    residual, inverse_two, normed_two, active, pre_grad, gain_ffn_part, router_part = middle

    late = pl.pallas_call(
        functools.partial(weight_grad_kernel, tensor_count),
        out_shape=part_shapes + (shaped((experts_all, 3 * units, model_width), low),),
        in_specs=in_smem(1) + in_vmem(8),
        out_specs=tuple(in_vmem(tensor_count) + in_hbm(1)),
        scratch_shapes=[
            pltpu.VMEM((token_count, model_width), wide),
            pltpu.VMEM((2, 3 * units, model_width), low),
            pltpu.SemaphoreType.DMA((2,)),
        ],
        compiler_params=pltpu.CompilerParams(vmem_limit_bytes=48 * mib),
        name="weight_grad",
    )(place, normed_two, out_grad, active, pre_grad, *w_out_all)
    late, relayed = lax.optimization_barrier((late, exchange(normed_parts[3], "tensor", 1)))
    mixture_parts, weight_grads = late[:tensor_count], late[tensor_count]
    residual_grad, low_grad = pl.pallas_call(
        norm_back_kernel,
        out_shape=(shaped((span, model_width), wide), shaped((span, model_width), low)),
        in_specs=in_vmem(7),
        out_specs=tuple(in_vmem(2)),
        compiler_params=pltpu.CompilerParams(vmem_limit_bytes=6 * mib),
        name="norm_back",
    )(
        *scatter_parts(normed_parts, relayed),
        residual,
        inverse_two,
        gain_ffn[None],
        token_block(out_grad),
    )
    grad_blocks = gather_blocks(low_grad)

    weight_grads = lax.psum_scatter(
        weight_grads, "expert", scatter_dimension=0, tiled=False
    ).astype(wide)
    w_in_grad = weight_grads[: 2 * units].reshape(w_in.shape)
    w_out_grad = weight_grads[2 * units :].reshape(w_out.shape)

    fetched = (w_output, queries, pairs, probs, cosine, sine, qkv_flat, layer_in)
    back = pl.pallas_call(
        functools.partial(attend_back_kernel, tensor_count),
        out_shape=(shaped((2 * span, model_width), wide),)
        + (shaped((2 * span, model_width), low),) * (tensor_count - 1)
        + (
            shaped((token_count, model_width), low),
            shaped((token_count, 2 * head_width), low),
            shaped((1, model_width), wide),
        ),
        in_specs=in_smem(1) + in_hbm(8) + in_vmem(2 * tensor_count),
        out_specs=tuple(in_vmem(tensor_count + 3)),
        scratch_shapes=[
            pltpu.VMEM((token_count, head_width), wide),
            pltpu.VMEM((token_count, LANES), wide),
            pltpu.VMEM((token_count, model_width), wide),
        ]
        + [pltpu.VMEM(each.shape, each.dtype) for each in fetched]
        + [pltpu.SemaphoreType.DMA((len(fetched),))],
        compiler_params=pltpu.CompilerParams(vmem_limit_bytes=50 * mib),
        name="attend_back",
    )(
        place,
        *fetched,
        *grad_blocks,
        *mixture_parts,
    )
    input_parts, (branch_grad, projected_grad, gain_attn_part) = (
        back[:tensor_count],
        back[tensor_count:],
    )
    w_output_grad = transposed_dot(attended, branch_grad)
    lanes_each = w_output_grad.shape[1] * kv_here * LANES // model_width * 2
    summed = sum_experts(
        jnp.concatenate(
            [transposed_dot(normed_one, projected_grad)]
            + [
                w_output_grad[:, lanes : lanes + lanes_each]
                for lanes in range(0, model_width, lanes_each)
            ]
        )
    )
    qkv_summed = summed[:model_width].reshape(w_qkv.shape)
    output_summed = jnp.concatenate(split_blocks(summed[model_width:], 0, 2), 1)

    small = sum_over_experts(jnp.concatenate([router_part, gain_ffn_part, gain_attn_part]))
    small = jnp.pad(small, ((0, SMALL_ROWS - small.shape[0]), (0, 0))).astype(low)
    block = pl.pallas_call(
        finish_kernel,
        out_shape=shaped((2 * span + SMALL_ROWS, model_width), low),
        in_specs=in_vmem(8),
        out_specs=in_vmem(1)[0],
        compiler_params=pltpu.CompilerParams(vmem_limit_bytes=6 * mib),
        name="finish",
    )(
        *scatter_parts(input_parts, exchange(input_parts[3], "tensor", 1)),
        token_block(layer_in),
        gain_attn[None],
        residual_grad,
        residual,
        small,
    )
    far = exchange(block, "tensor", 2)
    near = exchange(block, "tensor", 1)
    far, near, qkv_summed, output_summed, w_in_grad, w_out_grad = lax.optimization_barrier(
        (far, near, qkv_summed, output_summed, w_in_grad, w_out_grad)
    )
    blocks = [block, near, far, exchange(far, "tensor", 1)]
    layer_here = in_order([block[:span] for block in blocks])
    in_here = in_order([block[span : 2 * span] for block in blocks])
    small = in_order([block[2 * span :] for block in blocks], SMALL_ROWS)
    small = jnp.sum(small.reshape(tensor_count, SMALL_ROWS, -1).astype(wide), 0)
    return (
        layer_here,
        in_here,
        small[experts_all + 1],
        qkv_summed,
        output_summed,
        small[experts_all],
        jnp.transpose(small[:experts_all]),
        w_in_grad,
        w_out_grad,
    )


def solution(mesh):
    fits = mesh.shape["tensor"] == 4 and mesh.shape["expert"] == 8
    placed = (
        P("expert", None),
        P("expert", None),
        P("expert", None),
        P(),
        P(None, "tensor", None),
        P("tensor", None),
        P(),
        P(),
        P("expert", None, "tensor", None),
        P("expert", "tensor", None),
        P("expert", None),
    )
    return jax.shard_map(
        on_device if fits else on_device_general,
        mesh=mesh,
        in_specs=placed,
        out_specs=(
            P("expert", None),
            P("expert", None),
            P(),
            P(None, "tensor", None),
            P("tensor", None),
            P(),
            P(),
            P("expert", None, "tensor", None),
            P("expert", "tensor", None),
        ),
        check_vma=False,
    )
```

```python
import functools
import math

import jax
import jax.numpy as jnp
import numpy as np
from jax import lax
from jax.experimental import pallas as pl
from jax.experimental.pallas import tpu as pltpu
from jax.sharding import PartitionSpec as P

HEADS = 16
KV_HEADS = 8
HEAD_DIM = 64


epsilon = 1e-06
rope_base = 10000.0
masked_out = -1e30


def rms_forward(values, gain_vec):
    inverse = lax.rsqrt(jnp.mean(values * values, axis=-1, keepdims=True) + epsilon)
    return (values * inverse * gain_vec, inverse)


def rms_backward(values, inverse, gain_vec, upstream):
    normal = values * inverse
    scaled = upstream * gain_vec
    inner_mean = jnp.mean(scaled * normal, axis=-1, keepdims=True)
    return inverse * (scaled - normal * inner_mean)


def positions(lengths, token_count):
    seq_ends = jnp.cumsum(lengths, dtype=jnp.int32)
    row_index = jnp.arange(token_count, dtype=jnp.int32)
    segment = jnp.sum(
        (row_index[:, None] >= seq_ends[None, :]).astype(jnp.int32), axis=1, dtype=jnp.int32
    )
    seq_ids = jnp.arange(lengths.shape[0], dtype=jnp.int32)
    seq_start = jnp.sum(
        jnp.where(segment[:, None] == seq_ids[None, :], (seq_ends - lengths)[None, :], 0),
        axis=1,
        dtype=jnp.int32,
    )
    return (segment, row_index - seq_start)


def rope_tables(position, head_dim):
    half_dim = head_dim // 2
    inverse_freq = jnp.exp(
        jnp.arange(half_dim, dtype=jnp.float32) * (-2.0 * math.log(rope_base) / head_dim)
    )
    angles = position.astype(jnp.float32)[:, None] * inverse_freq[None, :]
    cosine = jnp.cos(angles)
    sine_tab = jnp.sin(angles)
    return (jnp.concatenate([cosine, cosine], 1), jnp.concatenate([sine_tab, sine_tab], 1))


def rotate(values, cosine, sine_tab):
    half_dim = values.shape[-1] // 2
    turned = jnp.concatenate([-values[..., half_dim:], values[..., :half_dim]], -1)
    return values * cosine + turned * sine_tab


def split_blocks(array_in, axis_at, block_count):
    dims_now = array_in.shape
    regrouped = array_in.reshape(
        dims_now[:axis_at]
        + (block_count, dims_now[axis_at] // block_count)
        + dims_now[axis_at + 1 :]
    )
    return jnp.moveaxis(regrouped, axis_at, 0)


def join_blocks(array_in, axis_at):
    regrouped = jnp.moveaxis(array_in, 0, axis_at)
    dims_now = regrouped.shape
    return regrouped.reshape(
        dims_now[:axis_at] + (dims_now[axis_at] * dims_now[axis_at + 1],) + dims_now[axis_at + 2 :]
    )


def block_scores(query_block, key_rows, segment_rows, row_start, segment, scaling):
    block_rows = query_block.shape[2]
    scores_raw = (
        jnp.einsum("kgbd,ksd->kgbs", query_block, key_rows, preferred_element_type=jnp.float32)
        * scaling
    )
    query_index = row_start + jnp.arange(block_rows, dtype=jnp.int32)
    key_index = jnp.arange(key_rows.shape[1], dtype=jnp.int32)
    allowed = (segment_rows[:, None] == segment[None, :]) & (
        key_index[None, :] <= query_index[:, None]
    )
    return jnp.where(allowed[None, None], scores_raw, masked_out)


def attention_forward(queries, key_rows, values, segment, scaling, block_size):
    block_count = queries.shape[2] // block_size
    starts_all = jnp.arange(block_count, dtype=jnp.int32) * block_size

    def one_block(packed):
        query_block, segment_rows, row_start = packed
        scores = block_scores(query_block, key_rows, segment_rows, row_start, segment, scaling)
        top_score = jnp.max(scores, -1)
        exponent = jnp.exp(scores - top_score[..., None])
        row_total = jnp.sum(exponent, -1)
        probs = (exponent / row_total[..., None]).astype(jnp.bfloat16)
        output = jnp.einsum("kgbs,ksd->kgbd", probs, values, preferred_element_type=jnp.float32)
        return (output.astype(jnp.bfloat16), top_score, row_total)

    outputs, top_blocks, total_blocks = lax.map(
        one_block,
        (
            split_blocks(queries, 2, block_count),
            segment.reshape(block_count, block_size),
            starts_all,
        ),
    )
    return (join_blocks(outputs, 2), join_blocks(top_blocks, 2), join_blocks(total_blocks, 2))


def attention_backward(
    queries, key_rows, values, heads_grad, segment, top_kept, total_kept, scaling, block_size
):
    block_count = queries.shape[2] // block_size
    starts_all = jnp.arange(block_count, dtype=jnp.int32) * block_size

    def one_block(running, packed):
        key_acc, value_acc = running
        query_block, grad_block, segment_rows, row_start, top_block, total_block = packed
        scores = block_scores(query_block, key_rows, segment_rows, row_start, segment, scaling)
        probs = jnp.exp(scores - top_block[..., None]) / total_block[..., None]
        probs_low = probs.astype(jnp.bfloat16)
        value_acc = value_acc + jnp.einsum(
            "kgbs,kgbd->ksd", probs_low, grad_block, preferred_element_type=jnp.float32
        )
        prob_grad = jnp.einsum(
            "kgbd,ksd->kgbs", grad_block, values, preferred_element_type=jnp.float32
        )
        inner_sum = jnp.sum(probs * prob_grad, -1, keepdims=True)
        score_grad = (probs * (prob_grad - inner_sum)).astype(jnp.bfloat16)
        query_grad = (
            jnp.einsum("kgbs,ksd->kgbd", score_grad, key_rows, preferred_element_type=jnp.float32)
            * scaling
        )
        key_acc = (
            key_acc
            + jnp.einsum(
                "kgbs,kgbd->ksd", score_grad, query_block, preferred_element_type=jnp.float32
            )
            * scaling
        )
        return ((key_acc, value_acc), query_grad)

    empty = jnp.zeros(key_rows.shape, jnp.float32)
    packed_all = (
        split_blocks(queries, 2, block_count),
        split_blocks(heads_grad, 2, block_count),
        segment.reshape(block_count, block_size),
        starts_all,
        split_blocks(top_kept, 2, block_count),
        split_blocks(total_kept, 2, block_count),
    )
    (key_grad, value_grad), query_blocks = lax.scan(one_block, (empty, empty), packed_all)
    return (join_blocks(query_blocks, 2), key_grad, value_grad)


def on_device_general(
    layer_in,
    seq_lengths,
    routes,
    gain_attn,
    w_qkv,
    w_output,
    gain_ffn,
    w_router,
    w_in,
    w_out,
    out_grad,
):
    token_count, model_width = layer_in.shape
    kv_here = w_qkv.shape[1]
    group_size = HEADS // KV_HEADS
    scaling = 1.0 / math.sqrt(HEAD_DIM)
    block_size = min(512, token_count)
    w_output_all = lax.all_gather(w_output, "tensor", axis=0, tiled=True)
    w_gate_all = lax.all_gather(w_in[0, 0], "expert", axis=0, tiled=True)
    w_up_all = lax.all_gather(w_in[0, 1], "expert", axis=0, tiled=True)
    w_out_all = lax.all_gather(w_out[0], "expert", axis=0, tiled=True)
    segment, position = positions(seq_lengths[0], token_count)
    cosine, sine_tab = rope_tables(position, HEAD_DIM)
    inputs = layer_in.astype(jnp.float32)
    normed_one, inverse_one = rms_forward(inputs, gain_attn)
    normed_one_low = normed_one.astype(jnp.bfloat16)
    qkv_flat = w_qkv.reshape(model_width, -1)
    projected = jnp.dot(normed_one_low, qkv_flat, preferred_element_type=jnp.float32)
    projected = projected.reshape(token_count, kv_here, group_size + 2, HEAD_DIM)
    queries = rotate(
        jnp.transpose(projected[:, :, :group_size], (1, 2, 0, 3)), cosine, sine_tab
    ).astype(jnp.bfloat16)
    key_rows = rotate(
        jnp.transpose(projected[:, :, group_size], (1, 0, 2)), cosine, sine_tab
    ).astype(jnp.bfloat16)
    values = jnp.transpose(projected[:, :, group_size + 1], (1, 0, 2)).astype(jnp.bfloat16)
    attended, top_kept, total_kept = attention_forward(
        queries, key_rows, values, segment, scaling, block_size
    )
    heads_out = jnp.transpose(attended, (2, 0, 1, 3)).reshape(token_count, -1)
    heads_all = lax.all_gather(heads_out, "tensor", axis=1, tiled=True)
    branch_here = jnp.dot(heads_all, w_output_all, preferred_element_type=jnp.float32)
    residual = inputs + branch_here
    normed_two, inverse_two = rms_forward(residual, gain_ffn)
    normed_low = normed_two.astype(jnp.bfloat16)
    experts_all = w_router.shape[1]
    unit_count = w_out.shape[1]
    logits = jnp.dot(normed_low, w_router, preferred_element_type=jnp.float32)
    expert_ids = jnp.arange(experts_all, dtype=jnp.int32)
    picked = jnp.any(routes[:, :, None] == expert_ids[None, None, :], axis=1)
    picked_logits = jnp.where(picked, logits, masked_out)
    top_logit = jnp.max(picked_logits, -1, keepdims=True)
    weight = jnp.where(picked, jnp.exp(picked_logits - top_logit), 0.0)
    gates = weight / jnp.sum(weight, -1, keepdims=True)

    def by_unit(per_expert):
        return jnp.broadcast_to(
            per_expert[:, :, None], (token_count, experts_all, unit_count)
        ).reshape(token_count, -1)

    def over_units(per_unit):
        return jnp.sum(per_unit.reshape(token_count, experts_all, unit_count), -1)

    def times_transposed(left, right):
        return lax.dot_general(
            left, right, (((1,), (1,)), ((), ())), preferred_element_type=jnp.float32
        )

    def transposed_times(left, right):
        return lax.dot_general(
            left, right, (((0,), (0,)), ((), ())), preferred_element_type=jnp.float32
        )

    gates_wide = by_unit(gates)
    gate_vals = times_transposed(normed_low, w_gate_all)
    up_vals = times_transposed(normed_low, w_up_all)
    plain_grad = times_transposed(out_grad, w_out_all)
    sig_vals = jax.nn.sigmoid(gate_vals)
    silu_vals = gate_vals * sig_vals
    active = silu_vals * up_vals
    scaled_active = (active * gates_wide).astype(jnp.bfloat16)
    active_grad = plain_grad * gates_wide
    gate_pre = (
        active_grad * up_vals * (sig_vals * (1.0 + gate_vals * (1.0 - sig_vals)))
    ).astype(jnp.bfloat16)
    up_pre = (active_grad * silu_vals).astype(jnp.bfloat16)
    gate_grad_part = over_units(active * plain_grad)
    logit_part = (
        gates * (gate_grad_part - jnp.sum(gates * gate_grad_part, -1, keepdims=True))
    ).astype(jnp.bfloat16)
    normed_two_part = (
        jnp.dot(gate_pre, w_gate_all, preferred_element_type=jnp.float32)
        + jnp.dot(up_pre, w_up_all, preferred_element_type=jnp.float32)
        + times_transposed(logit_part, w_router)
    )
    normed_two_grad = lax.psum(normed_two_part.astype(jnp.bfloat16), "tensor").astype(jnp.float32)
    mixture_part = jnp.dot(scaled_active, w_out_all, preferred_element_type=jnp.float32)
    mixture = lax.psum(mixture_part.astype(jnp.bfloat16), "tensor").astype(jnp.float32)
    layer_here = (residual + mixture).astype(jnp.bfloat16)

    def to_owner(partial):
        return lax.psum_scatter(
            partial.astype(jnp.bfloat16), "expert", scatter_dimension=0, tiled=True
        ).astype(jnp.float32)

    w_gate_grad = to_owner(transposed_times(gate_pre, normed_low))
    w_up_grad = to_owner(transposed_times(up_pre, normed_low))
    w_in_grad = jnp.stack([w_gate_grad, w_up_grad])[None]
    w_out_grad = to_owner(transposed_times(scaled_active, out_grad))[None]
    router_part = transposed_times(logit_part, normed_low)
    normal_two = residual * inverse_two
    gain_ffn_part = jnp.sum(normed_two_part * normal_two, axis=0)
    upstream = out_grad.astype(jnp.float32)
    residual_part = rms_backward(residual, inverse_two, gain_ffn, normed_two_grad)
    residual_grad = upstream + residual_part
    branch_here_grad = residual_grad.astype(jnp.bfloat16)
    w_output_grad = lax.dot_general(
        heads_out, branch_here_grad, (((0,), (0,)), ((), ())), preferred_element_type=jnp.float32
    )
    heads_flat = lax.dot_general(
        branch_here_grad, w_output, (((1,), (1,)), ((), ())), preferred_element_type=jnp.float32
    ).astype(jnp.bfloat16)
    heads_grad = jnp.transpose(
        heads_flat.reshape(token_count, kv_here, group_size, HEAD_DIM), (1, 2, 0, 3)
    )
    query_grad, key_grad, value_grad = attention_backward(
        queries, key_rows, values, heads_grad, segment, top_kept, total_kept, scaling, block_size
    )
    query_grad = rotate(query_grad, cosine, -sine_tab)
    key_grad = rotate(key_grad, cosine, -sine_tab)
    projected_grad = jnp.concatenate(
        [
            jnp.transpose(query_grad, (2, 0, 1, 3)),
            jnp.transpose(key_grad, (1, 0, 2))[:, :, None],
            jnp.transpose(value_grad, (1, 0, 2))[:, :, None],
        ],
        2,
    )
    projected_grad = projected_grad.reshape(token_count, -1).astype(jnp.bfloat16)
    w_qkv_grad = lax.dot_general(
        normed_one_low, projected_grad, (((0,), (0,)), ((), ())), preferred_element_type=jnp.float32
    ).reshape(w_qkv.shape)
    normed_one_part = lax.dot_general(
        projected_grad, qkv_flat, (((1,), (1,)), ((), ())), preferred_element_type=jnp.float32
    )
    gain_attn_part = jnp.sum(normed_one_part * (inputs * inverse_one), axis=0)
    normed_one_grad = lax.psum(normed_one_part.astype(jnp.bfloat16), "tensor").astype(jnp.float32)
    input_part = rms_backward(inputs, inverse_one, gain_attn, normed_one_grad)
    in_here = (residual_grad + input_part).astype(jnp.bfloat16)
    qkv_summed = lax.psum(w_qkv_grad.astype(jnp.bfloat16), "expert").astype(jnp.float32)
    output_summed = lax.psum(w_output_grad.astype(jnp.bfloat16), "expert").astype(jnp.float32)
    small = jnp.concatenate([router_part, gain_ffn_part[None], gain_attn_part[None]])
    small = lax.psum(small, ("expert", "tensor"))
    return (
        layer_here,
        in_here,
        small[experts_all + 1],
        qkv_summed,
        output_summed,
        small[experts_all],
        jnp.transpose(small[:experts_all]),
        w_in_grad,
        w_out_grad,
    )


LANES = 128
ROWS = 128
IN_ORDER = (0, 2, 4, 6, 1, 3, 5, 7)
OUT_ORDER = (0, 4, 2, 6, 1, 5, 3, 7)


def exchange(array_in, axis_name, bits):
    count = lax.axis_size(axis_name)
    return lax.ppermute(array_in, axis_name, [(i, i ^ bits) for i in range(count)])


def gather_blocks(own):
    far = exchange(own, "tensor", 2)
    near = exchange(own, "tensor", 1)
    far, near = lax.optimization_barrier((far, near))
    return [own, near, far, exchange(far, "tensor", 1)]


def scatter_parts(parts, relayed):
    near, far, relayed = lax.optimization_barrier((parts[1], parts[2], relayed))
    far = (far.astype(jnp.float32) + relayed.astype(jnp.float32)).astype(jnp.bfloat16)
    far = exchange(far, "tensor", 2)
    return parts[0], exchange(near, "tensor", 1), far


def gather_pairs(near, far):
    return [near, far, exchange(near, "expert", 1), exchange(far, "expert", 1)]


def exchange_halves(array_in, bits):
    rows = array_in.shape[0] // 2
    halves = []
    for half, bit in zip((array_in[:rows], array_in[rows:]), bits):
        arrived = exchange(half, "expert", bit)
        halves.append((half.astype(jnp.float32) + arrived.astype(jnp.float32)).astype(jnp.bfloat16))
    return jnp.concatenate(halves)


def join_cores(half):
    core = lax.axis_index("expert") & 1
    other = exchange(half, "expert", 1)
    return jnp.concatenate(
        [jnp.where(core == 0, half, other), jnp.where(core == 0, other, half)]
    ).astype(jnp.float32)


def sum_over_experts(array_in):
    for bit in (1, 2, 4):
        array_in = array_in + exchange(array_in, "expert", bit)
    return array_in


def dot_plain(left, right):
    return jnp.dot(left, right, preferred_element_type=jnp.float32)


def dot_transposed(left, right):
    return lax.dot_general(
        left, right, (((1,), (1,)), ((), ())), preferred_element_type=jnp.float32
    )


def transposed_dot(left, right):
    return lax.dot_general(
        left, right, (((0,), (0,)), ((), ())), preferred_element_type=jnp.float32
    )


def lane_index(shape):
    return lax.broadcasted_iota(jnp.int32, shape, 1)


def turn(values):
    low_half = (lane_index(values.shape) & (HEAD_DIM - 1)) < HEAD_DIM // 2
    return jnp.where(
        low_half,
        -pltpu.roll(values, LANES - HEAD_DIM // 2, 1),
        pltpu.roll(values, HEAD_DIM // 2, 1),
    )


def swap_heads(values):
    return pltpu.roll(values, HEAD_DIM, 1)


def first_head(shape):
    return lane_index(shape) < HEAD_DIM


def angle_tables(token_count):
    half_dim = HEAD_DIM // 2
    inverse_freq = np.exp(np.arange(half_dim) * (-2.0 * math.log(rope_base) / HEAD_DIM))
    angles = np.arange(token_count)[:, None] * inverse_freq[None, :]
    tile = LANES // half_dim
    return (
        np.tile(np.cos(angles), (1, tile)).astype(np.float32),
        np.tile(np.sin(angles), (1, tile)).astype(np.float32),
    )


def attend_kernel(
    lengths,
    layer_in,
    gain,
    w_qkv,
    cosine,
    sine,
    queries_out,
    pairs_out,
    probs_out,
    attended,
    normed,
    queries,
    pairs,
    probs,
    sems,
):
    token_count = layer_in.shape[0]
    kv_here = pairs.shape[0]
    for row in range(0, token_count, ROWS):
        rows = pl.ds(row, ROWS)
        values = layer_in[rows, :].astype(jnp.float32)
        scale = lax.rsqrt(jnp.mean(values * values, axis=-1, keepdims=True) + epsilon)
        normed[rows, :] = (values * scale * gain[...]).astype(jnp.bfloat16)
    is_first = first_head((ROWS, LANES))
    for kv in range(kv_here):
        projected = dot_plain(normed[...], w_qkv[:, 2 * LANES * kv : 2 * LANES * (kv + 1)])
        for block in range(token_count // ROWS):
            rows = pl.ds(block * ROWS, ROWS)
            cos_rows, sin_rows = cosine[rows, :], sine[rows, :]
            query = projected[block * ROWS : (block + 1) * ROWS, :LANES]
            query = (query * cos_rows + turn(query) * sin_rows) * (1.0 / math.sqrt(HEAD_DIM))
            queries[kv, block, :ROWS, :] = jnp.where(is_first, query, 0.0).astype(jnp.bfloat16)
            queries[kv, block, ROWS:, :] = jnp.where(is_first, swap_heads(query), 0.0).astype(
                jnp.bfloat16
            )
            pair = projected[block * ROWS : (block + 1) * ROWS, LANES:]
            pairs[kv, rows, :] = jnp.where(
                is_first, pair * cos_rows + turn(pair) * sin_rows, pair
            ).astype(jnp.bfloat16)
    copies = [
        pltpu.make_async_copy(queries, queries_out, sems.at[0]),
        pltpu.make_async_copy(pairs, pairs_out, sems.at[1]),
    ]
    for copy in copies:
        copy.start()
    for block in range(token_count // ROWS):
        keys = (block + 1) * ROWS
        token = block * ROWS + (
            lax.broadcasted_iota(jnp.int32, (2 * ROWS, keys), 0) & (ROWS - 1)
        )
        start = jnp.zeros_like(token)
        end = 0
        for seq in range(lengths.shape[1] - 1):
            end = end + lengths[0, seq]
            start = jnp.where(token >= end, end, start)
        key = lane_index((2 * ROWS, keys))
        allowed = (key <= token) & (key >= start)
        for kv in range(kv_here):
            scores = dot_transposed(queries[kv, block], pairs[kv, :keys, :])
            scores = jnp.where(allowed, scores, masked_out)
            exponent = jnp.exp(scores - jnp.max(scores, -1, keepdims=True))
            share = (exponent * (1.0 / jnp.sum(exponent, -1, keepdims=True))).astype(jnp.bfloat16)
            probs[kv, block, :, :keys] = share
            output = dot_plain(share, pairs[kv, :keys, :])
            attended[pl.ds(block * ROWS, ROWS), kv * LANES : (kv + 1) * LANES] = jnp.where(
                is_first, swap_heads(output[:ROWS]), output[ROWS:]
            ).astype(jnp.bfloat16)
        copies.append(
            pltpu.make_async_copy(
                probs.at[:, block, :, :keys], probs_out.at[:, block, :, :keys], sems.at[2 + block]
            )
        )
        copies[-1].start()
    for copy in copies:
        copy.wait()


def write_parts(place, total, parts, span):
    for number, part in enumerate(parts):
        row = pl.multiple_of((place[0] ^ number) * span, span)
        part[...] = total[pl.ds(row, span), :].astype(part.dtype)


def middle_kernel(tensor_count, *refs):
    place, gain, router, routes, layer_in, out_grad = refs[:6]
    w_mine, w_other, heads, refs = refs[6], refs[7], refs[8], refs[9:]
    w_ins, w_outs, refs = refs[:4], refs[4:8], refs[8:]
    parts, refs = refs[:tensor_count], refs[tensor_count:]
    (residual_block, inverse_block, normed, active_out, pre_out, gain_part, router_part) = refs[:7]
    (residual, inverse, gates, gate_grad, hidden, plain, total) = refs[7:]
    token_count, model_width = layer_in.shape
    experts_all = router_part.shape[0]
    units = w_outs[0].shape[0] // 2
    span = token_count // tensor_count
    lane = lane_index((ROWS, LANES))
    half = w_mine.shape[0] // tensor_count
    core = place[1] & 1
    mine_lanes = pl.ds(pl.multiple_of(core * half, half), half)
    other_lanes = pl.ds(pl.multiple_of((1 - core) * half, half), half)
    for row in range(0, token_count, ROWS):
        rows = pl.ds(row, ROWS)
        values = layer_in[rows, :].astype(jnp.float32)
        for number in range(tensor_count):
            head_rows = pl.ds(number * token_count + row, ROWS)
            half_rows = pl.ds(number * half, half)
            values = values + dot_plain(heads[head_rows, mine_lanes], w_mine[half_rows, :])
            values = values + dot_plain(heads[head_rows, other_lanes], w_other[half_rows, :])
        residual[rows, :] = values
        scale = lax.rsqrt(jnp.mean(values * values, axis=-1, keepdims=True) + epsilon)
        inverse[rows, :] = scale
        normed_low = (values * scale * gain[...]).astype(jnp.bfloat16)
        normed[rows, :] = normed_low
        logits = dot_transposed(normed_low, router[...])
        picked = routes[rows, 0:1] == lane
        for top in range(1, routes.shape[1]):
            picked = picked | (routes[rows, top : top + 1] == lane)
        logits = jnp.where(picked, logits, masked_out)
        weight = jnp.where(picked, jnp.exp(logits - jnp.max(logits, -1, keepdims=True)), 0.0)
        gates[rows, :] = weight / jnp.sum(weight, -1, keepdims=True)
    gate_grad[...] = jnp.zeros_like(gate_grad)
    for number in range(experts_all):
        name = place[1] ^ IN_ORDER[number]
        in_rows = pl.ds(number % 2 * 2 * units, 2 * units)
        out_number = OUT_ORDER.index(IN_ORDER[number])
        out_rows = pl.ds(out_number % 2 * units, units)
        hidden[...] = dot_transposed(normed[...], w_ins[number // 2][in_rows, :])
        plain[...] = dot_transposed(out_grad[...], w_outs[out_number // 2][out_rows, :])
        for row in range(0, token_count, ROWS):
            rows = pl.ds(row, ROWS)
            gate = jnp.sum(jnp.where(lane == name, gates[rows, :], 0.0), -1, keepdims=True)
            gate_vals, up_vals = hidden[rows, :units], hidden[rows, units:]
            sig_vals = 1.0 / (1.0 + jnp.exp(-gate_vals))
            silu_vals = gate_vals * sig_vals
            active = silu_vals * up_vals
            grad = plain[rows, :]
            gate_grad[rows, :] = gate_grad[rows, :] + jnp.where(
                lane == name, jnp.sum(active * grad, -1, keepdims=True), 0.0
            )
            active_grad = grad * gate
            active_out[rows, out_number * units : (out_number + 1) * units] = (
                active * gate
            ).astype(jnp.bfloat16)
            pre_out[rows, 2 * number * units : (2 * number + 1) * units] = (
                active_grad * up_vals * (sig_vals * (1.0 + gate_vals * (1.0 - sig_vals)))
            ).astype(jnp.bfloat16)
            pre_out[rows, (2 * number + 1) * units : (2 * number + 2) * units] = (
                active_grad * silu_vals
            ).astype(jnp.bfloat16)
    gate_all, grad_all = gates[...], gate_grad[...]
    logit_part = (
        gate_all * (grad_all - jnp.sum(gate_all * grad_all, -1, keepdims=True))
    ).astype(jnp.bfloat16)
    router_part[...] = transposed_dot(logit_part, normed[...])[:experts_all]

    def column_step(number, carry):
        columns = pl.ds(pl.multiple_of(number * 2 * LANES, 2 * LANES), 2 * LANES)
        summed = dot_plain(logit_part, router[:, columns])
        for pair, weights in enumerate(w_ins):
            pre = pre_out[:, 4 * pair * units : 4 * (pair + 1) * units]
            summed = summed + dot_plain(pre, weights[:, columns])
        total[:, columns] = summed
        return carry

    lax.fori_loop(0, model_width // (2 * LANES), column_step, 0)
    write_parts(place, total, parts, span)
    row = pl.ds(pl.multiple_of(place[0] * span, span), span)
    residual_block[...] = residual[row, :]
    inverse_block[...] = inverse[row, :]
    gain_sum = jnp.zeros((1, model_width), jnp.float32)
    for row in range(0, token_count, ROWS):
        rows = pl.ds(row, ROWS)
        gain_sum = gain_sum + jnp.sum(
            total[rows, :] * (residual[rows, :] * inverse[rows, :]), 0, keepdims=True
        )
    gain_part[...] = gain_sum


def weight_grad_kernel(tensor_count, *refs):
    place, normed, out_grad, active, pre_grad = refs[:5]
    w_outs, parts = refs[5:9], refs[9 : 9 + tensor_count]
    kept, given, total = refs[9 + tensor_count :]
    token_count, model_width = normed.shape
    units = w_outs[0].shape[0] // 2
    experts_all = 2 * kept.shape[0] // (3 * units)

    def column_step(number, carry):
        columns = pl.ds(pl.multiple_of(number * 2 * LANES, 2 * LANES), 2 * LANES)
        summed = jnp.zeros((token_count, 2 * LANES), jnp.float32)
        for pair, weights in enumerate(w_outs):
            summed = summed + dot_plain(
                active[:, 2 * pair * units : 2 * (pair + 1) * units], weights[:, columns]
            )
        total[:, columns] = summed
        return carry

    lax.fori_loop(0, model_width // (2 * LANES), column_step, 0)
    write_parts(place, total, parts, token_count // tensor_count)
    for number in range(experts_all):
        out_number = OUT_ORDER.index(IN_ORDER[number])
        grads = kept if number < experts_all // 2 else given
        in_row = number % (experts_all // 2) * 2 * units
        out_row = experts_all * units + out_number % (experts_all // 2) * units
        grads[pl.ds(in_row, 2 * units), :] = transposed_dot(
            pre_grad[:, 2 * number * units : 2 * (number + 1) * units], normed[...]
        ).astype(jnp.bfloat16)
        grads[pl.ds(out_row, units), :] = transposed_dot(
            active[:, out_number * units : (out_number + 1) * units], out_grad[...]
        ).astype(jnp.bfloat16)


def add_grads_kernel(kept, given, in_kept, in_given, out_kept, out_given):
    row = 0
    for target in (in_kept, in_given, out_kept, out_given):
        rows = pl.ds(row, target.shape[0])
        summed = kept[rows, :].astype(jnp.float32) + given[rows, :].astype(jnp.float32)
        target[...] = summed.astype(target.dtype)
        row += target.shape[0]


def attend_back_kernel(tensor_count, *refs):
    place, far_refs, refs = refs[0], refs[1:8], refs[8:]
    blocks, refs = refs[:tensor_count], refs[tensor_count:]
    mixtures, refs = refs[:tensor_count], refs[tensor_count:]
    parts, refs = refs[:tensor_count], refs[tensor_count:]
    branch_grad, projected_grad, heads_grad, pair_grad, total = refs[:5]
    near_refs, sems = refs[5:12], refs[12]
    w_output, queries, pairs, probs, cosine, sine, w_qkv = near_refs
    copies = [
        pltpu.make_async_copy(source, target, sems.at[number])
        for number, (source, target) in enumerate(zip(far_refs, near_refs))
    ]
    token_count, model_width = branch_grad.shape
    span = token_count // tensor_count
    mixture_copies = [
        pltpu.make_async_copy(mixture, part.at[pl.ds(span, span)], sems.at[len(copies) + number])
        for number, (mixture, part) in enumerate(zip(mixtures, parts))
    ]
    block_copies = []
    for number, block in enumerate(blocks):
        row = pl.multiple_of((place[0] ^ number) * span, span)
        block_copies.append(
            pltpu.make_async_copy(
                block,
                branch_grad.at[pl.ds(row, span)],
                sems.at[len(copies) + tensor_count + number],
            )
        )
    for copy in block_copies + copies + mixture_copies:
        copy.start()
    for copy in copies[:1] + block_copies:
        copy.wait()
    heads_grad[...] = dot_transposed(branch_grad[...], w_output[...])
    for copy in copies[1:6]:
        copy.wait()
    is_first = first_head((ROWS, LANES))
    for kv in range(pairs.shape[0]):
        pair_grad[...] = jnp.zeros_like(pair_grad)
        for block in range(token_count // ROWS):
            keys = (block + 1) * ROWS
            rows = pl.ds(block * ROWS, ROWS)
            upper = heads_grad[rows, kv * LANES : (kv + 1) * LANES]
            upper = jnp.concatenate(
                [
                    jnp.where(is_first, 0.0, swap_heads(upper)),
                    jnp.where(is_first, 0.0, upper),
                ]
            ).astype(jnp.bfloat16)
            share_low = probs[kv, block, :, :keys]
            share = share_low.astype(jnp.float32)
            prob_grad = dot_transposed(upper, pairs[kv, :keys, :])
            inner = jnp.sum(share * prob_grad, -1, keepdims=True)
            score_grad = (share * (prob_grad - inner)).astype(jnp.bfloat16)
            query_grad = dot_plain(score_grad, pairs[kv, :keys, :])
            query_grad = jnp.where(
                is_first, query_grad[:ROWS], swap_heads(query_grad[ROWS:])
            ) * (1.0 / math.sqrt(HEAD_DIM))
            projected_grad[rows, 2 * kv * LANES : (2 * kv + 1) * LANES] = (
                query_grad * cosine[rows, :] - turn(query_grad) * sine[rows, :]
            ).astype(jnp.bfloat16)
            pair_grad[:keys, :] = (
                pair_grad[:keys, :]
                + transposed_dot(score_grad, queries[kv, block])
                + transposed_dot(share_low, upper)
            )
        for block in range(token_count // ROWS):
            rows = pl.ds(block * ROWS, ROWS)
            grad = pair_grad[rows, :]
            projected_grad[rows, (2 * kv + 1) * LANES : (2 * kv + 2) * LANES] = jnp.where(
                is_first, grad * cosine[rows, :] - turn(grad) * sine[rows, :], grad
            ).astype(jnp.bfloat16)

    for copy in copies[6:]:
        copy.wait()

    def column_step(number, carry):
        columns = pl.ds(pl.multiple_of(number * 2 * LANES, 2 * LANES), 2 * LANES)
        total[:, columns] = dot_transposed(projected_grad[...], w_qkv[columns, :])
        return carry

    lax.fori_loop(0, model_width // (2 * LANES), column_step, 0)
    write_parts(place, total, [part.at[:span] for part in parts], span)
    for copy in mixture_copies:
        copy.wait()


def attend_grad_kernel(
    place, layer_in, gain, projected_grad, attended, branch_grad, kept, given, normed
):
    token_count, model_width = layer_in.shape
    for row in range(0, token_count, ROWS):
        rows = pl.ds(row, ROWS)
        values = layer_in[rows, :].astype(jnp.float32)
        scale = lax.rsqrt(jnp.mean(values * values, axis=-1, keepdims=True) + epsilon)
        normed[rows, :] = (values * scale * gain[...]).astype(jnp.bfloat16)
    width = projected_grad.shape[1]
    blocks = []
    for row in range(0, model_width, attended.shape[1]):
        lanes = pl.ds(row, attended.shape[1])
        blocks.append((normed, lanes, projected_grad, pl.ds(0, width)))
    for lane in range(0, model_width, width):
        blocks.append((attended, pl.ds(0, attended.shape[1]), branch_grad, pl.ds(lane, width)))
    half = len(blocks) // 2
    for number, (left, left_lanes, right, right_lanes) in enumerate(blocks):
        rows = pl.ds(number % half * attended.shape[1], attended.shape[1])
        grad = transposed_dot(left[:, left_lanes], right[:, right_lanes])
        mine = (place[1] & 1) == number // half

        @pl.when(mine)
        def _():
            kept[rows, :] = grad

        @pl.when(jnp.logical_not(mine))
        def _():
            given[rows, :] = grad.astype(jnp.bfloat16)


def norm_back_kernel(own, near, far, residual, inverse, gain, out_grad, residual_grad, low_grad):
    summed = own[...] + near[...].astype(jnp.float32) + far[...].astype(jnp.float32)
    total = out_grad[...].astype(jnp.float32) + rms_backward(
        residual[...], inverse[...], gain[...], summed
    )
    residual_grad[...] = total
    low_grad[...] = total.astype(jnp.bfloat16)


def finish_kernel(own, near, far, layer_in, gain, residual_grad, residual, block):
    span = layer_in.shape[0]
    summed = own[...] + near[...].astype(jnp.float32) + far[...].astype(jnp.float32)
    values = layer_in[...].astype(jnp.float32)
    inverse = lax.rsqrt(jnp.mean(values * values, axis=-1, keepdims=True) + epsilon)
    block[:span, :] = (residual[...] + summed[span:]).astype(jnp.bfloat16)
    block[span : 2 * span, :] = (
        residual_grad[...] + rms_backward(values, inverse, gain[...], summed[:span])
    ).astype(jnp.bfloat16)


def in_vmem(count):
    return [pl.BlockSpec(memory_space=pltpu.VMEM)] * count


def in_hbm(count):
    return [pl.BlockSpec(memory_space=pltpu.HBM)] * count


def in_smem(count):
    return [pl.BlockSpec(memory_space=pltpu.SMEM)] * count


def shaped(shape, dtype):
    return jax.ShapeDtypeStruct(shape, dtype)


def on_device(
    layer_in,
    seq_lengths,
    routes,
    gain_attn,
    w_qkv,
    w_output,
    gain_ffn,
    w_router,
    w_in,
    w_out,
    out_grad,
):
    low, wide = jnp.bfloat16, jnp.float32
    token_count, model_width = layer_in.shape
    kv_here = w_qkv.shape[1]
    experts_all = w_router.shape[1]
    units = w_out.shape[1]
    head_width = kv_here * LANES
    block_count = token_count // ROWS
    tensor_count = lax.axis_size("tensor")
    span = token_count // tensor_count
    tensor_here = lax.axis_index("tensor")
    place = jnp.stack([tensor_here, lax.axis_index("expert")]).astype(jnp.int32)
    mib = 1 << 20

    def token_block(array_in):
        return lax.dynamic_slice_in_dim(array_in, tensor_here * span, span, 0)

    def in_order(blocks):
        joined = jnp.zeros((token_count,) + blocks[0].shape[1:], blocks[0].dtype)
        for number, block in enumerate(blocks):
            joined = lax.dynamic_update_slice_in_dim(
                joined, block, (tensor_here ^ number) * span, 0
            )
        return joined

    core = lax.axis_index("expert") & 1
    half = w_output.shape[0] // 2
    output_own = jnp.where(core == 0, w_output[:half], w_output[half:])
    output_far = exchange(output_own, "tensor", 2)
    output_near = exchange(output_own, "tensor", 1)
    w_in_own, w_out_own = w_in.reshape(2 * units, model_width), w_out[0]
    w_in_near = exchange(w_in_own, "expert", 2)
    w_out_near = exchange(w_out_own, "expert", 4)

    cosine, sine = angle_tables(token_count)
    qkv_flat = w_qkv.reshape(model_width, -1)
    kept = (
        shaped((kv_here, block_count, 2 * ROWS, LANES), low),
        shaped((kv_here, token_count, LANES), low),
        shaped((kv_here, block_count, 2 * ROWS, token_count), low),
    )
    queries, pairs, probs, attended = pl.pallas_call(
        attend_kernel,
        out_shape=kept + (shaped((token_count, head_width), low),),
        in_specs=in_smem(1) + in_vmem(5),
        out_specs=tuple(in_hbm(3) + in_vmem(1)),
        scratch_shapes=[pltpu.VMEM((token_count, model_width), low)]
        + [pltpu.VMEM(each.shape, low) for each in kept]
        + [pltpu.SemaphoreType.DMA((2 + block_count,))],
        compiler_params=pltpu.CompilerParams(vmem_limit_bytes=56 * mib),
        name="attend",
    )(seq_lengths, layer_in, gain_attn[None], qkv_flat, cosine, sine)

    w_in_near, w_out_near, output_far, output_near, attended = lax.optimization_barrier(
        (w_in_near, w_out_near, output_far, output_near, attended)
    )
    w_in_near = jnp.concatenate([w_in_own, w_in_near])
    w_out_near = jnp.concatenate([w_out_own, w_out_near])
    w_in_far = exchange(w_in_near, "expert", 4)
    w_out_far = exchange(w_out_near, "expert", 2)
    heads_far = exchange(attended, "tensor", 2)
    heads_near = exchange(attended, "tensor", 1)
    output_both = exchange(output_far, "tensor", 1)
    heads_far, heads_near = lax.optimization_barrier((heads_far, heads_near))
    heads_both = exchange(heads_far, "tensor", 1)
    heads_both, output_both, w_in_near, w_in_far, w_out_near, w_out_far = (
        lax.optimization_barrier(
            (heads_both, output_both, w_in_near, w_in_far, w_out_near, w_out_far)
        )
    )
    w_in_all = gather_pairs(w_in_near, w_in_far)
    w_out_all = gather_pairs(w_out_near, w_out_far)
    heads_all = [attended, heads_near, heads_far, heads_both]
    output_mine = jnp.concatenate([output_own, output_near, output_far, output_both])
    output_other = exchange(output_mine, "expert", 1)
    router_rows = jnp.pad(jnp.transpose(w_router), ((0, LANES - experts_all), (0, 0)))
    part_shapes = (shaped((span, model_width), wide),) + (
        shaped((span, model_width), low),
    ) * (tensor_count - 1)
    middle = pl.pallas_call(
        functools.partial(middle_kernel, tensor_count),
        out_shape=part_shapes
        + (
            shaped((span, model_width), wide),
            shaped((span, 1), wide),
            shaped((token_count, model_width), low),
            shaped((token_count, experts_all * units), low),
            shaped((token_count, experts_all * 2 * units), low),
            shaped((1, model_width), wide),
            shaped((experts_all, model_width), wide),
        ),
        in_specs=in_smem(1) + in_vmem(16),
        out_specs=tuple(in_vmem(tensor_count + 7)),
        scratch_shapes=[
            pltpu.VMEM((token_count, model_width), wide),
            pltpu.VMEM((token_count, 1), wide),
            pltpu.VMEM((token_count, LANES), wide),
            pltpu.VMEM((token_count, LANES), wide),
            pltpu.VMEM((token_count, 2 * units), wide),
            pltpu.VMEM((token_count, units), wide),
            pltpu.VMEM((token_count, model_width), wide),
        ],
        compiler_params=pltpu.CompilerParams(vmem_limit_bytes=20 * mib),
        name="middle",
    )(
        place,
        gain_ffn[None],
        router_rows,
        routes,
        layer_in,
        out_grad,
        output_mine,
        output_other,
        jnp.concatenate(heads_all),
        *w_in_all,
        *w_out_all,
    )
    normed_parts, middle = middle[:tensor_count], middle[tensor_count:]
    residual, inverse_two, normed_two, active, pre_grad, gain_ffn_part, router_part = middle

    relayed = exchange(normed_parts[3], "tensor", 1)
    half_grads = shaped((experts_all // 2 * 3 * units, model_width), low)
    late = pl.pallas_call(
        functools.partial(weight_grad_kernel, tensor_count),
        out_shape=part_shapes + (half_grads,) * 2,
        in_specs=in_smem(1) + in_vmem(8),
        out_specs=tuple(in_vmem(tensor_count + 2)),
        scratch_shapes=[pltpu.VMEM((token_count, model_width), wide)],
        compiler_params=pltpu.CompilerParams(vmem_limit_bytes=16 * mib),
        name="weight_grad",
    )(place, normed_two, out_grad, active, pre_grad, *w_out_all)
    late, relayed = lax.optimization_barrier((late, relayed))
    normed_pieces = scatter_parts(normed_parts, relayed)
    mixture_parts, kept_grads, given_grads = late[:tensor_count], late[-2], late[-1]
    given_grads = exchange(given_grads, "expert", 1)

    in_rows, out_rows = experts_all * units // 2, experts_all * units // 4
    in_kept, in_given, out_kept, out_given = pl.pallas_call(
        add_grads_kernel,
        out_shape=(
            shaped((in_rows, model_width), wide),
            shaped((in_rows, model_width), low),
            shaped((out_rows, model_width), wide),
            shaped((out_rows, model_width), low),
        ),
        in_specs=in_vmem(2),
        out_specs=tuple(in_vmem(4)),
        compiler_params=pltpu.CompilerParams(vmem_limit_bytes=16 * mib),
        name="add_grads",
    )(kept_grads, given_grads)
    residual, in_kept, in_given, out_kept, out_given = lax.optimization_barrier(
        (residual, in_kept, in_given, out_kept, out_given)
    )
    residual_grad, low_grad = pl.pallas_call(
        norm_back_kernel,
        out_shape=(shaped((span, model_width), wide), shaped((span, model_width), low)),
        in_specs=in_vmem(7),
        out_specs=tuple(in_vmem(2)),
        compiler_params=pltpu.CompilerParams(vmem_limit_bytes=6 * mib),
        name="norm_back",
    )(
        *normed_pieces,
        residual,
        inverse_two,
        gain_ffn[None],
        token_block(out_grad),
    )
    grad_blocks = gather_blocks(low_grad)

    in_arrived = exchange(in_given, "expert", 4)
    out_arrived = exchange(out_given, "expert", 2)
    in_summed = in_kept + in_arrived.astype(wide)
    out_summed = out_kept + out_arrived.astype(wide)
    in_arrived = exchange(in_summed[in_rows // 2 :].astype(low), "expert", 2)
    out_arrived = exchange(out_summed[out_rows // 2 :].astype(low), "expert", 4)

    fetched = (w_output, queries, pairs, probs, cosine, sine, qkv_flat)
    back = pl.pallas_call(
        functools.partial(attend_back_kernel, tensor_count),
        out_shape=(shaped((2 * span, model_width), wide),)
        + (shaped((2 * span, model_width), low),) * (tensor_count - 1)
        + (
            shaped((token_count, model_width), low),
            shaped((token_count, 2 * head_width), low),
        ),
        in_specs=in_smem(1) + in_hbm(7 + 2 * tensor_count),
        out_specs=tuple(in_vmem(tensor_count + 2)),
        scratch_shapes=[
            pltpu.VMEM((token_count, head_width), wide),
            pltpu.VMEM((token_count, LANES), wide),
            pltpu.VMEM((token_count, model_width), wide),
        ]
        + [pltpu.VMEM(each.shape, each.dtype) for each in fetched]
        + [pltpu.SemaphoreType.DMA((len(fetched) + 2 * tensor_count,))],
        compiler_params=pltpu.CompilerParams(vmem_limit_bytes=58 * mib),
        name="attend_back",
    )(
        place,
        *fetched,
        *grad_blocks,
        *mixture_parts,
    )
    input_parts, (branch_grad, projected_grad) = (
        back[:tensor_count],
        back[tensor_count:],
    )
    relayed = exchange(input_parts[3], "tensor", 1)
    row_count = (model_width + w_output.shape[0] * model_width // (2 * head_width)) // 2
    kept_sums, given_sums = pl.pallas_call(
        attend_grad_kernel,
        out_shape=(
            shaped((row_count, 2 * head_width), wide),
            shaped((row_count, 2 * head_width), low),
        ),
        in_specs=in_smem(1) + in_vmem(5),
        out_specs=tuple(in_vmem(2)),
        scratch_shapes=[pltpu.VMEM((token_count, model_width), low)],
        compiler_params=pltpu.CompilerParams(vmem_limit_bytes=12 * mib),
        name="attend_grad",
    )(place, layer_in, gain_attn[None], projected_grad, attended, branch_grad)
    relayed, kept_sums, given_sums, in_summed, out_summed = lax.optimization_barrier(
        (relayed, kept_sums, given_sums, in_summed, out_summed)
    )
    sums_half = kept_sums + exchange(given_sums, "expert", 1).astype(wide)
    sums = exchange_halves(sums_half.astype(low), (2, 4))
    input_pieces = scatter_parts(input_parts, relayed)
    residual, in_arrived, out_arrived, sums = lax.optimization_barrier(
        (residual, in_arrived, out_arrived, sums)
    )
    w_in_grad = (in_summed[: in_rows // 2] + in_arrived.astype(wide)).reshape(w_in.shape)
    w_out_grad = (out_summed[: out_rows // 2] + out_arrived.astype(wide)).reshape(w_out.shape)
    block = pl.pallas_call(
        finish_kernel,
        out_shape=shaped((2 * span, model_width), low),
        in_specs=in_vmem(7),
        out_specs=in_vmem(1)[0],
        compiler_params=pltpu.CompilerParams(vmem_limit_bytes=6 * mib),
        name="finish",
    )(
        *input_pieces,
        token_block(layer_in),
        gain_attn[None],
        residual_grad,
        residual,
    )
    far = exchange(block, "tensor", 2)
    near = exchange(block, "tensor", 1)
    small = jnp.concatenate([router_part, gain_ffn_part])
    sums, small, _ = lax.optimization_barrier((sums, small, block))
    small = sum_over_experts(small)
    summed = join_cores(exchange_halves(sums, (4, 2)))
    qkv_summed = summed[:model_width].reshape(w_qkv.shape)
    output_summed = jnp.concatenate(split_blocks(summed[model_width:], 0, 2), 1)

    gain_part = jnp.sum(
        qkv_flat.astype(wide) * summed[:model_width], 1
    ) / gain_attn
    small = jnp.concatenate([small, gain_part[None]])
    far, near, small, summed = lax.optimization_barrier((far, near, small, summed))
    for bit in (1, 2):
        small = small + exchange(small, "tensor", bit)
    blocks = [block, near, far, exchange(far, "tensor", 1)]
    layer_here = in_order([block[:span] for block in blocks])
    in_here = in_order([block[span:] for block in blocks])
    return (
        layer_here,
        in_here,
        small[experts_all + 1],
        qkv_summed,
        output_summed,
        small[experts_all],
        jnp.transpose(small[:experts_all]),
        w_in_grad,
        w_out_grad,
    )


def solution(mesh):
    fits = mesh.shape["tensor"] == 4 and mesh.shape["expert"] == 8
    placed = (
        P("expert", None),
        P("expert", None),
        P("expert", None),
        P(),
        P(None, "tensor", None),
        P("tensor", None),
        P(),
        P(),
        P("expert", None, "tensor", None),
        P("expert", "tensor", None),
        P("expert", None),
    )
    return jax.shard_map(
        on_device if fits else on_device_general,
        mesh=mesh,
        in_specs=placed,
        out_specs=(
            P("expert", None),
            P("expert", None),
            P(),
            P(None, "tensor", None),
            P("tensor", None),
            P(),
            P(),
            P("expert", None, "tensor", None),
            P("expert", "tensor", None),
        ),
        check_vma=False,
    )
```

```python
import functools
import math

import jax
import jax.numpy as jnp
import numpy as np
from jax import lax
from jax.experimental import pallas as pl
from jax.experimental.pallas import tpu as pltpu
from jax.sharding import PartitionSpec as P

HEADS = 16
KV_HEADS = 8
HEAD_DIM = 64


epsilon = 1e-06
rope_base = 10000.0
masked_out = -1e30


def rms_forward(values, gain_vec):
    inverse = lax.rsqrt(jnp.mean(values * values, axis=-1, keepdims=True) + epsilon)
    return (values * inverse * gain_vec, inverse)


def rms_backward(values, inverse, gain_vec, upstream):
    normal = values * inverse
    scaled = upstream * gain_vec
    inner_mean = jnp.mean(scaled * normal, axis=-1, keepdims=True)
    return inverse * (scaled - normal * inner_mean)


def positions(lengths, token_count):
    seq_ends = jnp.cumsum(lengths, dtype=jnp.int32)
    row_index = jnp.arange(token_count, dtype=jnp.int32)
    segment = jnp.sum(
        (row_index[:, None] >= seq_ends[None, :]).astype(jnp.int32), axis=1, dtype=jnp.int32
    )
    seq_ids = jnp.arange(lengths.shape[0], dtype=jnp.int32)
    seq_start = jnp.sum(
        jnp.where(segment[:, None] == seq_ids[None, :], (seq_ends - lengths)[None, :], 0),
        axis=1,
        dtype=jnp.int32,
    )
    return (segment, row_index - seq_start)


def rope_tables(position, head_dim):
    half_dim = head_dim // 2
    inverse_freq = jnp.exp(
        jnp.arange(half_dim, dtype=jnp.float32) * (-2.0 * math.log(rope_base) / head_dim)
    )
    angles = position.astype(jnp.float32)[:, None] * inverse_freq[None, :]
    cosine = jnp.cos(angles)
    sine_tab = jnp.sin(angles)
    return (jnp.concatenate([cosine, cosine], 1), jnp.concatenate([sine_tab, sine_tab], 1))


def rotate(values, cosine, sine_tab):
    half_dim = values.shape[-1] // 2
    turned = jnp.concatenate([-values[..., half_dim:], values[..., :half_dim]], -1)
    return values * cosine + turned * sine_tab


def split_blocks(array_in, axis_at, block_count):
    dims_now = array_in.shape
    regrouped = array_in.reshape(
        dims_now[:axis_at]
        + (block_count, dims_now[axis_at] // block_count)
        + dims_now[axis_at + 1 :]
    )
    return jnp.moveaxis(regrouped, axis_at, 0)


def join_blocks(array_in, axis_at):
    regrouped = jnp.moveaxis(array_in, 0, axis_at)
    dims_now = regrouped.shape
    return regrouped.reshape(
        dims_now[:axis_at] + (dims_now[axis_at] * dims_now[axis_at + 1],) + dims_now[axis_at + 2 :]
    )


def block_scores(query_block, key_rows, segment_rows, row_start, segment, scaling):
    block_rows = query_block.shape[2]
    scores_raw = (
        jnp.einsum("kgbd,ksd->kgbs", query_block, key_rows, preferred_element_type=jnp.float32)
        * scaling
    )
    query_index = row_start + jnp.arange(block_rows, dtype=jnp.int32)
    key_index = jnp.arange(key_rows.shape[1], dtype=jnp.int32)
    allowed = (segment_rows[:, None] == segment[None, :]) & (
        key_index[None, :] <= query_index[:, None]
    )
    return jnp.where(allowed[None, None], scores_raw, masked_out)


def attention_forward(queries, key_rows, values, segment, scaling, block_size):
    block_count = queries.shape[2] // block_size
    starts_all = jnp.arange(block_count, dtype=jnp.int32) * block_size

    def one_block(packed):
        query_block, segment_rows, row_start = packed
        scores = block_scores(query_block, key_rows, segment_rows, row_start, segment, scaling)
        top_score = jnp.max(scores, -1)
        exponent = jnp.exp(scores - top_score[..., None])
        row_total = jnp.sum(exponent, -1)
        probs = (exponent / row_total[..., None]).astype(jnp.bfloat16)
        output = jnp.einsum("kgbs,ksd->kgbd", probs, values, preferred_element_type=jnp.float32)
        return (output.astype(jnp.bfloat16), top_score, row_total)

    outputs, top_blocks, total_blocks = lax.map(
        one_block,
        (
            split_blocks(queries, 2, block_count),
            segment.reshape(block_count, block_size),
            starts_all,
        ),
    )
    return (join_blocks(outputs, 2), join_blocks(top_blocks, 2), join_blocks(total_blocks, 2))


def attention_backward(
    queries, key_rows, values, heads_grad, segment, top_kept, total_kept, scaling, block_size
):
    block_count = queries.shape[2] // block_size
    starts_all = jnp.arange(block_count, dtype=jnp.int32) * block_size

    def one_block(running, packed):
        key_acc, value_acc = running
        query_block, grad_block, segment_rows, row_start, top_block, total_block = packed
        scores = block_scores(query_block, key_rows, segment_rows, row_start, segment, scaling)
        probs = jnp.exp(scores - top_block[..., None]) / total_block[..., None]
        probs_low = probs.astype(jnp.bfloat16)
        value_acc = value_acc + jnp.einsum(
            "kgbs,kgbd->ksd", probs_low, grad_block, preferred_element_type=jnp.float32
        )
        prob_grad = jnp.einsum(
            "kgbd,ksd->kgbs", grad_block, values, preferred_element_type=jnp.float32
        )
        inner_sum = jnp.sum(probs * prob_grad, -1, keepdims=True)
        score_grad = (probs * (prob_grad - inner_sum)).astype(jnp.bfloat16)
        query_grad = (
            jnp.einsum("kgbs,ksd->kgbd", score_grad, key_rows, preferred_element_type=jnp.float32)
            * scaling
        )
        key_acc = (
            key_acc
            + jnp.einsum(
                "kgbs,kgbd->ksd", score_grad, query_block, preferred_element_type=jnp.float32
            )
            * scaling
        )
        return ((key_acc, value_acc), query_grad)

    empty = jnp.zeros(key_rows.shape, jnp.float32)
    packed_all = (
        split_blocks(queries, 2, block_count),
        split_blocks(heads_grad, 2, block_count),
        segment.reshape(block_count, block_size),
        starts_all,
        split_blocks(top_kept, 2, block_count),
        split_blocks(total_kept, 2, block_count),
    )
    (key_grad, value_grad), query_blocks = lax.scan(one_block, (empty, empty), packed_all)
    return (join_blocks(query_blocks, 2), key_grad, value_grad)


def on_device_general(
    layer_in,
    seq_lengths,
    routes,
    gain_attn,
    w_qkv,
    w_output,
    gain_ffn,
    w_router,
    w_in,
    w_out,
    out_grad,
):
    token_count, model_width = layer_in.shape
    kv_here = w_qkv.shape[1]
    group_size = HEADS // KV_HEADS
    scaling = 1.0 / math.sqrt(HEAD_DIM)
    block_size = min(512, token_count)
    w_output_all = lax.all_gather(w_output, "tensor", axis=0, tiled=True)
    w_gate_all = lax.all_gather(w_in[0, 0], "expert", axis=0, tiled=True)
    w_up_all = lax.all_gather(w_in[0, 1], "expert", axis=0, tiled=True)
    w_out_all = lax.all_gather(w_out[0], "expert", axis=0, tiled=True)
    segment, position = positions(seq_lengths[0], token_count)
    cosine, sine_tab = rope_tables(position, HEAD_DIM)
    inputs = layer_in.astype(jnp.float32)
    normed_one, inverse_one = rms_forward(inputs, gain_attn)
    normed_one_low = normed_one.astype(jnp.bfloat16)
    qkv_flat = w_qkv.reshape(model_width, -1)
    projected = jnp.dot(normed_one_low, qkv_flat, preferred_element_type=jnp.float32)
    projected = projected.reshape(token_count, kv_here, group_size + 2, HEAD_DIM)
    queries = rotate(
        jnp.transpose(projected[:, :, :group_size], (1, 2, 0, 3)), cosine, sine_tab
    ).astype(jnp.bfloat16)
    key_rows = rotate(
        jnp.transpose(projected[:, :, group_size], (1, 0, 2)), cosine, sine_tab
    ).astype(jnp.bfloat16)
    values = jnp.transpose(projected[:, :, group_size + 1], (1, 0, 2)).astype(jnp.bfloat16)
    attended, top_kept, total_kept = attention_forward(
        queries, key_rows, values, segment, scaling, block_size
    )
    heads_out = jnp.transpose(attended, (2, 0, 1, 3)).reshape(token_count, -1)
    heads_all = lax.all_gather(heads_out, "tensor", axis=1, tiled=True)
    branch_here = jnp.dot(heads_all, w_output_all, preferred_element_type=jnp.float32)
    residual = inputs + branch_here
    normed_two, inverse_two = rms_forward(residual, gain_ffn)
    normed_low = normed_two.astype(jnp.bfloat16)
    experts_all = w_router.shape[1]
    unit_count = w_out.shape[1]
    logits = jnp.dot(normed_low, w_router, preferred_element_type=jnp.float32)
    expert_ids = jnp.arange(experts_all, dtype=jnp.int32)
    picked = jnp.any(routes[:, :, None] == expert_ids[None, None, :], axis=1)
    picked_logits = jnp.where(picked, logits, masked_out)
    top_logit = jnp.max(picked_logits, -1, keepdims=True)
    weight = jnp.where(picked, jnp.exp(picked_logits - top_logit), 0.0)
    gates = weight / jnp.sum(weight, -1, keepdims=True)

    def by_unit(per_expert):
        return jnp.broadcast_to(
            per_expert[:, :, None], (token_count, experts_all, unit_count)
        ).reshape(token_count, -1)

    def over_units(per_unit):
        return jnp.sum(per_unit.reshape(token_count, experts_all, unit_count), -1)

    def times_transposed(left, right):
        return lax.dot_general(
            left, right, (((1,), (1,)), ((), ())), preferred_element_type=jnp.float32
        )

    def transposed_times(left, right):
        return lax.dot_general(
            left, right, (((0,), (0,)), ((), ())), preferred_element_type=jnp.float32
        )

    gates_wide = by_unit(gates)
    gate_vals = times_transposed(normed_low, w_gate_all)
    up_vals = times_transposed(normed_low, w_up_all)
    plain_grad = times_transposed(out_grad, w_out_all)
    sig_vals = jax.nn.sigmoid(gate_vals)
    silu_vals = gate_vals * sig_vals
    active = silu_vals * up_vals
    scaled_active = (active * gates_wide).astype(jnp.bfloat16)
    active_grad = plain_grad * gates_wide
    gate_pre = (
        active_grad * up_vals * (sig_vals * (1.0 + gate_vals * (1.0 - sig_vals)))
    ).astype(jnp.bfloat16)
    up_pre = (active_grad * silu_vals).astype(jnp.bfloat16)
    gate_grad_part = over_units(active * plain_grad)
    logit_part = (
        gates * (gate_grad_part - jnp.sum(gates * gate_grad_part, -1, keepdims=True))
    ).astype(jnp.bfloat16)
    normed_two_part = (
        jnp.dot(gate_pre, w_gate_all, preferred_element_type=jnp.float32)
        + jnp.dot(up_pre, w_up_all, preferred_element_type=jnp.float32)
        + times_transposed(logit_part, w_router)
    )
    normed_two_grad = lax.psum(normed_two_part.astype(jnp.bfloat16), "tensor").astype(jnp.float32)
    mixture_part = jnp.dot(scaled_active, w_out_all, preferred_element_type=jnp.float32)
    mixture = lax.psum(mixture_part.astype(jnp.bfloat16), "tensor").astype(jnp.float32)
    layer_here = (residual + mixture).astype(jnp.bfloat16)

    def to_owner(partial):
        return lax.psum_scatter(
            partial.astype(jnp.bfloat16), "expert", scatter_dimension=0, tiled=True
        ).astype(jnp.float32)

    w_gate_grad = to_owner(transposed_times(gate_pre, normed_low))
    w_up_grad = to_owner(transposed_times(up_pre, normed_low))
    w_in_grad = jnp.stack([w_gate_grad, w_up_grad])[None]
    w_out_grad = to_owner(transposed_times(scaled_active, out_grad))[None]
    router_part = transposed_times(logit_part, normed_low)
    normal_two = residual * inverse_two
    gain_ffn_part = jnp.sum(normed_two_part * normal_two, axis=0)
    upstream = out_grad.astype(jnp.float32)
    residual_part = rms_backward(residual, inverse_two, gain_ffn, normed_two_grad)
    residual_grad = upstream + residual_part
    branch_here_grad = residual_grad.astype(jnp.bfloat16)
    w_output_grad = lax.dot_general(
        heads_out, branch_here_grad, (((0,), (0,)), ((), ())), preferred_element_type=jnp.float32
    )
    heads_flat = lax.dot_general(
        branch_here_grad, w_output, (((1,), (1,)), ((), ())), preferred_element_type=jnp.float32
    ).astype(jnp.bfloat16)
    heads_grad = jnp.transpose(
        heads_flat.reshape(token_count, kv_here, group_size, HEAD_DIM), (1, 2, 0, 3)
    )
    query_grad, key_grad, value_grad = attention_backward(
        queries, key_rows, values, heads_grad, segment, top_kept, total_kept, scaling, block_size
    )
    query_grad = rotate(query_grad, cosine, -sine_tab)
    key_grad = rotate(key_grad, cosine, -sine_tab)
    projected_grad = jnp.concatenate(
        [
            jnp.transpose(query_grad, (2, 0, 1, 3)),
            jnp.transpose(key_grad, (1, 0, 2))[:, :, None],
            jnp.transpose(value_grad, (1, 0, 2))[:, :, None],
        ],
        2,
    )
    projected_grad = projected_grad.reshape(token_count, -1).astype(jnp.bfloat16)
    w_qkv_grad = lax.dot_general(
        normed_one_low, projected_grad, (((0,), (0,)), ((), ())), preferred_element_type=jnp.float32
    ).reshape(w_qkv.shape)
    normed_one_part = lax.dot_general(
        projected_grad, qkv_flat, (((1,), (1,)), ((), ())), preferred_element_type=jnp.float32
    )
    gain_attn_part = jnp.sum(normed_one_part * (inputs * inverse_one), axis=0)
    normed_one_grad = lax.psum(normed_one_part.astype(jnp.bfloat16), "tensor").astype(jnp.float32)
    input_part = rms_backward(inputs, inverse_one, gain_attn, normed_one_grad)
    in_here = (residual_grad + input_part).astype(jnp.bfloat16)
    qkv_summed = lax.psum(w_qkv_grad.astype(jnp.bfloat16), "expert").astype(jnp.float32)
    output_summed = lax.psum(w_output_grad.astype(jnp.bfloat16), "expert").astype(jnp.float32)
    small = jnp.concatenate([router_part, gain_ffn_part[None], gain_attn_part[None]])
    small = lax.psum(small, ("expert", "tensor"))
    return (
        layer_here,
        in_here,
        small[experts_all + 1],
        qkv_summed,
        output_summed,
        small[experts_all],
        jnp.transpose(small[:experts_all]),
        w_in_grad,
        w_out_grad,
    )


LANES = 128
ROWS = 128
IN_ORDER = (0, 2, 4, 6, 1, 3, 5, 7)
OUT_ORDER = (0, 4, 2, 6, 1, 5, 3, 7)


def exchange(array_in, axis_name, bits):
    count = lax.axis_size(axis_name)
    return lax.ppermute(array_in, axis_name, [(i, i ^ bits) for i in range(count)])


def gather_blocks(own):
    far = exchange(own, "tensor", 2)
    near = exchange(own, "tensor", 1)
    far, near = lax.optimization_barrier((far, near))
    return [own, near, far, exchange(far, "tensor", 1)]


def scatter_parts(parts, relayed):
    near, far, relayed = lax.optimization_barrier((parts[1], parts[2], relayed))
    far = (far.astype(jnp.float32) + relayed.astype(jnp.float32)).astype(jnp.bfloat16)
    far = exchange(far, "tensor", 2)
    return parts[0], exchange(near, "tensor", 1), far


def gather_pairs(near, far):
    return [near, far, exchange(near, "expert", 1), exchange(far, "expert", 1)]


def exchange_halves(array_in, bits):
    rows = array_in.shape[0] // 2
    halves = []
    for half, bit in zip((array_in[:rows], array_in[rows:]), bits):
        arrived = exchange(half, "expert", bit)
        halves.append((half.astype(jnp.float32) + arrived.astype(jnp.float32)).astype(jnp.bfloat16))
    return jnp.concatenate(halves)


def join_cores(half):
    core = lax.axis_index("expert") & 1
    other = exchange(half, "expert", 1)
    return jnp.concatenate(
        [jnp.where(core == 0, half, other), jnp.where(core == 0, other, half)]
    ).astype(jnp.float32)


def sum_over_experts(array_in):
    for bit in (1, 2, 4):
        array_in = array_in + exchange(array_in, "expert", bit)
    return array_in


def dot_plain(left, right):
    return jnp.dot(left, right, preferred_element_type=jnp.float32)


def dot_transposed(left, right):
    return lax.dot_general(
        left, right, (((1,), (1,)), ((), ())), preferred_element_type=jnp.float32
    )


def transposed_dot(left, right):
    return lax.dot_general(
        left, right, (((0,), (0,)), ((), ())), preferred_element_type=jnp.float32
    )


def lane_index(shape):
    return lax.broadcasted_iota(jnp.int32, shape, 1)


def turn(values):
    low_half = (lane_index(values.shape) & (HEAD_DIM - 1)) < HEAD_DIM // 2
    return jnp.where(
        low_half,
        -pltpu.roll(values, LANES - HEAD_DIM // 2, 1),
        pltpu.roll(values, HEAD_DIM // 2, 1),
    )


def swap_heads(values):
    return pltpu.roll(values, HEAD_DIM, 1)


def first_head(shape):
    return lane_index(shape) < HEAD_DIM


def angle_tables(token_count):
    half_dim = HEAD_DIM // 2
    inverse_freq = np.exp(np.arange(half_dim) * (-2.0 * math.log(rope_base) / HEAD_DIM))
    angles = np.arange(token_count)[:, None] * inverse_freq[None, :]
    tile = LANES // half_dim
    return (
        np.tile(np.cos(angles), (1, tile)).astype(np.float32),
        np.tile(np.sin(angles), (1, tile)).astype(np.float32),
    )


def attend_kernel(
    lengths,
    layer_in,
    gain,
    w_qkv,
    cosine,
    sine,
    queries_out,
    pairs_out,
    probs_out,
    attended,
    normed,
    queries,
    pairs,
    probs,
    sems,
):
    token_count = layer_in.shape[0]
    kv_here = pairs.shape[0]
    for row in range(0, token_count, ROWS):
        rows = pl.ds(row, ROWS)
        values = layer_in[rows, :].astype(jnp.float32)
        scale = lax.rsqrt(jnp.mean(values * values, axis=-1, keepdims=True) + epsilon)
        normed[rows, :] = (values * scale * gain[...]).astype(jnp.bfloat16)
    is_first = first_head((ROWS, LANES))
    for kv in range(kv_here):
        projected = dot_plain(normed[...], w_qkv[:, 2 * LANES * kv : 2 * LANES * (kv + 1)])
        for block in range(token_count // ROWS):
            rows = pl.ds(block * ROWS, ROWS)
            cos_rows, sin_rows = cosine[rows, :], sine[rows, :]
            query = projected[block * ROWS : (block + 1) * ROWS, :LANES]
            query = (query * cos_rows + turn(query) * sin_rows) * (1.0 / math.sqrt(HEAD_DIM))
            queries[kv, block, :ROWS, :] = jnp.where(is_first, query, 0.0).astype(jnp.bfloat16)
            queries[kv, block, ROWS:, :] = jnp.where(is_first, swap_heads(query), 0.0).astype(
                jnp.bfloat16
            )
            pair = projected[block * ROWS : (block + 1) * ROWS, LANES:]
            pairs[kv, rows, :] = jnp.where(
                is_first, pair * cos_rows + turn(pair) * sin_rows, pair
            ).astype(jnp.bfloat16)
    copies = [
        pltpu.make_async_copy(queries, queries_out, sems.at[0]),
        pltpu.make_async_copy(pairs, pairs_out, sems.at[1]),
    ]
    for copy in copies:
        copy.start()
    for block in range(token_count // ROWS):
        keys = (block + 1) * ROWS
        token = block * ROWS + (
            lax.broadcasted_iota(jnp.int32, (2 * ROWS, keys), 0) & (ROWS - 1)
        )
        start = jnp.zeros_like(token)
        end = 0
        for seq in range(lengths.shape[1] - 1):
            end = end + lengths[0, seq]
            start = jnp.where(token >= end, end, start)
        key = lane_index((2 * ROWS, keys))
        allowed = (key <= token) & (key >= start)
        for kv in range(kv_here):
            scores = dot_transposed(queries[kv, block], pairs[kv, :keys, :])
            scores = jnp.where(allowed, scores, masked_out)
            exponent = jnp.exp(scores - jnp.max(scores, -1, keepdims=True))
            share = (exponent * (1.0 / jnp.sum(exponent, -1, keepdims=True))).astype(jnp.bfloat16)
            probs[kv, block, :, :keys] = share
            output = dot_plain(share, pairs[kv, :keys, :])
            attended[pl.ds(block * ROWS, ROWS), kv * LANES : (kv + 1) * LANES] = jnp.where(
                is_first, swap_heads(output[:ROWS]), output[ROWS:]
            ).astype(jnp.bfloat16)
        copies.append(
            pltpu.make_async_copy(
                probs.at[:, block, :, :keys], probs_out.at[:, block, :, :keys], sems.at[2 + block]
            )
        )
        copies[-1].start()
    for copy in copies:
        copy.wait()


def write_parts(place, total, parts, span):
    for number, part in enumerate(parts):
        row = pl.multiple_of((place[0] ^ number) * span, span)
        part[...] = total[pl.ds(row, span), :].astype(part.dtype)


def middle_kernel(tensor_count, *refs):
    place, gain, router, routes, layer_in, out_grad = refs[:6]
    w_mine, w_other, heads, refs = refs[6], refs[7], refs[8], refs[9:]
    w_ins, w_outs, refs = refs[:4], refs[4:8], refs[8:]
    parts, refs = refs[:tensor_count], refs[tensor_count:]
    (residual_block, inverse_block, normed, active_out, pre_out, gain_part, router_part) = refs[:7]
    (residual, inverse, gates, gate_grad, hidden, plain, total) = refs[7:]
    token_count, model_width = layer_in.shape
    experts_all = router_part.shape[0]
    units = w_outs[0].shape[0] // 2
    span = token_count // tensor_count
    lane = lane_index((ROWS, LANES))
    half = w_mine.shape[0] // tensor_count
    core = place[1] & 1
    mine_lanes = pl.ds(pl.multiple_of(core * half, half), half)
    other_lanes = pl.ds(pl.multiple_of((1 - core) * half, half), half)

    def branch_step(number, carry):
        columns = pl.ds(pl.multiple_of(number * 2 * LANES, 2 * LANES), 2 * LANES)
        summed = layer_in[:, columns].astype(jnp.float32)
        for number in range(tensor_count):
            head_rows = pl.ds(number * token_count, token_count)
            half_rows = pl.ds(number * half, half)
            summed = summed + dot_plain(heads[head_rows, mine_lanes], w_mine[half_rows, columns])
            summed = summed + dot_plain(heads[head_rows, other_lanes], w_other[half_rows, columns])
        residual[:, columns] = summed
        return carry

    lax.fori_loop(0, model_width // (2 * LANES), branch_step, 0)
    for row in range(0, token_count, ROWS):
        rows = pl.ds(row, ROWS)
        values = residual[rows, :]
        scale = lax.rsqrt(jnp.mean(values * values, axis=-1, keepdims=True) + epsilon)
        inverse[rows, :] = scale
        normed[rows, :] = (values * scale * gain[...]).astype(jnp.bfloat16)
    gates[...] = dot_transposed(normed[...], router[...])
    for row in range(0, token_count, ROWS):
        rows = pl.ds(row, ROWS)
        picked = routes[rows, 0:1] == lane
        for top in range(1, routes.shape[1]):
            picked = picked | (routes[rows, top : top + 1] == lane)
        logits = jnp.where(picked, gates[rows, :], masked_out)
        weight = jnp.where(picked, jnp.exp(logits - jnp.max(logits, -1, keepdims=True)), 0.0)
        gates[rows, :] = weight / jnp.sum(weight, -1, keepdims=True)
    gate_grad[...] = jnp.zeros_like(gate_grad)
    for number in range(experts_all):
        name = place[1] ^ IN_ORDER[number]
        in_rows = pl.ds(number % 2 * 2 * units, 2 * units)
        out_number = OUT_ORDER.index(IN_ORDER[number])
        out_rows = pl.ds(out_number % 2 * units, units)
        hidden[...] = dot_transposed(normed[...], w_ins[number // 2][in_rows, :])
        plain[...] = dot_transposed(out_grad[...], w_outs[out_number // 2][out_rows, :])
        for row in range(0, token_count, ROWS):
            rows = pl.ds(row, ROWS)
            gate = jnp.sum(jnp.where(lane == name, gates[rows, :], 0.0), -1, keepdims=True)
            gate_vals, up_vals = hidden[rows, :units], hidden[rows, units:]
            sig_vals = 0.5 + 0.5 * jnp.tanh(0.5 * gate_vals)
            silu_vals = gate_vals * sig_vals
            active = silu_vals * up_vals
            grad = plain[rows, :]
            gate_grad[rows, :] = gate_grad[rows, :] + jnp.where(
                lane == name, jnp.sum(active * grad, -1, keepdims=True), 0.0
            )
            active_grad = grad * gate
            active_out[rows, out_number * units : (out_number + 1) * units] = (
                active * gate
            ).astype(jnp.bfloat16)
            pre_out[rows, 2 * number * units : (2 * number + 1) * units] = (
                active_grad * up_vals * (sig_vals * (1.0 + gate_vals * (1.0 - sig_vals)))
            ).astype(jnp.bfloat16)
            pre_out[rows, (2 * number + 1) * units : (2 * number + 2) * units] = (
                active_grad * silu_vals
            ).astype(jnp.bfloat16)
    gate_all, grad_all = gates[...], gate_grad[...]
    logit_part = (
        gate_all * (grad_all - jnp.sum(gate_all * grad_all, -1, keepdims=True))
    ).astype(jnp.bfloat16)
    router_part[...] = transposed_dot(logit_part, normed[...])[:experts_all]

    def column_step(number, carry):
        columns = pl.ds(pl.multiple_of(number * 2 * LANES, 2 * LANES), 2 * LANES)
        summed = dot_plain(logit_part, router[:, columns])
        for pair, weights in enumerate(w_ins):
            pre = pre_out[:, 4 * pair * units : 4 * (pair + 1) * units]
            summed = summed + dot_plain(pre, weights[:, columns])
        total[:, columns] = summed
        return carry

    lax.fori_loop(0, model_width // (2 * LANES), column_step, 0)
    write_parts(place, total, parts, span)
    row = pl.ds(pl.multiple_of(place[0] * span, span), span)
    residual_block[...] = residual[row, :]
    inverse_block[...] = inverse[row, :]
    gain_sum = jnp.zeros((1, model_width), jnp.float32)
    for row in range(0, token_count, ROWS):
        rows = pl.ds(row, ROWS)
        gain_sum = gain_sum + jnp.sum(
            total[rows, :] * (residual[rows, :] * inverse[rows, :]), 0, keepdims=True
        )
    gain_part[...] = gain_sum


def weight_grad_kernel(tensor_count, *refs):
    place, normed, out_grad, active, pre_grad = refs[:5]
    w_outs, parts = refs[5:9], refs[9 : 9 + tensor_count]
    kept, given, total = refs[9 + tensor_count :]
    token_count, model_width = normed.shape
    units = w_outs[0].shape[0] // 2
    experts_all = 2 * kept.shape[0] // (3 * units)

    def column_step(number, carry):
        columns = pl.ds(pl.multiple_of(number * 2 * LANES, 2 * LANES), 2 * LANES)
        summed = jnp.zeros((token_count, 2 * LANES), jnp.float32)
        for pair, weights in enumerate(w_outs):
            summed = summed + dot_plain(
                active[:, 2 * pair * units : 2 * (pair + 1) * units], weights[:, columns]
            )
        total[:, columns] = summed
        return carry

    lax.fori_loop(0, model_width // (2 * LANES), column_step, 0)
    write_parts(place, total, parts, token_count // tensor_count)
    for number in range(experts_all):
        out_number = OUT_ORDER.index(IN_ORDER[number])
        grads = kept if number < experts_all // 2 else given
        in_row = number % (experts_all // 2) * 2 * units
        out_row = experts_all * units + out_number % (experts_all // 2) * units
        grads[pl.ds(in_row, 2 * units), :] = transposed_dot(
            pre_grad[:, 2 * number * units : 2 * (number + 1) * units], normed[...]
        ).astype(jnp.bfloat16)
        grads[pl.ds(out_row, units), :] = transposed_dot(
            active[:, out_number * units : (out_number + 1) * units], out_grad[...]
        ).astype(jnp.bfloat16)


def add_grads_kernel(kept, given, in_kept, in_given, out_kept, out_given):
    row = 0
    for target in (in_kept, in_given, out_kept, out_given):
        rows = pl.ds(row, target.shape[0])
        summed = kept[rows, :].astype(jnp.float32) + given[rows, :].astype(jnp.float32)
        target[...] = summed.astype(target.dtype)
        row += target.shape[0]


def attend_back_kernel(tensor_count, *refs):
    place, far_refs, refs = refs[0], refs[1:8], refs[8:]
    blocks, refs = refs[:tensor_count], refs[tensor_count:]
    mixtures, refs = refs[: tensor_count - 1], refs[tensor_count - 1 :]
    parts, refs = refs[:tensor_count], refs[tensor_count:]
    branch_grad, projected_grad, heads_grad, pair_grad, total = refs[:5]
    near_refs, sems = refs[5:12], refs[12]
    w_output, queries, pairs, probs, cosine, sine, w_qkv = near_refs
    copies = [
        pltpu.make_async_copy(source, target, sems.at[number])
        for number, (source, target) in enumerate(zip(far_refs, near_refs))
    ]
    token_count, model_width = branch_grad.shape
    span = token_count // tensor_count
    mixture_copies = [
        pltpu.make_async_copy(mixture, part.at[pl.ds(span, span)], sems.at[len(copies) + number])
        for number, (mixture, part) in enumerate(zip(mixtures, parts[:-1]))
    ]
    block_copies = []
    for number, block in enumerate(blocks):
        row = pl.multiple_of((place[0] ^ number) * span, span)
        block_copies.append(
            pltpu.make_async_copy(
                block,
                branch_grad.at[pl.ds(row, span)],
                sems.at[len(copies) + tensor_count + number],
            )
        )
    for copy in block_copies + copies + mixture_copies:
        copy.start()
    for copy in copies[:1] + block_copies:
        copy.wait()
    heads_grad[...] = dot_transposed(branch_grad[...], w_output[...])
    for copy in copies[1:6]:
        copy.wait()
    is_first = first_head((ROWS, LANES))
    for kv in range(pairs.shape[0]):
        pair_grad[...] = jnp.zeros_like(pair_grad)
        for block in range(token_count // ROWS):
            keys = (block + 1) * ROWS
            rows = pl.ds(block * ROWS, ROWS)
            upper = heads_grad[rows, kv * LANES : (kv + 1) * LANES]
            upper = jnp.concatenate(
                [
                    jnp.where(is_first, 0.0, swap_heads(upper)),
                    jnp.where(is_first, 0.0, upper),
                ]
            ).astype(jnp.bfloat16)
            share_low = probs[kv, block, :, :keys]
            share = share_low.astype(jnp.float32)
            prob_grad = dot_transposed(upper, pairs[kv, :keys, :])
            inner = jnp.sum(share * prob_grad, -1, keepdims=True)
            score_grad = (share * (prob_grad - inner)).astype(jnp.bfloat16)
            query_grad = dot_plain(score_grad, pairs[kv, :keys, :])
            query_grad = jnp.where(
                is_first, query_grad[:ROWS], swap_heads(query_grad[ROWS:])
            ) * (1.0 / math.sqrt(HEAD_DIM))
            projected_grad[rows, 2 * kv * LANES : (2 * kv + 1) * LANES] = (
                query_grad * cosine[rows, :] - turn(query_grad) * sine[rows, :]
            ).astype(jnp.bfloat16)
            pair_grad[:keys, :] = (
                pair_grad[:keys, :]
                + transposed_dot(score_grad, queries[kv, block])
                + transposed_dot(share_low, upper)
            )
        for block in range(token_count // ROWS):
            rows = pl.ds(block * ROWS, ROWS)
            grad = pair_grad[rows, :]
            projected_grad[rows, (2 * kv + 1) * LANES : (2 * kv + 2) * LANES] = jnp.where(
                is_first, grad * cosine[rows, :] - turn(grad) * sine[rows, :], grad
            ).astype(jnp.bfloat16)

    for copy in copies[6:]:
        copy.wait()

    def column_step(number, carry):
        columns = pl.ds(pl.multiple_of(number * 2 * LANES, 2 * LANES), 2 * LANES)
        total[:, columns] = dot_transposed(projected_grad[...], w_qkv[columns, :])
        return carry

    lax.fori_loop(0, model_width // (2 * LANES), column_step, 0)
    write_parts(place, total, [part.at[:span] for part in parts[:-1]] + [parts[-1]], span)
    for copy in mixture_copies:
        copy.wait()


def attend_grad_kernel(
    place, layer_in, gain, projected_grad, attended, branch_grad, kept, given, normed
):
    token_count, model_width = layer_in.shape
    for row in range(0, token_count, ROWS):
        rows = pl.ds(row, ROWS)
        values = layer_in[rows, :].astype(jnp.float32)
        scale = lax.rsqrt(jnp.mean(values * values, axis=-1, keepdims=True) + epsilon)
        normed[rows, :] = (values * scale * gain[...]).astype(jnp.bfloat16)
    width = projected_grad.shape[1]
    blocks = []
    for row in range(0, model_width, attended.shape[1]):
        lanes = pl.ds(row, attended.shape[1])
        blocks.append((normed, lanes, projected_grad, pl.ds(0, width)))
    for lane in range(0, model_width, width):
        blocks.append((attended, pl.ds(0, attended.shape[1]), branch_grad, pl.ds(lane, width)))
    half = len(blocks) // 2
    for number, (left, left_lanes, right, right_lanes) in enumerate(blocks):
        rows = pl.ds(number % half * attended.shape[1], attended.shape[1])
        grad = transposed_dot(left[:, left_lanes], right[:, right_lanes])
        mine = (place[1] & 1) == number // half

        @pl.when(mine)
        def _():
            kept[rows, :] = grad

        @pl.when(jnp.logical_not(mine))
        def _():
            given[rows, :] = grad.astype(jnp.bfloat16)


def norm_back_kernel(own, near, far, residual, inverse, gain, out_grad, residual_grad, low_grad):
    summed = own[...] + near[...].astype(jnp.float32) + far[...].astype(jnp.float32)
    total = out_grad[...].astype(jnp.float32) + rms_backward(
        residual[...], inverse[...], gain[...], summed
    )
    residual_grad[...] = total
    low_grad[...] = total.astype(jnp.bfloat16)


def finish_kernel(own, near, far, layer_in, gain, residual_grad, residual, block):
    span = layer_in.shape[0]
    summed = own[...] + near[...].astype(jnp.float32) + far[...].astype(jnp.float32)
    values = layer_in[...].astype(jnp.float32)
    inverse = lax.rsqrt(jnp.mean(values * values, axis=-1, keepdims=True) + epsilon)
    block[:span, :] = (residual[...] + summed[span:]).astype(jnp.bfloat16)
    block[span : 2 * span, :] = (
        residual_grad[...] + rms_backward(values, inverse, gain[...], summed[:span])
    ).astype(jnp.bfloat16)


def in_vmem(count):
    return [pl.BlockSpec(memory_space=pltpu.VMEM)] * count


def in_hbm(count):
    return [pl.BlockSpec(memory_space=pltpu.HBM)] * count


def in_smem(count):
    return [pl.BlockSpec(memory_space=pltpu.SMEM)] * count


def shaped(shape, dtype):
    return jax.ShapeDtypeStruct(shape, dtype)


def on_device(
    layer_in,
    seq_lengths,
    routes,
    gain_attn,
    w_qkv,
    w_output,
    gain_ffn,
    w_router,
    w_in,
    w_out,
    out_grad,
):
    low, wide = jnp.bfloat16, jnp.float32
    token_count, model_width = layer_in.shape
    kv_here = w_qkv.shape[1]
    experts_all = w_router.shape[1]
    units = w_out.shape[1]
    head_width = kv_here * LANES
    block_count = token_count // ROWS
    tensor_count = lax.axis_size("tensor")
    span = token_count // tensor_count
    tensor_here = lax.axis_index("tensor")
    place = jnp.stack([tensor_here, lax.axis_index("expert")]).astype(jnp.int32)
    mib = 1 << 20

    def token_block(array_in):
        return lax.dynamic_slice_in_dim(array_in, tensor_here * span, span, 0)

    def in_order(blocks):
        joined = jnp.zeros((token_count,) + blocks[0].shape[1:], blocks[0].dtype)
        for number, block in enumerate(blocks):
            joined = lax.dynamic_update_slice_in_dim(
                joined, block, (tensor_here ^ number) * span, 0
            )
        return joined

    core = lax.axis_index("expert") & 1
    half = w_output.shape[0] // 2
    output_own = jnp.where(core == 0, w_output[:half], w_output[half:])
    output_far = exchange(output_own, "tensor", 2)
    output_near = exchange(output_own, "tensor", 1)
    w_in_own, w_out_own = w_in.reshape(2 * units, model_width), w_out[0]
    w_in_near = exchange(w_in_own, "expert", 2)
    w_out_near = exchange(w_out_own, "expert", 4)

    cosine, sine = angle_tables(token_count)
    qkv_flat = w_qkv.reshape(model_width, -1)
    kept = (
        shaped((kv_here, block_count, 2 * ROWS, LANES), low),
        shaped((kv_here, token_count, LANES), low),
        shaped((kv_here, block_count, 2 * ROWS, token_count), low),
    )
    queries, pairs, probs, attended = pl.pallas_call(
        attend_kernel,
        out_shape=kept + (shaped((token_count, head_width), low),),
        in_specs=in_smem(1) + in_vmem(5),
        out_specs=tuple(in_hbm(3) + in_vmem(1)),
        scratch_shapes=[pltpu.VMEM((token_count, model_width), low)]
        + [pltpu.VMEM(each.shape, low) for each in kept]
        + [pltpu.SemaphoreType.DMA((2 + block_count,))],
        compiler_params=pltpu.CompilerParams(vmem_limit_bytes=56 * mib),
        name="attend",
    )(seq_lengths, layer_in, gain_attn[None], qkv_flat, cosine, sine)

    w_in_near, w_out_near, output_far, output_near, attended = lax.optimization_barrier(
        (w_in_near, w_out_near, output_far, output_near, attended)
    )
    w_in_near = jnp.concatenate([w_in_own, w_in_near])
    w_out_near = jnp.concatenate([w_out_own, w_out_near])
    w_in_far = exchange(w_in_near, "expert", 4)
    w_out_far = exchange(w_out_near, "expert", 2)
    heads_far = exchange(attended, "tensor", 2)
    heads_near = exchange(attended, "tensor", 1)
    output_both = exchange(output_far, "tensor", 1)
    heads_far, heads_near, w_in_near, w_out_near = lax.optimization_barrier(
        (heads_far, heads_near, w_in_near, w_out_near)
    )
    heads_both = exchange(heads_far, "tensor", 1)
    heads_both, output_both, w_in_far, w_out_far = lax.optimization_barrier(
        (heads_both, output_both, w_in_far, w_out_far)
    )
    w_in_all = gather_pairs(w_in_near, w_in_far)
    w_out_all = gather_pairs(w_out_near, w_out_far)
    heads_all = [attended, heads_near, heads_far, heads_both]
    output_mine = jnp.concatenate([output_own, output_near, output_far, output_both])
    output_other = exchange(output_mine, "expert", 1)
    router_rows = jnp.pad(jnp.transpose(w_router), ((0, LANES - experts_all), (0, 0)))
    part_shapes = (shaped((span, model_width), wide),) + (
        shaped((span, model_width), low),
    ) * (tensor_count - 1)
    middle = pl.pallas_call(
        functools.partial(middle_kernel, tensor_count),
        out_shape=part_shapes
        + (
            shaped((span, model_width), wide),
            shaped((span, 1), wide),
            shaped((token_count, model_width), low),
            shaped((token_count, experts_all * units), low),
            shaped((token_count, experts_all * 2 * units), low),
            shaped((1, model_width), wide),
            shaped((experts_all, model_width), wide),
        ),
        in_specs=in_smem(1) + in_vmem(16),
        out_specs=tuple(in_vmem(tensor_count + 7)),
        scratch_shapes=[
            pltpu.VMEM((token_count, model_width), wide),
            pltpu.VMEM((token_count, 1), wide),
            pltpu.VMEM((token_count, LANES), wide),
            pltpu.VMEM((token_count, LANES), wide),
            pltpu.VMEM((token_count, 2 * units), wide),
            pltpu.VMEM((token_count, units), wide),
            pltpu.VMEM((token_count, model_width), wide),
        ],
        compiler_params=pltpu.CompilerParams(vmem_limit_bytes=20 * mib),
        name="middle",
    )(
        place,
        gain_ffn[None],
        router_rows,
        routes,
        layer_in,
        out_grad,
        output_mine,
        output_other,
        jnp.concatenate(heads_all),
        *w_in_all,
        *w_out_all,
    )
    normed_parts, middle = middle[:tensor_count], middle[tensor_count:]
    residual, inverse_two, normed_two, active, pre_grad, gain_ffn_part, router_part = middle

    relayed = exchange(normed_parts[3], "tensor", 1)
    half_grads = shaped((experts_all // 2 * 3 * units, model_width), low)
    late = pl.pallas_call(
        functools.partial(weight_grad_kernel, tensor_count),
        out_shape=part_shapes + (half_grads,) * 2,
        in_specs=in_smem(1) + in_vmem(8),
        out_specs=tuple(in_vmem(tensor_count + 2)),
        scratch_shapes=[pltpu.VMEM((token_count, model_width), wide)],
        compiler_params=pltpu.CompilerParams(vmem_limit_bytes=16 * mib),
        name="weight_grad",
    )(place, normed_two, out_grad, active, pre_grad, *w_out_all)
    late, relayed = lax.optimization_barrier((late, relayed))
    normed_pieces = scatter_parts(normed_parts, relayed)
    mixture_parts, kept_grads, given_grads = late[:tensor_count], late[-2], late[-1]
    given_grads = exchange(given_grads, "expert", 1)

    in_rows, out_rows = experts_all * units // 2, experts_all * units // 4
    in_kept, in_given, out_kept, out_given = pl.pallas_call(
        add_grads_kernel,
        out_shape=(
            shaped((in_rows, model_width), wide),
            shaped((in_rows, model_width), low),
            shaped((out_rows, model_width), wide),
            shaped((out_rows, model_width), low),
        ),
        in_specs=in_vmem(2),
        out_specs=tuple(in_vmem(4)),
        compiler_params=pltpu.CompilerParams(vmem_limit_bytes=16 * mib),
        name="add_grads",
    )(kept_grads, given_grads)
    residual, in_kept, in_given, out_kept, out_given = lax.optimization_barrier(
        (residual, in_kept, in_given, out_kept, out_given)
    )
    residual_grad, low_grad = pl.pallas_call(
        norm_back_kernel,
        out_shape=(shaped((span, model_width), wide), shaped((span, model_width), low)),
        in_specs=in_vmem(7),
        out_specs=tuple(in_vmem(2)),
        compiler_params=pltpu.CompilerParams(vmem_limit_bytes=6 * mib),
        name="norm_back",
    )(
        *normed_pieces,
        residual,
        inverse_two,
        gain_ffn[None],
        token_block(out_grad),
    )
    grad_blocks = gather_blocks(low_grad)

    in_arrived = exchange(in_given, "expert", 4)
    out_arrived = exchange(out_given, "expert", 2)
    mixture_last, *grad_blocks = lax.optimization_barrier((mixture_parts[3], *grad_blocks))
    mixture_relayed = exchange(mixture_last, "tensor", 1)
    fetched = (w_output, queries, pairs, probs, cosine, sine, qkv_flat)
    back = pl.pallas_call(
        functools.partial(attend_back_kernel, tensor_count),
        out_shape=(shaped((2 * span, model_width), wide),)
        + (shaped((2 * span, model_width), low),) * (tensor_count - 2)
        + (shaped((span, model_width), low),)
        + (
            shaped((token_count, model_width), low),
            shaped((token_count, 2 * head_width), low),
        ),
        in_specs=in_smem(1) + in_hbm(6 + 2 * tensor_count),
        out_specs=tuple(in_vmem(tensor_count + 2)),
        scratch_shapes=[
            pltpu.VMEM((token_count, head_width), wide),
            pltpu.VMEM((token_count, LANES), wide),
            pltpu.VMEM((token_count, model_width), wide),
        ]
        + [pltpu.VMEM(each.shape, each.dtype) for each in fetched]
        + [pltpu.SemaphoreType.DMA((len(fetched) + 2 * tensor_count,))],
        compiler_params=pltpu.CompilerParams(vmem_limit_bytes=58 * mib),
        name="attend_back",
    )(
        place,
        *fetched,
        *grad_blocks,
        *mixture_parts[:-1],
    )
    input_parts, (branch_grad, projected_grad) = (
        back[:tensor_count],
        back[tensor_count:],
    )
    *input_parts, projected_grad, in_arrived, out_arrived, mixture_relayed = (
        lax.optimization_barrier(
            (*input_parts, projected_grad, in_arrived, out_arrived, mixture_relayed)
        )
    )
    in_summed = in_kept + in_arrived.astype(wide)
    out_summed = out_kept + out_arrived.astype(wide)
    in_arrived = exchange(in_summed[in_rows // 2 :].astype(low), "expert", 2)
    out_arrived = exchange(out_summed[out_rows // 2 :].astype(low), "expert", 4)

    relayed = exchange(input_parts[3], "tensor", 1)
    row_count = (model_width + w_output.shape[0] * model_width // (2 * head_width)) // 2
    kept_sums, given_sums = pl.pallas_call(
        attend_grad_kernel,
        out_shape=(
            shaped((row_count, 2 * head_width), wide),
            shaped((row_count, 2 * head_width), low),
        ),
        in_specs=in_smem(1) + in_vmem(5),
        out_specs=tuple(in_vmem(2)),
        scratch_shapes=[pltpu.VMEM((token_count, model_width), low)],
        compiler_params=pltpu.CompilerParams(vmem_limit_bytes=12 * mib),
        name="attend_grad",
    )(place, layer_in, gain_attn[None], projected_grad, attended, branch_grad)
    relayed, kept_sums, given_sums, in_summed, out_summed = lax.optimization_barrier(
        (relayed, kept_sums, given_sums, in_summed, out_summed)
    )
    sums_half = kept_sums + exchange(given_sums, "expert", 1).astype(wide)
    sums = exchange_halves(sums_half.astype(low), (2, 4))
    input_pieces = scatter_parts(input_parts, jnp.concatenate([relayed, mixture_relayed]))
    residual, in_arrived, out_arrived, sums = lax.optimization_barrier(
        (residual, in_arrived, out_arrived, sums)
    )
    w_in_grad = (in_summed[: in_rows // 2] + in_arrived.astype(wide)).reshape(w_in.shape)
    w_out_grad = (out_summed[: out_rows // 2] + out_arrived.astype(wide)).reshape(w_out.shape)
    block = pl.pallas_call(
        finish_kernel,
        out_shape=shaped((2 * span, model_width), low),
        in_specs=in_vmem(7),
        out_specs=in_vmem(1)[0],
        compiler_params=pltpu.CompilerParams(vmem_limit_bytes=6 * mib),
        name="finish",
    )(
        *input_pieces,
        token_block(layer_in),
        gain_attn[None],
        residual_grad,
        residual,
    )
    far = exchange(block, "tensor", 2)
    near = exchange(block, "tensor", 1)
    small = jnp.concatenate([router_part, gain_ffn_part])
    sums, small, _ = lax.optimization_barrier((sums, small, block))
    small = sum_over_experts(small)
    summed = join_cores(exchange_halves(sums, (4, 2)))
    qkv_summed = summed[:model_width].reshape(w_qkv.shape)
    output_summed = jnp.concatenate(split_blocks(summed[model_width:], 0, 2), 1)

    gain_part = jnp.sum(
        qkv_flat.astype(wide) * summed[:model_width], 1
    ) / gain_attn
    small = jnp.concatenate([small, gain_part[None]])
    far, near, small, summed = lax.optimization_barrier((far, near, small, summed))
    for bit in (1, 2):
        small = small + exchange(small, "tensor", bit)
    blocks = [block, near, far, exchange(far, "tensor", 1)]
    layer_here = in_order([block[:span] for block in blocks])
    in_here = in_order([block[span:] for block in blocks])
    return (
        layer_here,
        in_here,
        small[experts_all + 1],
        qkv_summed,
        output_summed,
        small[experts_all],
        jnp.transpose(small[:experts_all]),
        w_in_grad,
        w_out_grad,
    )


def solution(mesh):
    fits = mesh.shape["tensor"] == 4 and mesh.shape["expert"] == 8
    placed = (
        P("expert", None),
        P("expert", None),
        P("expert", None),
        P(),
        P(None, "tensor", None),
        P("tensor", None),
        P(),
        P(),
        P("expert", None, "tensor", None),
        P("expert", "tensor", None),
        P("expert", None),
    )
    return jax.shard_map(
        on_device if fits else on_device_general,
        mesh=mesh,
        in_specs=placed,
        out_specs=(
            P("expert", None),
            P("expert", None),
            P(),
            P(None, "tensor", None),
            P("tensor", None),
            P(),
            P(),
            P("expert", None, "tensor", None),
            P("expert", "tensor", None),
        ),
        check_vma=False,
    )
```

```python
import functools
import math

import jax
import jax.numpy as jnp
import numpy as np
from jax import lax
from jax.experimental import pallas as pl
from jax.experimental.pallas import tpu as pltpu
from jax.sharding import PartitionSpec as P

HEADS = 16
KV_HEADS = 8
HEAD_DIM = 64


epsilon = 1e-06
rope_base = 10000.0
masked_out = -1e30


def rms_forward(values, gain_vec):
    inverse = lax.rsqrt(jnp.mean(values * values, axis=-1, keepdims=True) + epsilon)
    return (values * inverse * gain_vec, inverse)


def rms_backward(values, inverse, gain_vec, upstream):
    normal = values * inverse
    scaled = upstream * gain_vec
    inner_mean = jnp.mean(scaled * normal, axis=-1, keepdims=True)
    return inverse * (scaled - normal * inner_mean)


def positions(lengths, token_count):
    seq_ends = jnp.cumsum(lengths, dtype=jnp.int32)
    row_index = jnp.arange(token_count, dtype=jnp.int32)
    segment = jnp.sum(
        (row_index[:, None] >= seq_ends[None, :]).astype(jnp.int32), axis=1, dtype=jnp.int32
    )
    seq_ids = jnp.arange(lengths.shape[0], dtype=jnp.int32)
    seq_start = jnp.sum(
        jnp.where(segment[:, None] == seq_ids[None, :], (seq_ends - lengths)[None, :], 0),
        axis=1,
        dtype=jnp.int32,
    )
    return (segment, row_index - seq_start)


def rope_tables(position, head_dim):
    half_dim = head_dim // 2
    inverse_freq = jnp.exp(
        jnp.arange(half_dim, dtype=jnp.float32) * (-2.0 * math.log(rope_base) / head_dim)
    )
    angles = position.astype(jnp.float32)[:, None] * inverse_freq[None, :]
    cosine = jnp.cos(angles)
    sine_tab = jnp.sin(angles)
    return (jnp.concatenate([cosine, cosine], 1), jnp.concatenate([sine_tab, sine_tab], 1))


def rotate(values, cosine, sine_tab):
    half_dim = values.shape[-1] // 2
    turned = jnp.concatenate([-values[..., half_dim:], values[..., :half_dim]], -1)
    return values * cosine + turned * sine_tab


def split_blocks(array_in, axis_at, block_count):
    dims_now = array_in.shape
    regrouped = array_in.reshape(
        dims_now[:axis_at]
        + (block_count, dims_now[axis_at] // block_count)
        + dims_now[axis_at + 1 :]
    )
    return jnp.moveaxis(regrouped, axis_at, 0)


def join_blocks(array_in, axis_at):
    regrouped = jnp.moveaxis(array_in, 0, axis_at)
    dims_now = regrouped.shape
    return regrouped.reshape(
        dims_now[:axis_at] + (dims_now[axis_at] * dims_now[axis_at + 1],) + dims_now[axis_at + 2 :]
    )


def block_scores(query_block, key_rows, segment_rows, row_start, segment, scaling):
    block_rows = query_block.shape[2]
    scores_raw = (
        jnp.einsum("kgbd,ksd->kgbs", query_block, key_rows, preferred_element_type=jnp.float32)
        * scaling
    )
    query_index = row_start + jnp.arange(block_rows, dtype=jnp.int32)
    key_index = jnp.arange(key_rows.shape[1], dtype=jnp.int32)
    allowed = (segment_rows[:, None] == segment[None, :]) & (
        key_index[None, :] <= query_index[:, None]
    )
    return jnp.where(allowed[None, None], scores_raw, masked_out)


def attention_forward(queries, key_rows, values, segment, scaling, block_size):
    block_count = queries.shape[2] // block_size
    starts_all = jnp.arange(block_count, dtype=jnp.int32) * block_size

    def one_block(packed):
        query_block, segment_rows, row_start = packed
        scores = block_scores(query_block, key_rows, segment_rows, row_start, segment, scaling)
        top_score = jnp.max(scores, -1)
        exponent = jnp.exp(scores - top_score[..., None])
        row_total = jnp.sum(exponent, -1)
        probs = (exponent / row_total[..., None]).astype(jnp.bfloat16)
        output = jnp.einsum("kgbs,ksd->kgbd", probs, values, preferred_element_type=jnp.float32)
        return (output.astype(jnp.bfloat16), top_score, row_total)

    outputs, top_blocks, total_blocks = lax.map(
        one_block,
        (
            split_blocks(queries, 2, block_count),
            segment.reshape(block_count, block_size),
            starts_all,
        ),
    )
    return (join_blocks(outputs, 2), join_blocks(top_blocks, 2), join_blocks(total_blocks, 2))


def attention_backward(
    queries, key_rows, values, heads_grad, segment, top_kept, total_kept, scaling, block_size
):
    block_count = queries.shape[2] // block_size
    starts_all = jnp.arange(block_count, dtype=jnp.int32) * block_size

    def one_block(running, packed):
        key_acc, value_acc = running
        query_block, grad_block, segment_rows, row_start, top_block, total_block = packed
        scores = block_scores(query_block, key_rows, segment_rows, row_start, segment, scaling)
        probs = jnp.exp(scores - top_block[..., None]) / total_block[..., None]
        probs_low = probs.astype(jnp.bfloat16)
        value_acc = value_acc + jnp.einsum(
            "kgbs,kgbd->ksd", probs_low, grad_block, preferred_element_type=jnp.float32
        )
        prob_grad = jnp.einsum(
            "kgbd,ksd->kgbs", grad_block, values, preferred_element_type=jnp.float32
        )
        inner_sum = jnp.sum(probs * prob_grad, -1, keepdims=True)
        score_grad = (probs * (prob_grad - inner_sum)).astype(jnp.bfloat16)
        query_grad = (
            jnp.einsum("kgbs,ksd->kgbd", score_grad, key_rows, preferred_element_type=jnp.float32)
            * scaling
        )
        key_acc = (
            key_acc
            + jnp.einsum(
                "kgbs,kgbd->ksd", score_grad, query_block, preferred_element_type=jnp.float32
            )
            * scaling
        )
        return ((key_acc, value_acc), query_grad)

    empty = jnp.zeros(key_rows.shape, jnp.float32)
    packed_all = (
        split_blocks(queries, 2, block_count),
        split_blocks(heads_grad, 2, block_count),
        segment.reshape(block_count, block_size),
        starts_all,
        split_blocks(top_kept, 2, block_count),
        split_blocks(total_kept, 2, block_count),
    )
    (key_grad, value_grad), query_blocks = lax.scan(one_block, (empty, empty), packed_all)
    return (join_blocks(query_blocks, 2), key_grad, value_grad)


def on_device_general(
    layer_in,
    seq_lengths,
    routes,
    gain_attn,
    w_qkv,
    w_output,
    gain_ffn,
    w_router,
    w_in,
    w_out,
    out_grad,
):
    token_count, model_width = layer_in.shape
    kv_here = w_qkv.shape[1]
    group_size = HEADS // KV_HEADS
    scaling = 1.0 / math.sqrt(HEAD_DIM)
    block_size = min(512, token_count)
    w_output_all = lax.all_gather(w_output, "tensor", axis=0, tiled=True)
    w_gate_all = lax.all_gather(w_in[0, 0], "expert", axis=0, tiled=True)
    w_up_all = lax.all_gather(w_in[0, 1], "expert", axis=0, tiled=True)
    w_out_all = lax.all_gather(w_out[0], "expert", axis=0, tiled=True)
    segment, position = positions(seq_lengths[0], token_count)
    cosine, sine_tab = rope_tables(position, HEAD_DIM)
    inputs = layer_in.astype(jnp.float32)
    normed_one, inverse_one = rms_forward(inputs, gain_attn)
    normed_one_low = normed_one.astype(jnp.bfloat16)
    qkv_flat = w_qkv.reshape(model_width, -1)
    projected = jnp.dot(normed_one_low, qkv_flat, preferred_element_type=jnp.float32)
    projected = projected.reshape(token_count, kv_here, group_size + 2, HEAD_DIM)
    queries = rotate(
        jnp.transpose(projected[:, :, :group_size], (1, 2, 0, 3)), cosine, sine_tab
    ).astype(jnp.bfloat16)
    key_rows = rotate(
        jnp.transpose(projected[:, :, group_size], (1, 0, 2)), cosine, sine_tab
    ).astype(jnp.bfloat16)
    values = jnp.transpose(projected[:, :, group_size + 1], (1, 0, 2)).astype(jnp.bfloat16)
    attended, top_kept, total_kept = attention_forward(
        queries, key_rows, values, segment, scaling, block_size
    )
    heads_out = jnp.transpose(attended, (2, 0, 1, 3)).reshape(token_count, -1)
    heads_all = lax.all_gather(heads_out, "tensor", axis=1, tiled=True)
    branch_here = jnp.dot(heads_all, w_output_all, preferred_element_type=jnp.float32)
    residual = inputs + branch_here
    normed_two, inverse_two = rms_forward(residual, gain_ffn)
    normed_low = normed_two.astype(jnp.bfloat16)
    experts_all = w_router.shape[1]
    unit_count = w_out.shape[1]
    logits = jnp.dot(normed_low, w_router, preferred_element_type=jnp.float32)
    expert_ids = jnp.arange(experts_all, dtype=jnp.int32)
    picked = jnp.any(routes[:, :, None] == expert_ids[None, None, :], axis=1)
    picked_logits = jnp.where(picked, logits, masked_out)
    top_logit = jnp.max(picked_logits, -1, keepdims=True)
    weight = jnp.where(picked, jnp.exp(picked_logits - top_logit), 0.0)
    gates = weight / jnp.sum(weight, -1, keepdims=True)

    def by_unit(per_expert):
        return jnp.broadcast_to(
            per_expert[:, :, None], (token_count, experts_all, unit_count)
        ).reshape(token_count, -1)

    def over_units(per_unit):
        return jnp.sum(per_unit.reshape(token_count, experts_all, unit_count), -1)

    def times_transposed(left, right):
        return lax.dot_general(
            left, right, (((1,), (1,)), ((), ())), preferred_element_type=jnp.float32
        )

    def transposed_times(left, right):
        return lax.dot_general(
            left, right, (((0,), (0,)), ((), ())), preferred_element_type=jnp.float32
        )

    gates_wide = by_unit(gates)
    gate_vals = times_transposed(normed_low, w_gate_all)
    up_vals = times_transposed(normed_low, w_up_all)
    plain_grad = times_transposed(out_grad, w_out_all)
    sig_vals = jax.nn.sigmoid(gate_vals)
    silu_vals = gate_vals * sig_vals
    active = silu_vals * up_vals
    scaled_active = (active * gates_wide).astype(jnp.bfloat16)
    active_grad = plain_grad * gates_wide
    gate_pre = (
        active_grad * up_vals * (sig_vals * (1.0 + gate_vals * (1.0 - sig_vals)))
    ).astype(jnp.bfloat16)
    up_pre = (active_grad * silu_vals).astype(jnp.bfloat16)
    gate_grad_part = over_units(active * plain_grad)
    logit_part = (
        gates * (gate_grad_part - jnp.sum(gates * gate_grad_part, -1, keepdims=True))
    ).astype(jnp.bfloat16)
    normed_two_part = (
        jnp.dot(gate_pre, w_gate_all, preferred_element_type=jnp.float32)
        + jnp.dot(up_pre, w_up_all, preferred_element_type=jnp.float32)
        + times_transposed(logit_part, w_router)
    )
    normed_two_grad = lax.psum(normed_two_part.astype(jnp.bfloat16), "tensor").astype(jnp.float32)
    mixture_part = jnp.dot(scaled_active, w_out_all, preferred_element_type=jnp.float32)
    mixture = lax.psum(mixture_part.astype(jnp.bfloat16), "tensor").astype(jnp.float32)
    layer_here = (residual + mixture).astype(jnp.bfloat16)

    def to_owner(partial):
        return lax.psum_scatter(
            partial.astype(jnp.bfloat16), "expert", scatter_dimension=0, tiled=True
        ).astype(jnp.float32)

    w_gate_grad = to_owner(transposed_times(gate_pre, normed_low))
    w_up_grad = to_owner(transposed_times(up_pre, normed_low))
    w_in_grad = jnp.stack([w_gate_grad, w_up_grad])[None]
    w_out_grad = to_owner(transposed_times(scaled_active, out_grad))[None]
    router_part = transposed_times(logit_part, normed_low)
    normal_two = residual * inverse_two
    gain_ffn_part = jnp.sum(normed_two_part * normal_two, axis=0)
    upstream = out_grad.astype(jnp.float32)
    residual_part = rms_backward(residual, inverse_two, gain_ffn, normed_two_grad)
    residual_grad = upstream + residual_part
    branch_here_grad = residual_grad.astype(jnp.bfloat16)
    w_output_grad = lax.dot_general(
        heads_out, branch_here_grad, (((0,), (0,)), ((), ())), preferred_element_type=jnp.float32
    )
    heads_flat = lax.dot_general(
        branch_here_grad, w_output, (((1,), (1,)), ((), ())), preferred_element_type=jnp.float32
    ).astype(jnp.bfloat16)
    heads_grad = jnp.transpose(
        heads_flat.reshape(token_count, kv_here, group_size, HEAD_DIM), (1, 2, 0, 3)
    )
    query_grad, key_grad, value_grad = attention_backward(
        queries, key_rows, values, heads_grad, segment, top_kept, total_kept, scaling, block_size
    )
    query_grad = rotate(query_grad, cosine, -sine_tab)
    key_grad = rotate(key_grad, cosine, -sine_tab)
    projected_grad = jnp.concatenate(
        [
            jnp.transpose(query_grad, (2, 0, 1, 3)),
            jnp.transpose(key_grad, (1, 0, 2))[:, :, None],
            jnp.transpose(value_grad, (1, 0, 2))[:, :, None],
        ],
        2,
    )
    projected_grad = projected_grad.reshape(token_count, -1).astype(jnp.bfloat16)
    w_qkv_grad = lax.dot_general(
        normed_one_low, projected_grad, (((0,), (0,)), ((), ())), preferred_element_type=jnp.float32
    ).reshape(w_qkv.shape)
    normed_one_part = lax.dot_general(
        projected_grad, qkv_flat, (((1,), (1,)), ((), ())), preferred_element_type=jnp.float32
    )
    gain_attn_part = jnp.sum(normed_one_part * (inputs * inverse_one), axis=0)
    normed_one_grad = lax.psum(normed_one_part.astype(jnp.bfloat16), "tensor").astype(jnp.float32)
    input_part = rms_backward(inputs, inverse_one, gain_attn, normed_one_grad)
    in_here = (residual_grad + input_part).astype(jnp.bfloat16)
    qkv_summed = lax.psum(w_qkv_grad.astype(jnp.bfloat16), "expert").astype(jnp.float32)
    output_summed = lax.psum(w_output_grad.astype(jnp.bfloat16), "expert").astype(jnp.float32)
    small = jnp.concatenate([router_part, gain_ffn_part[None], gain_attn_part[None]])
    small = lax.psum(small, ("expert", "tensor"))
    return (
        layer_here,
        in_here,
        small[experts_all + 1],
        qkv_summed,
        output_summed,
        small[experts_all],
        jnp.transpose(small[:experts_all]),
        w_in_grad,
        w_out_grad,
    )


LANES = 128
ROWS = 128
IN_ORDER = (0, 2, 4, 6, 1, 3, 5, 7)
OUT_ORDER = (0, 4, 2, 6, 1, 5, 3, 7)


def exchange(array_in, axis_name, bits):
    count = lax.axis_size(axis_name)
    return lax.ppermute(array_in, axis_name, [(i, i ^ bits) for i in range(count)])


def gather_blocks(own):
    far = exchange(own, "tensor", 2)
    near = exchange(own, "tensor", 1)
    far, near = lax.optimization_barrier((far, near))
    return [own, near, far, exchange(far, "tensor", 1)]


def scatter_parts(parts, relayed):
    near, far, relayed = lax.optimization_barrier((parts[1], parts[2], relayed))
    far = (far.astype(jnp.float32) + relayed.astype(jnp.float32)).astype(jnp.bfloat16)
    far = exchange(far, "tensor", 2)
    return parts[0], exchange(near, "tensor", 1), far


def gather_pairs(near, far):
    return [near, far, exchange(near, "expert", 1), exchange(far, "expert", 1)]


def exchange_halves(array_in, bits):
    rows = array_in.shape[0] // 2
    halves = []
    for half, bit in zip((array_in[:rows], array_in[rows:]), bits):
        arrived = exchange(half, "expert", bit)
        halves.append((half.astype(jnp.float32) + arrived.astype(jnp.float32)).astype(jnp.bfloat16))
    return jnp.concatenate(halves)


def join_cores(half):
    core = lax.axis_index("expert") & 1
    other = exchange(half, "expert", 1)
    return jnp.concatenate(
        [jnp.where(core == 0, half, other), jnp.where(core == 0, other, half)]
    ).astype(jnp.float32)


def sum_over_experts(array_in):
    for bit in (1, 2, 4):
        array_in = array_in + exchange(array_in, "expert", bit)
    return array_in


def dot_plain(left, right):
    return jnp.dot(left, right, preferred_element_type=jnp.float32)


def dot_transposed(left, right):
    return lax.dot_general(
        left, right, (((1,), (1,)), ((), ())), preferred_element_type=jnp.float32
    )


def transposed_dot(left, right):
    return lax.dot_general(
        left, right, (((0,), (0,)), ((), ())), preferred_element_type=jnp.float32
    )


def lane_index(shape):
    return lax.broadcasted_iota(jnp.int32, shape, 1)


def turn(values):
    low_half = (lane_index(values.shape) & (HEAD_DIM - 1)) < HEAD_DIM // 2
    return jnp.where(
        low_half,
        -pltpu.roll(values, LANES - HEAD_DIM // 2, 1),
        pltpu.roll(values, HEAD_DIM // 2, 1),
    )


def swap_heads(values):
    return pltpu.roll(values, HEAD_DIM, 1)


def first_head(shape):
    return lane_index(shape) < HEAD_DIM


def angle_tables(token_count):
    half_dim = HEAD_DIM // 2
    inverse_freq = np.exp(np.arange(half_dim) * (-2.0 * math.log(rope_base) / HEAD_DIM))
    angles = np.arange(token_count)[:, None] * inverse_freq[None, :]
    tile = LANES // half_dim
    return (
        np.tile(np.cos(angles), (1, tile)).astype(np.float32),
        np.tile(np.sin(angles), (1, tile)).astype(np.float32),
    )


def attend_kernel(
    lengths,
    layer_in,
    gain,
    w_qkv,
    cosine,
    sine,
    queries_out,
    pairs_out,
    probs_out,
    attended,
    normed,
    queries,
    pairs,
    probs,
    sems,
):
    token_count = layer_in.shape[0]
    kv_here = pairs.shape[0]
    for row in range(0, token_count, ROWS):
        rows = pl.ds(row, ROWS)
        values = layer_in[rows, :].astype(jnp.float32)
        scale = lax.rsqrt(jnp.mean(values * values, axis=-1, keepdims=True) + epsilon)
        normed[rows, :] = (values * scale * gain[...]).astype(jnp.bfloat16)
    is_first = first_head((ROWS, LANES))
    for kv in range(kv_here):
        projected = dot_plain(normed[...], w_qkv[:, 2 * LANES * kv : 2 * LANES * (kv + 1)])
        for block in range(token_count // ROWS):
            rows = pl.ds(block * ROWS, ROWS)
            cos_rows, sin_rows = cosine[rows, :], sine[rows, :]
            query = projected[block * ROWS : (block + 1) * ROWS, :LANES]
            query = (query * cos_rows + turn(query) * sin_rows) * (1.0 / math.sqrt(HEAD_DIM))
            queries[kv, block, :ROWS, :] = jnp.where(is_first, query, 0.0).astype(jnp.bfloat16)
            queries[kv, block, ROWS:, :] = jnp.where(is_first, swap_heads(query), 0.0).astype(
                jnp.bfloat16
            )
            pair = projected[block * ROWS : (block + 1) * ROWS, LANES:]
            pairs[kv, rows, :] = jnp.where(
                is_first, pair * cos_rows + turn(pair) * sin_rows, pair
            ).astype(jnp.bfloat16)
    copies = [
        pltpu.make_async_copy(queries, queries_out, sems.at[0]),
        pltpu.make_async_copy(pairs, pairs_out, sems.at[1]),
    ]
    for copy in copies:
        copy.start()
    for block in range(token_count // ROWS):
        keys = (block + 1) * ROWS
        token = block * ROWS + (
            lax.broadcasted_iota(jnp.int32, (2 * ROWS, keys), 0) & (ROWS - 1)
        )
        start = jnp.zeros_like(token)
        end = 0
        for seq in range(lengths.shape[1] - 1):
            end = end + lengths[0, seq]
            start = jnp.where(token >= end, end, start)
        key = lane_index((2 * ROWS, keys))
        allowed = (key <= token) & (key >= start)
        for kv in range(kv_here):
            scores = dot_transposed(queries[kv, block], pairs[kv, :keys, :])
            scores = jnp.where(allowed, scores, masked_out)
            exponent = jnp.exp(scores - jnp.max(scores, -1, keepdims=True))
            share = (exponent * (1.0 / jnp.sum(exponent, -1, keepdims=True))).astype(jnp.bfloat16)
            probs[kv, block, :, :keys] = share
            output = dot_plain(share, pairs[kv, :keys, :])
            attended[pl.ds(block * ROWS, ROWS), kv * LANES : (kv + 1) * LANES] = jnp.where(
                is_first, swap_heads(output[:ROWS]), output[ROWS:]
            ).astype(jnp.bfloat16)
        copies.append(
            pltpu.make_async_copy(
                probs.at[:, block, :, :keys], probs_out.at[:, block, :, :keys], sems.at[2 + block]
            )
        )
        copies[-1].start()
    for copy in copies:
        copy.wait()


def write_parts(place, total, parts, span):
    for number, part in enumerate(parts):
        row = pl.multiple_of((place[0] ^ number) * span, span)
        part[...] = total[pl.ds(row, span), :].astype(part.dtype)


def branch_kernel(
    place,
    gain,
    router,
    routes,
    layer_in,
    w_mine,
    w_other,
    heads,
    residual,
    inverse,
    normed,
    gates,
    w_output,
):
    token_count, model_width = layer_in.shape
    half = LANES
    mine = (place[1] & 1) * half
    for row in range(0, model_width, 2 * half):
        rows = pl.ds(row // 2, half)
        w_output[pl.ds(pl.multiple_of(row + mine, half), half), :] = w_mine[rows, :]
        w_output[pl.ds(pl.multiple_of(row + half - mine, half), half), :] = w_other[rows, :]

    def branch_step(number, carry):
        columns = pl.ds(pl.multiple_of(number * 2 * LANES, 2 * LANES), 2 * LANES)
        residual[:, columns] = layer_in[:, columns].astype(jnp.float32) + dot_plain(
            heads[...], w_output[:, columns]
        )
        return carry

    lax.fori_loop(0, model_width // (2 * LANES), branch_step, 0)
    for row in range(0, token_count, ROWS):
        rows = pl.ds(row, ROWS)
        values = residual[rows, :]
        scale = lax.rsqrt(jnp.mean(values * values, axis=-1, keepdims=True) + epsilon)
        inverse[rows, :] = scale
        normed[rows, :] = (values * scale * gain[...]).astype(jnp.bfloat16)
    gates[...] = dot_transposed(normed[...], router[...])
    lane = lane_index((ROWS, LANES))
    for row in range(0, token_count, ROWS):
        rows = pl.ds(row, ROWS)
        picked = routes[rows, 0:1] == lane
        for top in range(1, routes.shape[1]):
            picked = picked | (routes[rows, top : top + 1] == lane)
        logits = jnp.where(picked, gates[rows, :], masked_out)
        weight = jnp.where(picked, jnp.exp(logits - jnp.max(logits, -1, keepdims=True)), 0.0)
        gates[rows, :] = weight / jnp.sum(weight, -1, keepdims=True)


def middle_kernel(tensor_count, *refs):
    place, router, out_grad, residual, inverse, normed, gates = refs[:7]
    w_ins, w_outs, refs = refs[7:11], refs[11:15], refs[15:]
    parts, refs = refs[:tensor_count], refs[tensor_count:]
    (residual_block, inverse_block, active_out, pre_out, gain_part, router_part) = refs[:6]
    (gate_wide, product, hidden, plain, total) = refs[6:]
    token_count, model_width = normed.shape
    experts_all = router_part.shape[0]
    units = w_outs[0].shape[0] // 2
    span = token_count // tensor_count
    for pair, weights in enumerate(w_outs):
        plain[:, 2 * pair * units : 2 * (pair + 1) * units] = dot_transposed(
            out_grad[...], weights[...]
        )
    gates_high = gates[...].astype(jnp.bfloat16)
    gates_low = (gates[...] - gates_high.astype(jnp.float32)).astype(jnp.bfloat16)
    total_grad = jnp.zeros((token_count, LANES), jnp.float32)
    for number in range(experts_all):
        name = place[1] ^ IN_ORDER[number]
        in_rows = pl.ds(number % 2 * 2 * units, 2 * units)
        out_number = OUT_ORDER.index(IN_ORDER[number])
        hidden[...] = dot_transposed(normed[...], w_ins[number // 2][in_rows, :])
        out_lanes = pl.ds(out_number * units, units)
        chosen = lax.broadcasted_iota(jnp.int32, (LANES, units), 0) == name
        chosen = jnp.where(chosen, 1.0, 0.0).astype(jnp.bfloat16)
        gate_wide[...] = dot_plain(gates_high, chosen) + dot_plain(gates_low, chosen)
        for row in range(0, token_count, ROWS):
            rows = pl.ds(row, ROWS)
            gate = gate_wide[rows, :]
            gate_vals, up_vals = hidden[rows, :units], hidden[rows, units:]
            sig_vals = 0.5 + 0.5 * jnp.tanh(0.5 * gate_vals)
            silu_vals = gate_vals * sig_vals
            active = silu_vals * up_vals
            grad = plain[rows, out_lanes]
            product[rows, :] = (active * grad).astype(jnp.bfloat16)
            active_grad = grad * gate
            active_out[rows, out_number * units : (out_number + 1) * units] = (
                active * gate
            ).astype(jnp.bfloat16)
            pre_out[rows, 2 * number * units : (2 * number + 1) * units] = (
                active_grad * up_vals * (sig_vals * (1.0 + gate_vals * (1.0 - sig_vals)))
            ).astype(jnp.bfloat16)
            pre_out[rows, (2 * number + 1) * units : (2 * number + 2) * units] = (
                active_grad * silu_vals
            ).astype(jnp.bfloat16)
        total_grad = total_grad + dot_transposed(product[...], chosen)
    gate_all, grad_all = gates[...], total_grad
    logit_part = (
        gate_all * (grad_all - jnp.sum(gate_all * grad_all, -1, keepdims=True))
    ).astype(jnp.bfloat16)
    router_part[...] = transposed_dot(logit_part, normed[...])[:experts_all]

    def column_step(number, carry):
        columns = pl.ds(pl.multiple_of(number * 2 * LANES, 2 * LANES), 2 * LANES)
        summed = dot_plain(logit_part, router[:, columns])
        for pair, weights in enumerate(w_ins):
            pre = pre_out[:, 4 * pair * units : 4 * (pair + 1) * units]
            summed = summed + dot_plain(pre, weights[:, columns])
        total[:, columns] = summed
        return carry

    lax.fori_loop(0, model_width // (2 * LANES), column_step, 0)
    write_parts(place, total, parts, span)
    row = pl.ds(pl.multiple_of(place[0] * span, span), span)
    residual_block[...] = residual[row, :]
    inverse_block[...] = inverse[row, :]
    gain_sum = jnp.zeros((1, model_width), jnp.float32)
    for row in range(0, token_count, ROWS):
        rows = pl.ds(row, ROWS)
        gain_sum = gain_sum + jnp.sum(
            total[rows, :] * (residual[rows, :] * inverse[rows, :]), 0, keepdims=True
        )
    gain_part[...] = gain_sum


def weight_grad_kernel(tensor_count, *refs):
    place, normed, out_grad, active, pre_grad = refs[:5]
    w_outs, parts = refs[5:9], refs[9 : 9 + tensor_count]
    kept, given, total = refs[9 + tensor_count :]
    token_count, model_width = normed.shape
    units = w_outs[0].shape[0] // 2
    experts_all = 2 * kept.shape[0] // (3 * units)

    def column_step(number, carry):
        columns = pl.ds(pl.multiple_of(number * 2 * LANES, 2 * LANES), 2 * LANES)
        summed = jnp.zeros((token_count, 2 * LANES), jnp.float32)
        for pair, weights in enumerate(w_outs):
            summed = summed + dot_plain(
                active[:, 2 * pair * units : 2 * (pair + 1) * units], weights[:, columns]
            )
        total[:, columns] = summed
        return carry

    lax.fori_loop(0, model_width // (2 * LANES), column_step, 0)
    write_parts(place, total, parts, token_count // tensor_count)
    for number in range(experts_all):
        out_number = OUT_ORDER.index(IN_ORDER[number])
        grads = kept if number < experts_all // 2 else given
        in_row = number % (experts_all // 2) * 2 * units
        out_row = experts_all * units + out_number % (experts_all // 2) * units
        grads[pl.ds(in_row, 2 * units), :] = transposed_dot(
            pre_grad[:, 2 * number * units : 2 * (number + 1) * units], normed[...]
        ).astype(jnp.bfloat16)
        grads[pl.ds(out_row, units), :] = transposed_dot(
            active[:, out_number * units : (out_number + 1) * units], out_grad[...]
        ).astype(jnp.bfloat16)


def add_grads_kernel(kept, given, in_kept, in_given, out_kept, out_given):
    row = 0
    for target in (in_kept, in_given, out_kept, out_given):
        rows = pl.ds(row, target.shape[0])
        summed = kept[rows, :].astype(jnp.float32) + given[rows, :].astype(jnp.float32)
        target[...] = summed.astype(target.dtype)
        row += target.shape[0]


def attend_back_kernel(tensor_count, *refs):
    place, far_refs, refs = refs[0], refs[1:8], refs[8:]
    blocks, refs = refs[:tensor_count], refs[tensor_count:]
    mixtures, refs = refs[: tensor_count - 1], refs[tensor_count - 1 :]
    parts, refs = refs[:tensor_count], refs[tensor_count:]
    branch_grad, projected_grad, heads_grad, pair_grad, total = refs[:5]
    near_refs, sems = refs[5:12], refs[12]
    w_output, queries, pairs, probs, cosine, sine, w_qkv = near_refs
    copies, prob_copies = [], []
    for number, (source, target) in enumerate(zip(far_refs, near_refs)):
        if target is probs:
            for block in range(probs.shape[1]):
                part = (slice(None), block, slice(None), slice((block + 1) * ROWS))
                prob_copies.append(
                    pltpu.make_async_copy(
                        source.at[part], target.at[part], sems.at[len(near_refs) + block]
                    )
                )
        else:
            copies.append(pltpu.make_async_copy(source, target, sems.at[number]))
    more = len(near_refs) + len(prob_copies)
    token_count, model_width = branch_grad.shape
    span = token_count // tensor_count
    mixture_copies = [
        pltpu.make_async_copy(mixture, part.at[pl.ds(span, span)], sems.at[more + number])
        for number, (mixture, part) in enumerate(zip(mixtures, parts[:-1]))
    ]
    block_copies = []
    for number, block in enumerate(blocks):
        row = pl.multiple_of((place[0] ^ number) * span, span)
        block_copies.append(
            pltpu.make_async_copy(
                block,
                branch_grad.at[pl.ds(row, span)],
                sems.at[more + tensor_count + number],
            )
        )
    for copy in block_copies + copies[:5] + prob_copies + copies[5:] + mixture_copies:
        copy.start()
    for copy in copies[:1] + block_copies:
        copy.wait()
    heads_grad[...] = dot_transposed(branch_grad[...], w_output[...])
    for copy in copies[1:5]:
        copy.wait()
    is_first = first_head((ROWS, LANES))
    for kv in range(pairs.shape[0]):
        pair_grad[...] = jnp.zeros_like(pair_grad)
        for block in range(token_count // ROWS):
            keys = (block + 1) * ROWS
            rows = pl.ds(block * ROWS, ROWS)
            upper = heads_grad[rows, kv * LANES : (kv + 1) * LANES]
            upper = jnp.concatenate(
                [
                    jnp.where(is_first, 0.0, swap_heads(upper)),
                    jnp.where(is_first, 0.0, upper),
                ]
            ).astype(jnp.bfloat16)
            if kv == 0:
                prob_copies[block].wait()
            share_low = probs[kv, block, :, :keys]
            share = share_low.astype(jnp.float32)
            prob_grad = dot_transposed(upper, pairs[kv, :keys, :])
            inner = jnp.sum(share * prob_grad, -1, keepdims=True)
            score_grad = (share * (prob_grad - inner)).astype(jnp.bfloat16)
            query_grad = dot_plain(score_grad, pairs[kv, :keys, :])
            query_grad = jnp.where(
                is_first, query_grad[:ROWS], swap_heads(query_grad[ROWS:])
            ) * (1.0 / math.sqrt(HEAD_DIM))
            projected_grad[rows, 2 * kv * LANES : (2 * kv + 1) * LANES] = (
                query_grad * cosine[rows, :] - turn(query_grad) * sine[rows, :]
            ).astype(jnp.bfloat16)
            pair_grad[:keys, :] = (
                pair_grad[:keys, :]
                + transposed_dot(score_grad, queries[kv, block])
                + transposed_dot(share_low, upper)
            )
        for block in range(token_count // ROWS):
            rows = pl.ds(block * ROWS, ROWS)
            grad = pair_grad[rows, :]
            projected_grad[rows, (2 * kv + 1) * LANES : (2 * kv + 2) * LANES] = jnp.where(
                is_first, grad * cosine[rows, :] - turn(grad) * sine[rows, :], grad
            ).astype(jnp.bfloat16)

    for copy in copies[5:]:
        copy.wait()

    def column_step(number, carry):
        columns = pl.ds(pl.multiple_of(number * 2 * LANES, 2 * LANES), 2 * LANES)
        total[:, columns] = dot_transposed(projected_grad[...], w_qkv[columns, :])
        return carry

    lax.fori_loop(0, model_width // (2 * LANES), column_step, 0)
    write_parts(place, total, [part.at[:span] for part in parts[:-1]] + [parts[-1]], span)
    for copy in mixture_copies:
        copy.wait()


def attend_grad_kernel(
    place, layer_in, gain, projected_grad, attended, branch_grad, kept, given, normed
):
    token_count, model_width = layer_in.shape
    for row in range(0, token_count, ROWS):
        rows = pl.ds(row, ROWS)
        values = layer_in[rows, :].astype(jnp.float32)
        scale = lax.rsqrt(jnp.mean(values * values, axis=-1, keepdims=True) + epsilon)
        normed[rows, :] = (values * scale * gain[...]).astype(jnp.bfloat16)
    width = projected_grad.shape[1]
    blocks = []
    for row in range(0, model_width, attended.shape[1]):
        lanes = pl.ds(row, attended.shape[1])
        blocks.append((normed, lanes, projected_grad, pl.ds(0, width)))
    for lane in range(0, model_width, width):
        blocks.append((attended, pl.ds(0, attended.shape[1]), branch_grad, pl.ds(lane, width)))
    half = len(blocks) // 2
    for number, (left, left_lanes, right, right_lanes) in enumerate(blocks):
        rows = pl.ds(number % half * attended.shape[1], attended.shape[1])
        grad = transposed_dot(left[:, left_lanes], right[:, right_lanes])
        mine = (place[1] & 1) == number // half

        @pl.when(mine)
        def _():
            kept[rows, :] = grad

        @pl.when(jnp.logical_not(mine))
        def _():
            given[rows, :] = grad.astype(jnp.bfloat16)


def norm_back_kernel(own, near, far, residual, inverse, gain, out_grad, residual_grad, low_grad):
    summed = own[...] + near[...].astype(jnp.float32) + far[...].astype(jnp.float32)
    total = out_grad[...].astype(jnp.float32) + rms_backward(
        residual[...], inverse[...], gain[...], summed
    )
    residual_grad[...] = total
    low_grad[...] = total.astype(jnp.bfloat16)


def finish_kernel(own, near, far, layer_in, gain, residual_grad, residual, block):
    span = layer_in.shape[0]
    summed = own[...] + near[...].astype(jnp.float32) + far[...].astype(jnp.float32)
    values = layer_in[...].astype(jnp.float32)
    inverse = lax.rsqrt(jnp.mean(values * values, axis=-1, keepdims=True) + epsilon)
    block[:span, :] = (residual[...] + summed[span:]).astype(jnp.bfloat16)
    block[span : 2 * span, :] = (
        residual_grad[...] + rms_backward(values, inverse, gain[...], summed[:span])
    ).astype(jnp.bfloat16)


def in_vmem(count):
    return [pl.BlockSpec(memory_space=pltpu.VMEM)] * count


def in_hbm(count):
    return [pl.BlockSpec(memory_space=pltpu.HBM)] * count


def in_smem(count):
    return [pl.BlockSpec(memory_space=pltpu.SMEM)] * count


def shaped(shape, dtype):
    return jax.ShapeDtypeStruct(shape, dtype)


def on_device(
    layer_in,
    seq_lengths,
    routes,
    gain_attn,
    w_qkv,
    w_output,
    gain_ffn,
    w_router,
    w_in,
    w_out,
    out_grad,
):
    low, wide = jnp.bfloat16, jnp.float32
    token_count, model_width = layer_in.shape
    kv_here = w_qkv.shape[1]
    experts_all = w_router.shape[1]
    units = w_out.shape[1]
    head_width = kv_here * LANES
    block_count = token_count // ROWS
    tensor_count = lax.axis_size("tensor")
    span = token_count // tensor_count
    tensor_here = lax.axis_index("tensor")
    place = jnp.stack([tensor_here, lax.axis_index("expert")]).astype(jnp.int32)
    mib = 1 << 20

    def token_block(array_in):
        return lax.dynamic_slice_in_dim(array_in, tensor_here * span, span, 0)

    def in_order(blocks):
        joined = jnp.zeros((token_count,) + blocks[0].shape[1:], blocks[0].dtype)
        for number, block in enumerate(blocks):
            joined = lax.dynamic_update_slice_in_dim(
                joined, block, (tensor_here ^ number) * span, 0
            )
        return joined

    core = lax.axis_index("expert") & 1
    half = w_output.shape[0] // 2
    output_own = jnp.where(core == 0, w_output[:half], w_output[half:])
    output_far = exchange(output_own, "tensor", 2)
    output_near = exchange(output_own, "tensor", 1)
    w_in_own, w_out_own = w_in.reshape(2 * units, model_width), w_out[0]
    w_in_near = exchange(w_in_own, "expert", 2)
    w_out_near = exchange(w_out_own, "expert", 4)

    cosine, sine = angle_tables(token_count)
    qkv_flat = w_qkv.reshape(model_width, -1)
    kept = (
        shaped((kv_here, block_count, 2 * ROWS, LANES), low),
        shaped((kv_here, token_count, LANES), low),
        shaped((kv_here, block_count, 2 * ROWS, token_count), low),
    )
    queries, pairs, probs, attended = pl.pallas_call(
        attend_kernel,
        out_shape=kept + (shaped((token_count, head_width), low),),
        in_specs=in_smem(1) + in_vmem(5),
        out_specs=tuple(in_hbm(3) + in_vmem(1)),
        scratch_shapes=[pltpu.VMEM((token_count, model_width), low)]
        + [pltpu.VMEM(each.shape, low) for each in kept]
        + [pltpu.SemaphoreType.DMA((2 + block_count,))],
        compiler_params=pltpu.CompilerParams(vmem_limit_bytes=56 * mib),
        name="attend",
    )(seq_lengths, layer_in, gain_attn[None], qkv_flat, cosine, sine)

    w_in_near, w_out_near, output_far, output_near, attended = lax.optimization_barrier(
        (w_in_near, w_out_near, output_far, output_near, attended)
    )
    w_in_near = jnp.concatenate([w_in_own, w_in_near])
    w_out_near = jnp.concatenate([w_out_own, w_out_near])
    w_in_far = exchange(w_in_near, "expert", 4)
    w_out_far = exchange(w_out_near, "expert", 2)
    heads_far = exchange(attended, "tensor", 2)
    heads_near = exchange(attended, "tensor", 1)
    output_both = exchange(output_far, "tensor", 1)
    heads_far, heads_near, w_in_near, w_out_near, output_both = lax.optimization_barrier(
        (heads_far, heads_near, w_in_near, w_out_near, output_both)
    )
    heads_both = exchange(heads_far, "tensor", 1)
    heads_both, w_in_far, w_out_far = lax.optimization_barrier((heads_both, w_in_far, w_out_far))
    w_in_all = gather_pairs(w_in_near, w_in_far)
    w_out_all = gather_pairs(w_out_near, w_out_far)
    heads_all = [attended, heads_near, heads_far, heads_both]
    output_mine = jnp.concatenate([output_own, output_near, output_far, output_both])
    output_other = exchange(output_mine, "expert", 1)
    router_rows = jnp.pad(jnp.transpose(w_router), ((0, LANES - experts_all), (0, 0)))
    part_shapes = (shaped((span, model_width), wide),) + (
        shaped((span, model_width), low),
    ) * (tensor_count - 1)
    residual_all, inverse_all, normed_two, gates = pl.pallas_call(
        branch_kernel,
        out_shape=(
            shaped((token_count, model_width), wide),
            shaped((token_count, 1), wide),
            shaped((token_count, model_width), low),
            shaped((token_count, LANES), wide),
        ),
        in_specs=in_smem(1) + in_vmem(7),
        out_specs=tuple(in_vmem(4)),
        scratch_shapes=[pltpu.VMEM((model_width, model_width), low)],
        compiler_params=pltpu.CompilerParams(vmem_limit_bytes=12 * mib),
        name="branch",
    )(
        place,
        gain_ffn[None],
        router_rows,
        routes,
        layer_in,
        output_mine,
        output_other,
        jnp.concatenate(heads_all, 1),
    )
    middle = pl.pallas_call(
        functools.partial(middle_kernel, tensor_count),
        out_shape=part_shapes
        + (
            shaped((span, model_width), wide),
            shaped((span, 1), wide),
            shaped((token_count, experts_all * units), low),
            shaped((token_count, experts_all * 2 * units), low),
            shaped((1, model_width), wide),
            shaped((experts_all, model_width), wide),
        ),
        in_specs=in_smem(1) + in_vmem(14),
        out_specs=tuple(in_vmem(tensor_count + 6)),
        scratch_shapes=[
            pltpu.VMEM((token_count, units), wide),
            pltpu.VMEM((token_count, units), low),
            pltpu.VMEM((token_count, 2 * units), wide),
            pltpu.VMEM((token_count, experts_all * units), wide),
            pltpu.VMEM((token_count, model_width), wide),
        ],
        compiler_params=pltpu.CompilerParams(vmem_limit_bytes=24 * mib),
        name="middle",
    )(
        place,
        router_rows,
        out_grad,
        residual_all,
        inverse_all,
        normed_two,
        gates,
        *w_in_all,
        *w_out_all,
    )
    normed_parts, middle = middle[:tensor_count], middle[tensor_count:]
    residual, inverse_two, active, pre_grad, gain_ffn_part, router_part = middle

    relayed = exchange(normed_parts[3], "tensor", 1)
    half_grads = shaped((experts_all // 2 * 3 * units, model_width), low)
    late = pl.pallas_call(
        functools.partial(weight_grad_kernel, tensor_count),
        out_shape=part_shapes + (half_grads,) * 2,
        in_specs=in_smem(1) + in_vmem(8),
        out_specs=tuple(in_vmem(tensor_count + 2)),
        scratch_shapes=[pltpu.VMEM((token_count, model_width), wide)],
        compiler_params=pltpu.CompilerParams(vmem_limit_bytes=16 * mib),
        name="weight_grad",
    )(place, normed_two, out_grad, active, pre_grad, *w_out_all)
    late, relayed = lax.optimization_barrier((late, relayed))
    normed_pieces = scatter_parts(normed_parts, relayed)
    mixture_parts, kept_grads, given_grads = late[:tensor_count], late[-2], late[-1]
    given_grads = exchange(given_grads, "expert", 1)

    in_rows, out_rows = experts_all * units // 2, experts_all * units // 4
    in_kept, in_given, out_kept, out_given = pl.pallas_call(
        add_grads_kernel,
        out_shape=(
            shaped((in_rows, model_width), wide),
            shaped((in_rows, model_width), low),
            shaped((out_rows, model_width), wide),
            shaped((out_rows, model_width), low),
        ),
        in_specs=in_vmem(2),
        out_specs=tuple(in_vmem(4)),
        compiler_params=pltpu.CompilerParams(vmem_limit_bytes=16 * mib),
        name="add_grads",
    )(kept_grads, given_grads)
    residual, in_kept, in_given, out_kept, out_given = lax.optimization_barrier(
        (residual, in_kept, in_given, out_kept, out_given)
    )
    residual_grad, low_grad = pl.pallas_call(
        norm_back_kernel,
        out_shape=(shaped((span, model_width), wide), shaped((span, model_width), low)),
        in_specs=in_vmem(7),
        out_specs=tuple(in_vmem(2)),
        compiler_params=pltpu.CompilerParams(vmem_limit_bytes=6 * mib),
        name="norm_back",
    )(
        *normed_pieces,
        residual,
        inverse_two,
        gain_ffn[None],
        token_block(out_grad),
    )
    grad_blocks = gather_blocks(low_grad)

    in_arrived = exchange(in_given, "expert", 4)
    out_arrived = exchange(out_given, "expert", 2)
    mixture_last, *grad_blocks = lax.optimization_barrier((mixture_parts[3], *grad_blocks))
    mixture_relayed = exchange(mixture_last, "tensor", 1)
    fetched = (w_output, queries, pairs, probs, cosine, sine, qkv_flat)
    back = pl.pallas_call(
        functools.partial(attend_back_kernel, tensor_count),
        out_shape=(shaped((2 * span, model_width), wide),)
        + (shaped((2 * span, model_width), low),) * (tensor_count - 2)
        + (shaped((span, model_width), low),)
        + (
            shaped((token_count, model_width), low),
            shaped((token_count, 2 * head_width), low),
        ),
        in_specs=in_smem(1) + in_hbm(6 + 2 * tensor_count),
        out_specs=tuple(in_vmem(tensor_count + 2)),
        scratch_shapes=[
            pltpu.VMEM((token_count, head_width), wide),
            pltpu.VMEM((token_count, LANES), wide),
            pltpu.VMEM((token_count, model_width), wide),
        ]
        + [pltpu.VMEM(each.shape, each.dtype) for each in fetched]
        + [pltpu.SemaphoreType.DMA((len(fetched) + block_count + 2 * tensor_count,))],
        compiler_params=pltpu.CompilerParams(vmem_limit_bytes=58 * mib),
        name="attend_back",
    )(
        place,
        *fetched,
        *grad_blocks,
        *mixture_parts[:-1],
    )
    input_parts, (branch_grad, projected_grad) = (
        back[:tensor_count],
        back[tensor_count:],
    )
    *input_parts, projected_grad, in_arrived, out_arrived, mixture_relayed = (
        lax.optimization_barrier(
            (*input_parts, projected_grad, in_arrived, out_arrived, mixture_relayed)
        )
    )
    in_summed = in_kept + in_arrived.astype(wide)
    out_summed = out_kept + out_arrived.astype(wide)
    in_arrived = exchange(in_summed[in_rows // 2 :].astype(low), "expert", 2)
    out_arrived = exchange(out_summed[out_rows // 2 :].astype(low), "expert", 4)

    relayed = exchange(input_parts[3], "tensor", 1)
    row_count = (model_width + w_output.shape[0] * model_width // (2 * head_width)) // 2
    kept_sums, given_sums = pl.pallas_call(
        attend_grad_kernel,
        out_shape=(
            shaped((row_count, 2 * head_width), wide),
            shaped((row_count, 2 * head_width), low),
        ),
        in_specs=in_smem(1) + in_vmem(5),
        out_specs=tuple(in_vmem(2)),
        scratch_shapes=[pltpu.VMEM((token_count, model_width), low)],
        compiler_params=pltpu.CompilerParams(vmem_limit_bytes=12 * mib),
        name="attend_grad",
    )(place, layer_in, gain_attn[None], projected_grad, attended, branch_grad)
    relayed, kept_sums, given_sums, in_summed, out_summed = lax.optimization_barrier(
        (relayed, kept_sums, given_sums, in_summed, out_summed)
    )
    sums_half = kept_sums + exchange(given_sums, "expert", 1).astype(wide)
    sums = exchange_halves(sums_half.astype(low), (2, 4))
    input_pieces = scatter_parts(input_parts, jnp.concatenate([relayed, mixture_relayed]))
    residual, in_arrived, out_arrived, sums = lax.optimization_barrier(
        (residual, in_arrived, out_arrived, sums)
    )
    w_in_grad = (in_summed[: in_rows // 2] + in_arrived.astype(wide)).reshape(w_in.shape)
    w_out_grad = (out_summed[: out_rows // 2] + out_arrived.astype(wide)).reshape(w_out.shape)
    block = pl.pallas_call(
        finish_kernel,
        out_shape=shaped((2 * span, model_width), low),
        in_specs=in_vmem(7),
        out_specs=in_vmem(1)[0],
        compiler_params=pltpu.CompilerParams(vmem_limit_bytes=6 * mib),
        name="finish",
    )(
        *input_pieces,
        token_block(layer_in),
        gain_attn[None],
        residual_grad,
        residual,
    )
    far = exchange(block, "tensor", 2)
    near = exchange(block, "tensor", 1)
    small = jnp.concatenate([router_part, gain_ffn_part])
    sums, small, _ = lax.optimization_barrier((sums, small, block))
    small = sum_over_experts(small)
    summed = join_cores(exchange_halves(sums, (4, 2)))
    qkv_summed = summed[:model_width].reshape(w_qkv.shape)
    output_summed = jnp.concatenate(split_blocks(summed[model_width:], 0, 2), 1)

    gain_part = jnp.sum(
        qkv_flat.astype(wide) * summed[:model_width], 1
    ) / gain_attn
    small = jnp.concatenate([small, gain_part[None]])
    far, near, small, summed = lax.optimization_barrier((far, near, small, summed))
    for bit in (1, 2):
        small = small + exchange(small, "tensor", bit)
    blocks = [block, near, far, exchange(far, "tensor", 1)]
    layer_here = in_order([block[:span] for block in blocks])
    in_here = in_order([block[span:] for block in blocks])
    return (
        layer_here,
        in_here,
        small[experts_all + 1],
        qkv_summed,
        output_summed,
        small[experts_all],
        jnp.transpose(small[:experts_all]),
        w_in_grad,
        w_out_grad,
    )


def solution(mesh):
    fits = mesh.shape["tensor"] == 4 and mesh.shape["expert"] == 8
    placed = (
        P("expert", None),
        P("expert", None),
        P("expert", None),
        P(),
        P(None, "tensor", None),
        P("tensor", None),
        P(),
        P(),
        P("expert", None, "tensor", None),
        P("expert", "tensor", None),
        P("expert", None),
    )
    return jax.shard_map(
        on_device if fits else on_device_general,
        mesh=mesh,
        in_specs=placed,
        out_specs=(
            P("expert", None),
            P("expert", None),
            P(),
            P(None, "tensor", None),
            P("tensor", None),
            P(),
            P(),
            P("expert", None, "tensor", None),
            P("expert", "tensor", None),
        ),
        check_vma=False,
    )
```

```python
import functools
import math

import jax
import jax.numpy as jnp
import numpy as np
from jax import lax
from jax.experimental import pallas as pl
from jax.experimental.pallas import tpu as pltpu
from jax.sharding import PartitionSpec as P

HEADS = 16
KV_HEADS = 8
HEAD_DIM = 64


epsilon = 1e-06
rope_base = 10000.0
masked_out = -1e30


def rms_forward(values, gain_vec):
    inverse = lax.rsqrt(jnp.mean(values * values, axis=-1, keepdims=True) + epsilon)
    return (values * inverse * gain_vec, inverse)


def rms_backward(values, inverse, gain_vec, upstream):
    normal = values * inverse
    scaled = upstream * gain_vec
    inner_mean = jnp.mean(scaled * normal, axis=-1, keepdims=True)
    return inverse * (scaled - normal * inner_mean)


def positions(lengths, token_count):
    seq_ends = jnp.cumsum(lengths, dtype=jnp.int32)
    row_index = jnp.arange(token_count, dtype=jnp.int32)
    segment = jnp.sum(
        (row_index[:, None] >= seq_ends[None, :]).astype(jnp.int32), axis=1, dtype=jnp.int32
    )
    seq_ids = jnp.arange(lengths.shape[0], dtype=jnp.int32)
    seq_start = jnp.sum(
        jnp.where(segment[:, None] == seq_ids[None, :], (seq_ends - lengths)[None, :], 0),
        axis=1,
        dtype=jnp.int32,
    )
    return (segment, row_index - seq_start)


def rope_tables(position, head_dim):
    half_dim = head_dim // 2
    inverse_freq = jnp.exp(
        jnp.arange(half_dim, dtype=jnp.float32) * (-2.0 * math.log(rope_base) / head_dim)
    )
    angles = position.astype(jnp.float32)[:, None] * inverse_freq[None, :]
    cosine = jnp.cos(angles)
    sine_tab = jnp.sin(angles)
    return (jnp.concatenate([cosine, cosine], 1), jnp.concatenate([sine_tab, sine_tab], 1))


def rotate(values, cosine, sine_tab):
    half_dim = values.shape[-1] // 2
    turned = jnp.concatenate([-values[..., half_dim:], values[..., :half_dim]], -1)
    return values * cosine + turned * sine_tab


def split_blocks(array_in, axis_at, block_count):
    dims_now = array_in.shape
    regrouped = array_in.reshape(
        dims_now[:axis_at]
        + (block_count, dims_now[axis_at] // block_count)
        + dims_now[axis_at + 1 :]
    )
    return jnp.moveaxis(regrouped, axis_at, 0)


def join_blocks(array_in, axis_at):
    regrouped = jnp.moveaxis(array_in, 0, axis_at)
    dims_now = regrouped.shape
    return regrouped.reshape(
        dims_now[:axis_at] + (dims_now[axis_at] * dims_now[axis_at + 1],) + dims_now[axis_at + 2 :]
    )


def block_scores(query_block, key_rows, segment_rows, row_start, segment, scaling):
    block_rows = query_block.shape[2]
    scores_raw = (
        jnp.einsum("kgbd,ksd->kgbs", query_block, key_rows, preferred_element_type=jnp.float32)
        * scaling
    )
    query_index = row_start + jnp.arange(block_rows, dtype=jnp.int32)
    key_index = jnp.arange(key_rows.shape[1], dtype=jnp.int32)
    allowed = (segment_rows[:, None] == segment[None, :]) & (
        key_index[None, :] <= query_index[:, None]
    )
    return jnp.where(allowed[None, None], scores_raw, masked_out)


def attention_forward(queries, key_rows, values, segment, scaling, block_size):
    block_count = queries.shape[2] // block_size
    starts_all = jnp.arange(block_count, dtype=jnp.int32) * block_size

    def one_block(packed):
        query_block, segment_rows, row_start = packed
        scores = block_scores(query_block, key_rows, segment_rows, row_start, segment, scaling)
        top_score = jnp.max(scores, -1)
        exponent = jnp.exp(scores - top_score[..., None])
        row_total = jnp.sum(exponent, -1)
        probs = (exponent / row_total[..., None]).astype(jnp.bfloat16)
        output = jnp.einsum("kgbs,ksd->kgbd", probs, values, preferred_element_type=jnp.float32)
        return (output.astype(jnp.bfloat16), top_score, row_total)

    outputs, top_blocks, total_blocks = lax.map(
        one_block,
        (
            split_blocks(queries, 2, block_count),
            segment.reshape(block_count, block_size),
            starts_all,
        ),
    )
    return (join_blocks(outputs, 2), join_blocks(top_blocks, 2), join_blocks(total_blocks, 2))


def attention_backward(
    queries, key_rows, values, heads_grad, segment, top_kept, total_kept, scaling, block_size
):
    block_count = queries.shape[2] // block_size
    starts_all = jnp.arange(block_count, dtype=jnp.int32) * block_size

    def one_block(running, packed):
        key_acc, value_acc = running
        query_block, grad_block, segment_rows, row_start, top_block, total_block = packed
        scores = block_scores(query_block, key_rows, segment_rows, row_start, segment, scaling)
        probs = jnp.exp(scores - top_block[..., None]) / total_block[..., None]
        probs_low = probs.astype(jnp.bfloat16)
        value_acc = value_acc + jnp.einsum(
            "kgbs,kgbd->ksd", probs_low, grad_block, preferred_element_type=jnp.float32
        )
        prob_grad = jnp.einsum(
            "kgbd,ksd->kgbs", grad_block, values, preferred_element_type=jnp.float32
        )
        inner_sum = jnp.sum(probs * prob_grad, -1, keepdims=True)
        score_grad = (probs * (prob_grad - inner_sum)).astype(jnp.bfloat16)
        query_grad = (
            jnp.einsum("kgbs,ksd->kgbd", score_grad, key_rows, preferred_element_type=jnp.float32)
            * scaling
        )
        key_acc = (
            key_acc
            + jnp.einsum(
                "kgbs,kgbd->ksd", score_grad, query_block, preferred_element_type=jnp.float32
            )
            * scaling
        )
        return ((key_acc, value_acc), query_grad)

    empty = jnp.zeros(key_rows.shape, jnp.float32)
    packed_all = (
        split_blocks(queries, 2, block_count),
        split_blocks(heads_grad, 2, block_count),
        segment.reshape(block_count, block_size),
        starts_all,
        split_blocks(top_kept, 2, block_count),
        split_blocks(total_kept, 2, block_count),
    )
    (key_grad, value_grad), query_blocks = lax.scan(one_block, (empty, empty), packed_all)
    return (join_blocks(query_blocks, 2), key_grad, value_grad)


def on_device_general(
    layer_in,
    seq_lengths,
    routes,
    gain_attn,
    w_qkv,
    w_output,
    gain_ffn,
    w_router,
    w_in,
    w_out,
    out_grad,
):
    token_count, model_width = layer_in.shape
    kv_here = w_qkv.shape[1]
    group_size = HEADS // KV_HEADS
    scaling = 1.0 / math.sqrt(HEAD_DIM)
    block_size = min(512, token_count)
    w_output_all = lax.all_gather(w_output, "tensor", axis=0, tiled=True)
    w_gate_all = lax.all_gather(w_in[0, 0], "expert", axis=0, tiled=True)
    w_up_all = lax.all_gather(w_in[0, 1], "expert", axis=0, tiled=True)
    w_out_all = lax.all_gather(w_out[0], "expert", axis=0, tiled=True)
    segment, position = positions(seq_lengths[0], token_count)
    cosine, sine_tab = rope_tables(position, HEAD_DIM)
    inputs = layer_in.astype(jnp.float32)
    normed_one, inverse_one = rms_forward(inputs, gain_attn)
    normed_one_low = normed_one.astype(jnp.bfloat16)
    qkv_flat = w_qkv.reshape(model_width, -1)
    projected = jnp.dot(normed_one_low, qkv_flat, preferred_element_type=jnp.float32)
    projected = projected.reshape(token_count, kv_here, group_size + 2, HEAD_DIM)
    queries = rotate(
        jnp.transpose(projected[:, :, :group_size], (1, 2, 0, 3)), cosine, sine_tab
    ).astype(jnp.bfloat16)
    key_rows = rotate(
        jnp.transpose(projected[:, :, group_size], (1, 0, 2)), cosine, sine_tab
    ).astype(jnp.bfloat16)
    values = jnp.transpose(projected[:, :, group_size + 1], (1, 0, 2)).astype(jnp.bfloat16)
    attended, top_kept, total_kept = attention_forward(
        queries, key_rows, values, segment, scaling, block_size
    )
    heads_out = jnp.transpose(attended, (2, 0, 1, 3)).reshape(token_count, -1)
    heads_all = lax.all_gather(heads_out, "tensor", axis=1, tiled=True)
    branch_here = jnp.dot(heads_all, w_output_all, preferred_element_type=jnp.float32)
    residual = inputs + branch_here
    normed_two, inverse_two = rms_forward(residual, gain_ffn)
    normed_low = normed_two.astype(jnp.bfloat16)
    experts_all = w_router.shape[1]
    unit_count = w_out.shape[1]
    logits = jnp.dot(normed_low, w_router, preferred_element_type=jnp.float32)
    expert_ids = jnp.arange(experts_all, dtype=jnp.int32)
    picked = jnp.any(routes[:, :, None] == expert_ids[None, None, :], axis=1)
    picked_logits = jnp.where(picked, logits, masked_out)
    top_logit = jnp.max(picked_logits, -1, keepdims=True)
    weight = jnp.where(picked, jnp.exp(picked_logits - top_logit), 0.0)
    gates = weight / jnp.sum(weight, -1, keepdims=True)

    def by_unit(per_expert):
        return jnp.broadcast_to(
            per_expert[:, :, None], (token_count, experts_all, unit_count)
        ).reshape(token_count, -1)

    def over_units(per_unit):
        return jnp.sum(per_unit.reshape(token_count, experts_all, unit_count), -1)

    def times_transposed(left, right):
        return lax.dot_general(
            left, right, (((1,), (1,)), ((), ())), preferred_element_type=jnp.float32
        )

    def transposed_times(left, right):
        return lax.dot_general(
            left, right, (((0,), (0,)), ((), ())), preferred_element_type=jnp.float32
        )

    gates_wide = by_unit(gates)
    gate_vals = times_transposed(normed_low, w_gate_all)
    up_vals = times_transposed(normed_low, w_up_all)
    plain_grad = times_transposed(out_grad, w_out_all)
    sig_vals = jax.nn.sigmoid(gate_vals)
    silu_vals = gate_vals * sig_vals
    active = silu_vals * up_vals
    scaled_active = (active * gates_wide).astype(jnp.bfloat16)
    active_grad = plain_grad * gates_wide
    gate_pre = (
        active_grad * up_vals * (sig_vals * (1.0 + gate_vals * (1.0 - sig_vals)))
    ).astype(jnp.bfloat16)
    up_pre = (active_grad * silu_vals).astype(jnp.bfloat16)
    gate_grad_part = over_units(active * plain_grad)
    logit_part = (
        gates * (gate_grad_part - jnp.sum(gates * gate_grad_part, -1, keepdims=True))
    ).astype(jnp.bfloat16)
    normed_two_part = (
        jnp.dot(gate_pre, w_gate_all, preferred_element_type=jnp.float32)
        + jnp.dot(up_pre, w_up_all, preferred_element_type=jnp.float32)
        + times_transposed(logit_part, w_router)
    )
    normed_two_grad = lax.psum(normed_two_part.astype(jnp.bfloat16), "tensor").astype(jnp.float32)
    mixture_part = jnp.dot(scaled_active, w_out_all, preferred_element_type=jnp.float32)
    mixture = lax.psum(mixture_part.astype(jnp.bfloat16), "tensor").astype(jnp.float32)
    layer_here = (residual + mixture).astype(jnp.bfloat16)

    def to_owner(partial):
        return lax.psum_scatter(
            partial.astype(jnp.bfloat16), "expert", scatter_dimension=0, tiled=True
        ).astype(jnp.float32)

    w_gate_grad = to_owner(transposed_times(gate_pre, normed_low))
    w_up_grad = to_owner(transposed_times(up_pre, normed_low))
    w_in_grad = jnp.stack([w_gate_grad, w_up_grad])[None]
    w_out_grad = to_owner(transposed_times(scaled_active, out_grad))[None]
    router_part = transposed_times(logit_part, normed_low)
    normal_two = residual * inverse_two
    gain_ffn_part = jnp.sum(normed_two_part * normal_two, axis=0)
    upstream = out_grad.astype(jnp.float32)
    residual_part = rms_backward(residual, inverse_two, gain_ffn, normed_two_grad)
    residual_grad = upstream + residual_part
    branch_here_grad = residual_grad.astype(jnp.bfloat16)
    w_output_grad = lax.dot_general(
        heads_out, branch_here_grad, (((0,), (0,)), ((), ())), preferred_element_type=jnp.float32
    )
    heads_flat = lax.dot_general(
        branch_here_grad, w_output, (((1,), (1,)), ((), ())), preferred_element_type=jnp.float32
    ).astype(jnp.bfloat16)
    heads_grad = jnp.transpose(
        heads_flat.reshape(token_count, kv_here, group_size, HEAD_DIM), (1, 2, 0, 3)
    )
    query_grad, key_grad, value_grad = attention_backward(
        queries, key_rows, values, heads_grad, segment, top_kept, total_kept, scaling, block_size
    )
    query_grad = rotate(query_grad, cosine, -sine_tab)
    key_grad = rotate(key_grad, cosine, -sine_tab)
    projected_grad = jnp.concatenate(
        [
            jnp.transpose(query_grad, (2, 0, 1, 3)),
            jnp.transpose(key_grad, (1, 0, 2))[:, :, None],
            jnp.transpose(value_grad, (1, 0, 2))[:, :, None],
        ],
        2,
    )
    projected_grad = projected_grad.reshape(token_count, -1).astype(jnp.bfloat16)
    w_qkv_grad = lax.dot_general(
        normed_one_low, projected_grad, (((0,), (0,)), ((), ())), preferred_element_type=jnp.float32
    ).reshape(w_qkv.shape)
    normed_one_part = lax.dot_general(
        projected_grad, qkv_flat, (((1,), (1,)), ((), ())), preferred_element_type=jnp.float32
    )
    gain_attn_part = jnp.sum(normed_one_part * (inputs * inverse_one), axis=0)
    normed_one_grad = lax.psum(normed_one_part.astype(jnp.bfloat16), "tensor").astype(jnp.float32)
    input_part = rms_backward(inputs, inverse_one, gain_attn, normed_one_grad)
    in_here = (residual_grad + input_part).astype(jnp.bfloat16)
    qkv_summed = lax.psum(w_qkv_grad.astype(jnp.bfloat16), "expert").astype(jnp.float32)
    output_summed = lax.psum(w_output_grad.astype(jnp.bfloat16), "expert").astype(jnp.float32)
    small = jnp.concatenate([router_part, gain_ffn_part[None], gain_attn_part[None]])
    small = lax.psum(small, ("expert", "tensor"))
    return (
        layer_here,
        in_here,
        small[experts_all + 1],
        qkv_summed,
        output_summed,
        small[experts_all],
        jnp.transpose(small[:experts_all]),
        w_in_grad,
        w_out_grad,
    )


LANES = 128
ROWS = 128
IN_ORDER = (0, 2, 4, 6, 1, 3, 5, 7)
OUT_ORDER = (0, 4, 2, 6, 1, 5, 3, 7)


def exchange(array_in, axis_name, bits):
    count = lax.axis_size(axis_name)
    return lax.ppermute(array_in, axis_name, [(i, i ^ bits) for i in range(count)])


def gather_blocks(own):
    far = exchange(own, "tensor", 2)
    near = exchange(own, "tensor", 1)
    far, near = lax.optimization_barrier((far, near))
    return [own, near, far, exchange(far, "tensor", 1)]


def scatter_parts(parts, relayed):
    near, far, relayed = lax.optimization_barrier((parts[1], parts[2], relayed))
    far = (far.astype(jnp.float32) + relayed.astype(jnp.float32)).astype(jnp.bfloat16)
    far = exchange(far, "tensor", 2)
    return parts[0], exchange(near, "tensor", 1), far


def gather_pairs(near, far):
    return [near, far, exchange(near, "expert", 1), exchange(far, "expert", 1)]


def exchange_halves(array_in, bits):
    rows = array_in.shape[0] // 2
    halves = []
    for half, bit in zip((array_in[:rows], array_in[rows:]), bits):
        arrived = exchange(half, "expert", bit)
        halves.append((half.astype(jnp.float32) + arrived.astype(jnp.float32)).astype(jnp.bfloat16))
    return jnp.concatenate(halves)


def join_cores(half):
    core = lax.axis_index("expert") & 1
    other = exchange(half, "expert", 1)
    return jnp.concatenate(
        [jnp.where(core == 0, half, other), jnp.where(core == 0, other, half)]
    ).astype(jnp.float32)


def sum_over_experts(array_in):
    for bit in (1, 2, 4):
        array_in = array_in + exchange(array_in, "expert", bit)
    return array_in


def dot_plain(left, right):
    return jnp.dot(left, right, preferred_element_type=jnp.float32)


def dot_transposed(left, right):
    return lax.dot_general(
        left, right, (((1,), (1,)), ((), ())), preferred_element_type=jnp.float32
    )


def transposed_dot(left, right):
    return lax.dot_general(
        left, right, (((0,), (0,)), ((), ())), preferred_element_type=jnp.float32
    )


def lane_index(shape):
    return lax.broadcasted_iota(jnp.int32, shape, 1)


def turn(values):
    low_half = (lane_index(values.shape) & (HEAD_DIM - 1)) < HEAD_DIM // 2
    return jnp.where(
        low_half,
        -pltpu.roll(values, LANES - HEAD_DIM // 2, 1),
        pltpu.roll(values, HEAD_DIM // 2, 1),
    )


def swap_heads(values):
    return pltpu.roll(values, HEAD_DIM, 1)


def first_head(shape):
    return lane_index(shape) < HEAD_DIM


def angle_tables(token_count):
    half_dim = HEAD_DIM // 2
    inverse_freq = np.exp(np.arange(half_dim) * (-2.0 * math.log(rope_base) / HEAD_DIM))
    angles = np.arange(token_count)[:, None] * inverse_freq[None, :]
    tile = LANES // half_dim
    return (
        np.tile(np.cos(angles), (1, tile)).astype(np.float32),
        np.tile(np.sin(angles), (1, tile)).astype(np.float32),
    )


def attend_kernel(
    lengths,
    layer_in,
    gain,
    w_qkv,
    cosine,
    sine,
    queries_out,
    pairs_out,
    probs_out,
    attended,
    normed,
    queries,
    pairs,
    probs,
    sems,
):
    token_count = layer_in.shape[0]
    kv_here = pairs.shape[0]
    for row in range(0, token_count, ROWS):
        rows = pl.ds(row, ROWS)
        values = layer_in[rows, :].astype(jnp.float32)
        scale = lax.rsqrt(jnp.mean(values * values, axis=-1, keepdims=True) + epsilon)
        normed[rows, :] = (values * scale * gain[...]).astype(jnp.bfloat16)
    is_first = first_head((ROWS, LANES))
    for kv in range(kv_here):
        projected = dot_plain(normed[...], w_qkv[:, 2 * LANES * kv : 2 * LANES * (kv + 1)])
        for block in range(token_count // ROWS):
            rows = pl.ds(block * ROWS, ROWS)
            cos_rows, sin_rows = cosine[rows, :], sine[rows, :]
            query = projected[block * ROWS : (block + 1) * ROWS, :LANES]
            query = (query * cos_rows + turn(query) * sin_rows) * (1.0 / math.sqrt(HEAD_DIM))
            queries[kv, block, :ROWS, :] = jnp.where(is_first, query, 0.0).astype(jnp.bfloat16)
            queries[kv, block, ROWS:, :] = jnp.where(is_first, swap_heads(query), 0.0).astype(
                jnp.bfloat16
            )
            pair = projected[block * ROWS : (block + 1) * ROWS, LANES:]
            pairs[kv, rows, :] = jnp.where(
                is_first, pair * cos_rows + turn(pair) * sin_rows, pair
            ).astype(jnp.bfloat16)
    copies = [
        pltpu.make_async_copy(queries, queries_out, sems.at[0]),
        pltpu.make_async_copy(pairs, pairs_out, sems.at[1]),
    ]
    for copy in copies:
        copy.start()
    for block in range(token_count // ROWS):
        keys = (block + 1) * ROWS
        token = block * ROWS + (
            lax.broadcasted_iota(jnp.int32, (2 * ROWS, keys), 0) & (ROWS - 1)
        )
        start = jnp.zeros_like(token)
        end = 0
        for seq in range(lengths.shape[1] - 1):
            end = end + lengths[0, seq]
            start = jnp.where(token >= end, end, start)
        key = lane_index((2 * ROWS, keys))
        allowed = (key <= token) & (key >= start)
        for kv in range(kv_here):
            scores = dot_transposed(queries[kv, block], pairs[kv, :keys, :])
            scores = jnp.where(allowed, scores, masked_out)
            exponent = jnp.exp(scores - jnp.max(scores, -1, keepdims=True))
            share = (exponent * (1.0 / jnp.sum(exponent, -1, keepdims=True))).astype(jnp.bfloat16)
            probs[kv, block, :, :keys] = share
            output = dot_plain(share, pairs[kv, :keys, :])
            attended[pl.ds(block * ROWS, ROWS), kv * LANES : (kv + 1) * LANES] = jnp.where(
                is_first, swap_heads(output[:ROWS]), output[ROWS:]
            ).astype(jnp.bfloat16)
        copies.append(
            pltpu.make_async_copy(
                probs.at[:, block, :, :keys], probs_out.at[:, block, :, :keys], sems.at[2 + block]
            )
        )
        copies[-1].start()
    for copy in copies:
        copy.wait()


def write_parts(place, total, parts, span):
    for number, part in enumerate(parts):
        row = pl.multiple_of((place[0] ^ number) * span, span)
        part[...] = total[pl.ds(row, span), :].astype(part.dtype)


def branch_kernel(
    place,
    gain,
    router,
    routes,
    layer_in,
    w_mine,
    w_other,
    heads,
    residual,
    inverse,
    normed,
    gates,
    w_output,
):
    token_count, model_width = layer_in.shape
    half = LANES
    mine = (place[1] & 1) * half
    for row in range(0, model_width, 2 * half):
        rows = pl.ds(row // 2, half)
        w_output[pl.ds(pl.multiple_of(row + mine, half), half), :] = w_mine[rows, :]
        w_output[pl.ds(pl.multiple_of(row + half - mine, half), half), :] = w_other[rows, :]

    def branch_step(number, carry):
        columns = pl.ds(pl.multiple_of(number * 2 * LANES, 2 * LANES), 2 * LANES)
        residual[:, columns] = layer_in[:, columns].astype(jnp.float32) + dot_plain(
            heads[...], w_output[:, columns]
        )
        return carry

    lax.fori_loop(0, model_width // (2 * LANES), branch_step, 0)
    for row in range(0, token_count, ROWS):
        rows = pl.ds(row, ROWS)
        values = residual[rows, :]
        scale = lax.rsqrt(jnp.mean(values * values, axis=-1, keepdims=True) + epsilon)
        inverse[rows, :] = scale
        normed[rows, :] = (values * scale * gain[...]).astype(jnp.bfloat16)
    gates[...] = dot_transposed(normed[...], router[...])
    lane = lane_index((ROWS, LANES))
    for row in range(0, token_count, ROWS):
        rows = pl.ds(row, ROWS)
        picked = routes[rows, 0:1] == lane
        for top in range(1, routes.shape[1]):
            picked = picked | (routes[rows, top : top + 1] == lane)
        logits = jnp.where(picked, gates[rows, :], masked_out)
        weight = jnp.where(picked, jnp.exp(logits - jnp.max(logits, -1, keepdims=True)), 0.0)
        gates[rows, :] = weight / jnp.sum(weight, -1, keepdims=True)


def middle_kernel(tensor_count, *refs):
    place, router, out_grad, residual, inverse, normed, gates = refs[:7]
    w_ins, w_outs, refs = refs[7:11], refs[11:15], refs[15:]
    parts, refs = refs[:tensor_count], refs[tensor_count:]
    (residual_block, inverse_block, active_out, pre_out, gain_part, router_part) = refs[:6]
    (gate_wide, product, hidden, plain, total) = refs[6:]
    token_count, model_width = normed.shape
    experts_all = router_part.shape[0]
    units = w_outs[0].shape[0] // 2
    span = token_count // tensor_count
    for pair, weights in enumerate(w_outs):
        plain[:, 2 * pair * units : 2 * (pair + 1) * units] = dot_transposed(
            out_grad[...], weights[...]
        )
    gates_high = gates[...].astype(jnp.bfloat16)
    gates_low = (gates[...] - gates_high.astype(jnp.float32)).astype(jnp.bfloat16)
    total_grad = jnp.zeros((token_count, LANES), jnp.float32)
    for number in range(experts_all):
        name = place[1] ^ IN_ORDER[number]
        in_rows = pl.ds(number % 2 * 2 * units, 2 * units)
        out_number = OUT_ORDER.index(IN_ORDER[number])
        hidden[...] = dot_transposed(normed[...], w_ins[number // 2][in_rows, :])
        out_lanes = pl.ds(out_number * units, units)
        chosen = lax.broadcasted_iota(jnp.int32, (LANES, units), 0) == name
        chosen = jnp.where(chosen, 1.0, 0.0).astype(jnp.bfloat16)
        gate_wide[...] = dot_plain(gates_high, chosen) + dot_plain(gates_low, chosen)
        for row in range(0, token_count, ROWS):
            rows = pl.ds(row, ROWS)
            gate = gate_wide[rows, :]
            gate_vals, up_vals = hidden[rows, :units], hidden[rows, units:]
            sig_vals = 0.5 + 0.5 * jnp.tanh(0.5 * gate_vals)
            silu_vals = gate_vals * sig_vals
            active = silu_vals * up_vals
            grad = plain[rows, out_lanes]
            product[rows, :] = (active * grad).astype(jnp.bfloat16)
            active_grad = grad * gate
            active_out[rows, out_number * units : (out_number + 1) * units] = (
                active * gate
            ).astype(jnp.bfloat16)
            pre_out[rows, 2 * number * units : (2 * number + 1) * units] = (
                active_grad * up_vals * (sig_vals * (1.0 + gate_vals * (1.0 - sig_vals)))
            ).astype(jnp.bfloat16)
            pre_out[rows, (2 * number + 1) * units : (2 * number + 2) * units] = (
                active_grad * silu_vals
            ).astype(jnp.bfloat16)
        total_grad = total_grad + dot_transposed(product[...], chosen)
    gate_all, grad_all = gates[...], total_grad
    logit_part = (
        gate_all * (grad_all - jnp.sum(gate_all * grad_all, -1, keepdims=True))
    ).astype(jnp.bfloat16)
    router_part[...] = transposed_dot(logit_part, normed[...])[:experts_all]

    def column_step(number, carry):
        columns = pl.ds(pl.multiple_of(number * 2 * LANES, 2 * LANES), 2 * LANES)
        summed = dot_plain(logit_part, router[:, columns])
        for pair, weights in enumerate(w_ins):
            pre = pre_out[:, 4 * pair * units : 4 * (pair + 1) * units]
            summed = summed + dot_plain(pre, weights[:, columns])
        total[:, columns] = summed
        return carry

    lax.fori_loop(0, model_width // (2 * LANES), column_step, 0)
    write_parts(place, total, parts, span)
    row = pl.ds(pl.multiple_of(place[0] * span, span), span)
    residual_block[...] = residual[row, :]
    inverse_block[...] = inverse[row, :]
    gain_sum = jnp.zeros((1, model_width), jnp.float32)
    for row in range(0, token_count, ROWS):
        rows = pl.ds(row, ROWS)
        gain_sum = gain_sum + jnp.sum(
            total[rows, :] * (residual[rows, :] * inverse[rows, :]), 0, keepdims=True
        )
    gain_part[...] = gain_sum


def weight_grad_kernel(tensor_count, *refs):
    place, normed, out_grad, active, pre_grad = refs[:5]
    w_outs, parts = refs[5:9], refs[9 : 9 + tensor_count]
    kept, given, total = refs[9 + tensor_count :]
    token_count, model_width = normed.shape
    units = w_outs[0].shape[0] // 2
    experts_all = 2 * kept.shape[0] // (3 * units)

    def column_step(number, carry):
        columns = pl.ds(pl.multiple_of(number * 2 * LANES, 2 * LANES), 2 * LANES)
        summed = jnp.zeros((token_count, 2 * LANES), jnp.float32)
        for pair, weights in enumerate(w_outs):
            summed = summed + dot_plain(
                active[:, 2 * pair * units : 2 * (pair + 1) * units], weights[:, columns]
            )
        total[:, columns] = summed
        return carry

    lax.fori_loop(0, model_width // (2 * LANES), column_step, 0)
    write_parts(place, total, parts, token_count // tensor_count)
    for number in range(experts_all):
        out_number = OUT_ORDER.index(IN_ORDER[number])
        grads = kept if number < experts_all // 2 else given
        in_row = number % (experts_all // 2) * 2 * units
        out_row = experts_all * units + out_number % (experts_all // 2) * units
        grads[pl.ds(in_row, 2 * units), :] = transposed_dot(
            pre_grad[:, 2 * number * units : 2 * (number + 1) * units], normed[...]
        ).astype(jnp.bfloat16)
        grads[pl.ds(out_row, units), :] = transposed_dot(
            active[:, out_number * units : (out_number + 1) * units], out_grad[...]
        ).astype(jnp.bfloat16)


def add_grads_kernel(kept, given, in_kept, in_given, out_kept, out_given):
    row = 0
    for target in (in_kept, in_given, out_kept, out_given):
        rows = pl.ds(row, target.shape[0])
        summed = kept[rows, :].astype(jnp.float32) + given[rows, :].astype(jnp.float32)
        target[...] = summed.astype(target.dtype)
        row += target.shape[0]


def attend_back_kernel(tensor_count, *refs):
    place, far_refs, refs = refs[0], refs[1:8], refs[8:]
    blocks, refs = refs[:tensor_count], refs[tensor_count:]
    mixtures, refs = refs[: tensor_count - 1], refs[tensor_count - 1 :]
    parts, refs = refs[:tensor_count], refs[tensor_count:]
    branch_grad, projected_grad, heads_grad, pair_grad, total = refs[:5]
    near_refs, sems = refs[5:12], refs[12]
    w_output, queries, pairs, probs, cosine, sine, w_qkv = near_refs
    copies, prob_copies = [], []
    for number, (source, target) in enumerate(zip(far_refs, near_refs)):
        if target is probs:
            for block in range(probs.shape[1]):
                part = (slice(None), block, slice(None), slice((block + 1) * ROWS))
                prob_copies.append(
                    pltpu.make_async_copy(
                        source.at[part], target.at[part], sems.at[len(near_refs) + block]
                    )
                )
        else:
            copies.append(pltpu.make_async_copy(source, target, sems.at[number]))
    more = len(near_refs) + len(prob_copies)
    token_count, model_width = branch_grad.shape
    span = token_count // tensor_count
    mixture_copies = [
        pltpu.make_async_copy(mixture, part.at[pl.ds(span, span)], sems.at[more + number])
        for number, (mixture, part) in enumerate(zip(mixtures, parts[:-1]))
    ]
    block_copies = []
    for number, block in enumerate(blocks):
        row = pl.multiple_of((place[0] ^ number) * span, span)
        block_copies.append(
            pltpu.make_async_copy(
                block,
                branch_grad.at[pl.ds(row, span)],
                sems.at[more + tensor_count + number],
            )
        )
    for copy in block_copies + copies[:5] + prob_copies + copies[5:] + mixture_copies:
        copy.start()
    for copy in copies[:1] + block_copies:
        copy.wait()
    heads_grad[...] = dot_transposed(branch_grad[...], w_output[...])
    for copy in copies[1:5]:
        copy.wait()
    is_first = first_head((ROWS, LANES))
    for kv in range(pairs.shape[0]):
        pair_grad[...] = jnp.zeros_like(pair_grad)
        for block in range(token_count // ROWS):
            keys = (block + 1) * ROWS
            rows = pl.ds(block * ROWS, ROWS)
            upper = heads_grad[rows, kv * LANES : (kv + 1) * LANES]
            upper = jnp.concatenate(
                [
                    jnp.where(is_first, 0.0, swap_heads(upper)),
                    jnp.where(is_first, 0.0, upper),
                ]
            ).astype(jnp.bfloat16)
            if kv == 0:
                prob_copies[block].wait()
            share_low = probs[kv, block, :, :keys]
            share = share_low.astype(jnp.float32)
            prob_grad = dot_transposed(upper, pairs[kv, :keys, :])
            inner = jnp.sum(share * prob_grad, -1, keepdims=True)
            score_grad = (share * (prob_grad - inner)).astype(jnp.bfloat16)
            query_grad = dot_plain(score_grad, pairs[kv, :keys, :])
            query_grad = jnp.where(
                is_first, query_grad[:ROWS], swap_heads(query_grad[ROWS:])
            ) * (1.0 / math.sqrt(HEAD_DIM))
            projected_grad[rows, 2 * kv * LANES : (2 * kv + 1) * LANES] = (
                query_grad * cosine[rows, :] - turn(query_grad) * sine[rows, :]
            ).astype(jnp.bfloat16)
            pair_grad[:keys, :] = (
                pair_grad[:keys, :]
                + transposed_dot(score_grad, queries[kv, block])
                + transposed_dot(share_low, upper)
            )
        for block in range(token_count // ROWS):
            rows = pl.ds(block * ROWS, ROWS)
            grad = pair_grad[rows, :]
            projected_grad[rows, (2 * kv + 1) * LANES : (2 * kv + 2) * LANES] = jnp.where(
                is_first, grad * cosine[rows, :] - turn(grad) * sine[rows, :], grad
            ).astype(jnp.bfloat16)

    for copy in copies[5:]:
        copy.wait()

    def column_step(number, carry):
        columns = pl.ds(pl.multiple_of(number * 2 * LANES, 2 * LANES), 2 * LANES)
        total[:, columns] = dot_transposed(projected_grad[...], w_qkv[columns, :])
        return carry

    lax.fori_loop(0, model_width // (2 * LANES), column_step, 0)
    write_parts(place, total, [part.at[:span] for part in parts[:-1]] + [parts[-1]], span)
    for copy in mixture_copies:
        copy.wait()


def attend_grad_kernel(
    place, layer_in, gain, projected_grad, attended, branch_grad, kept, given, normed
):
    token_count, model_width = layer_in.shape
    for row in range(0, token_count, ROWS):
        rows = pl.ds(row, ROWS)
        values = layer_in[rows, :].astype(jnp.float32)
        scale = lax.rsqrt(jnp.mean(values * values, axis=-1, keepdims=True) + epsilon)
        normed[rows, :] = (values * scale * gain[...]).astype(jnp.bfloat16)
    width = projected_grad.shape[1]
    blocks = []
    for row in range(0, model_width, attended.shape[1]):
        lanes = pl.ds(row, attended.shape[1])
        blocks.append((normed, lanes, projected_grad, pl.ds(0, width)))
    for lane in range(0, model_width, width):
        blocks.append((attended, pl.ds(0, attended.shape[1]), branch_grad, pl.ds(lane, width)))
    half = len(blocks) // 2
    for number, (left, left_lanes, right, right_lanes) in enumerate(blocks):
        rows = pl.ds(number % half * attended.shape[1], attended.shape[1])
        grad = transposed_dot(left[:, left_lanes], right[:, right_lanes])
        mine = (place[1] & 1) == number // half

        @pl.when(mine)
        def _():
            kept[rows, :] = grad

        @pl.when(jnp.logical_not(mine))
        def _():
            given[rows, :] = grad.astype(jnp.bfloat16)


def norm_back_kernel(own, near, far, residual, inverse, gain, out_grad, residual_grad, low_grad):
    summed = own[...] + near[...].astype(jnp.float32) + far[...].astype(jnp.float32)
    total = out_grad[...].astype(jnp.float32) + rms_backward(
        residual[...], inverse[...], gain[...], summed
    )
    residual_grad[...] = total
    low_grad[...] = total.astype(jnp.bfloat16)


def finish_kernel(own, near, far, layer_in, gain, residual_grad, residual, block):
    span = layer_in.shape[0]
    summed = own[...] + near[...].astype(jnp.float32) + far[...].astype(jnp.float32)
    values = layer_in[...].astype(jnp.float32)
    inverse = lax.rsqrt(jnp.mean(values * values, axis=-1, keepdims=True) + epsilon)
    block[:span, :] = (residual[...] + summed[span:]).astype(jnp.bfloat16)
    block[span : 2 * span, :] = (
        residual_grad[...] + rms_backward(values, inverse, gain[...], summed[:span])
    ).astype(jnp.bfloat16)


def in_vmem(count):
    return [pl.BlockSpec(memory_space=pltpu.VMEM)] * count


def in_hbm(count):
    return [pl.BlockSpec(memory_space=pltpu.HBM)] * count


def in_smem(count):
    return [pl.BlockSpec(memory_space=pltpu.SMEM)] * count


def shaped(shape, dtype):
    return jax.ShapeDtypeStruct(shape, dtype)


def on_device(
    layer_in,
    seq_lengths,
    routes,
    gain_attn,
    w_qkv,
    w_output,
    gain_ffn,
    w_router,
    w_in,
    w_out,
    out_grad,
):
    low, wide = jnp.bfloat16, jnp.float32
    token_count, model_width = layer_in.shape
    kv_here = w_qkv.shape[1]
    experts_all = w_router.shape[1]
    units = w_out.shape[1]
    head_width = kv_here * LANES
    block_count = token_count // ROWS
    tensor_count = lax.axis_size("tensor")
    span = token_count // tensor_count
    tensor_here = lax.axis_index("tensor")
    place = jnp.stack([tensor_here, lax.axis_index("expert")]).astype(jnp.int32)
    mib = 1 << 20

    def token_block(array_in):
        return lax.dynamic_slice_in_dim(array_in, tensor_here * span, span, 0)

    def in_order(blocks):
        joined = jnp.zeros((token_count,) + blocks[0].shape[1:], blocks[0].dtype)
        for number, block in enumerate(blocks):
            joined = lax.dynamic_update_slice_in_dim(
                joined, block, (tensor_here ^ number) * span, 0
            )
        return joined

    core = lax.axis_index("expert") & 1
    half = w_output.shape[0] // 2
    output_own = jnp.where(core == 0, w_output[:half], w_output[half:])
    output_far = exchange(output_own, "tensor", 2)
    output_near = exchange(output_own, "tensor", 1)
    w_in_own, w_out_own = w_in.reshape(2 * units, model_width), w_out[0]
    w_in_near = exchange(w_in_own, "expert", 2)
    w_out_near = exchange(w_out_own, "expert", 4)

    cosine, sine = angle_tables(token_count)
    qkv_flat = w_qkv.reshape(model_width, -1)
    kept = (
        shaped((kv_here, block_count, 2 * ROWS, LANES), low),
        shaped((kv_here, token_count, LANES), low),
        shaped((kv_here, block_count, 2 * ROWS, token_count), low),
    )
    queries, pairs, probs, attended = pl.pallas_call(
        attend_kernel,
        out_shape=kept + (shaped((token_count, head_width), low),),
        in_specs=in_smem(1) + in_vmem(5),
        out_specs=tuple(in_hbm(3) + in_vmem(1)),
        scratch_shapes=[pltpu.VMEM((token_count, model_width), low)]
        + [pltpu.VMEM(each.shape, low) for each in kept]
        + [pltpu.SemaphoreType.DMA((2 + block_count,))],
        compiler_params=pltpu.CompilerParams(vmem_limit_bytes=46 * mib),
        name="attend",
    )(seq_lengths, layer_in, gain_attn[None], qkv_flat, cosine, sine)

    w_in_near, w_out_near, output_far, output_near, attended = lax.optimization_barrier(
        (w_in_near, w_out_near, output_far, output_near, attended)
    )
    w_in_near = jnp.concatenate([w_in_own, w_in_near])
    w_out_near = jnp.concatenate([w_out_own, w_out_near])
    w_in_far = exchange(w_in_near, "expert", 4)
    w_out_far = exchange(w_out_near, "expert", 2)
    heads_far = exchange(attended, "tensor", 2)
    heads_near = exchange(attended, "tensor", 1)
    output_both = exchange(output_far, "tensor", 1)
    heads_far, heads_near, w_in_near, w_out_near, output_both = lax.optimization_barrier(
        (heads_far, heads_near, w_in_near, w_out_near, output_both)
    )
    heads_both = exchange(heads_far, "tensor", 1)
    heads_both, w_in_far, w_out_far = lax.optimization_barrier((heads_both, w_in_far, w_out_far))
    w_in_all = gather_pairs(w_in_near, w_in_far)
    w_out_all = gather_pairs(w_out_near, w_out_far)
    heads_all = [attended, heads_near, heads_far, heads_both]
    output_mine = jnp.concatenate([output_own, output_near, output_far, output_both])
    output_other = exchange(output_mine, "expert", 1)
    router_rows = jnp.pad(jnp.transpose(w_router), ((0, LANES - experts_all), (0, 0)))
    part_shapes = (shaped((span, model_width), wide),) + (
        shaped((span, model_width), low),
    ) * (tensor_count - 1)
    residual_all, inverse_all, normed_two, gates = pl.pallas_call(
        branch_kernel,
        out_shape=(
            shaped((token_count, model_width), wide),
            shaped((token_count, 1), wide),
            shaped((token_count, model_width), low),
            shaped((token_count, LANES), wide),
        ),
        in_specs=in_smem(1) + in_vmem(7),
        out_specs=tuple(in_vmem(4)),
        scratch_shapes=[pltpu.VMEM((model_width, model_width), low)],
        compiler_params=pltpu.CompilerParams(vmem_limit_bytes=12 * mib),
        name="branch",
    )(
        place,
        gain_ffn[None],
        router_rows,
        routes,
        layer_in,
        output_mine,
        output_other,
        jnp.concatenate(heads_all, 1),
    )
    middle = pl.pallas_call(
        functools.partial(middle_kernel, tensor_count),
        out_shape=part_shapes
        + (
            shaped((span, model_width), wide),
            shaped((span, 1), wide),
            shaped((token_count, experts_all * units), low),
            shaped((token_count, experts_all * 2 * units), low),
            shaped((1, model_width), wide),
            shaped((experts_all, model_width), wide),
        ),
        in_specs=in_smem(1) + in_vmem(14),
        out_specs=tuple(in_vmem(tensor_count + 6)),
        scratch_shapes=[
            pltpu.VMEM((token_count, units), wide),
            pltpu.VMEM((token_count, units), low),
            pltpu.VMEM((token_count, 2 * units), wide),
            pltpu.VMEM((token_count, experts_all * units), wide),
            pltpu.VMEM((token_count, model_width), wide),
        ],
        compiler_params=pltpu.CompilerParams(vmem_limit_bytes=24 * mib),
        name="middle",
    )(
        place,
        router_rows,
        out_grad,
        residual_all,
        inverse_all,
        normed_two,
        gates,
        *w_in_all,
        *w_out_all,
    )
    normed_parts, middle = middle[:tensor_count], middle[tensor_count:]
    residual, inverse_two, active, pre_grad, gain_ffn_part, router_part = middle

    relayed = exchange(normed_parts[3], "tensor", 1)
    half_grads = shaped((experts_all // 2 * 3 * units, model_width), low)
    late = pl.pallas_call(
        functools.partial(weight_grad_kernel, tensor_count),
        out_shape=part_shapes + (half_grads,) * 2,
        in_specs=in_smem(1) + in_vmem(8),
        out_specs=tuple(in_vmem(tensor_count + 2)),
        scratch_shapes=[pltpu.VMEM((token_count, model_width), wide)],
        compiler_params=pltpu.CompilerParams(vmem_limit_bytes=16 * mib),
        name="weight_grad",
    )(place, normed_two, out_grad, active, pre_grad, *w_out_all)
    late, relayed = lax.optimization_barrier((late, relayed))
    normed_pieces = scatter_parts(normed_parts, relayed)
    mixture_parts, kept_grads, given_grads = late[:tensor_count], late[-2], late[-1]
    given_grads = exchange(given_grads, "expert", 1)

    in_rows, out_rows = experts_all * units // 2, experts_all * units // 4
    in_kept, in_given, out_kept, out_given = pl.pallas_call(
        add_grads_kernel,
        out_shape=(
            shaped((in_rows, model_width), wide),
            shaped((in_rows, model_width), low),
            shaped((out_rows, model_width), wide),
            shaped((out_rows, model_width), low),
        ),
        in_specs=in_vmem(2),
        out_specs=tuple(in_vmem(4)),
        compiler_params=pltpu.CompilerParams(vmem_limit_bytes=16 * mib),
        name="add_grads",
    )(kept_grads, given_grads)
    residual, in_kept, in_given, out_kept, out_given = lax.optimization_barrier(
        (residual, in_kept, in_given, out_kept, out_given)
    )
    residual_grad, low_grad = pl.pallas_call(
        norm_back_kernel,
        out_shape=(shaped((span, model_width), wide), shaped((span, model_width), low)),
        in_specs=in_vmem(7),
        out_specs=tuple(in_vmem(2)),
        compiler_params=pltpu.CompilerParams(vmem_limit_bytes=6 * mib),
        name="norm_back",
    )(
        *normed_pieces,
        residual,
        inverse_two,
        gain_ffn[None],
        token_block(out_grad),
    )
    grad_blocks = gather_blocks(low_grad)

    in_arrived = exchange(in_given, "expert", 4)
    out_arrived = exchange(out_given, "expert", 2)
    mixture_last, *grad_blocks = lax.optimization_barrier((mixture_parts[3], *grad_blocks))
    mixture_relayed = exchange(mixture_last, "tensor", 1)
    fetched = (w_output, queries, pairs, probs, cosine, sine, qkv_flat)
    back = pl.pallas_call(
        functools.partial(attend_back_kernel, tensor_count),
        out_shape=(shaped((2 * span, model_width), wide),)
        + (shaped((2 * span, model_width), low),) * (tensor_count - 2)
        + (shaped((span, model_width), low),)
        + (
            shaped((token_count, model_width), low),
            shaped((token_count, 2 * head_width), low),
        ),
        in_specs=in_smem(1) + in_hbm(6 + 2 * tensor_count),
        out_specs=tuple(in_vmem(tensor_count + 2)),
        scratch_shapes=[
            pltpu.VMEM((token_count, head_width), wide),
            pltpu.VMEM((token_count, LANES), wide),
            pltpu.VMEM((token_count, model_width), wide),
        ]
        + [pltpu.VMEM(each.shape, each.dtype) for each in fetched]
        + [pltpu.SemaphoreType.DMA((len(fetched) + block_count + 2 * tensor_count,))],
        compiler_params=pltpu.CompilerParams(vmem_limit_bytes=58 * mib),
        name="attend_back",
    )(
        place,
        *fetched,
        *grad_blocks,
        *mixture_parts[:-1],
    )
    input_parts, (branch_grad, projected_grad) = (
        back[:tensor_count],
        back[tensor_count:],
    )
    *input_parts, projected_grad, in_arrived, out_arrived, mixture_relayed = (
        lax.optimization_barrier(
            (*input_parts, projected_grad, in_arrived, out_arrived, mixture_relayed)
        )
    )
    in_summed = in_kept + in_arrived.astype(wide)
    out_summed = out_kept + out_arrived.astype(wide)
    in_arrived = exchange(in_summed[in_rows // 2 :].astype(low), "expert", 2)
    out_arrived = exchange(out_summed[out_rows // 2 :].astype(low), "expert", 4)

    relayed = exchange(input_parts[3], "tensor", 1)
    row_count = (model_width + w_output.shape[0] * model_width // (2 * head_width)) // 2
    kept_sums, given_sums = pl.pallas_call(
        attend_grad_kernel,
        out_shape=(
            shaped((row_count, 2 * head_width), wide),
            shaped((row_count, 2 * head_width), low),
        ),
        in_specs=in_smem(1) + in_vmem(5),
        out_specs=tuple(in_vmem(2)),
        scratch_shapes=[pltpu.VMEM((token_count, model_width), low)],
        compiler_params=pltpu.CompilerParams(vmem_limit_bytes=12 * mib),
        name="attend_grad",
    )(place, layer_in, gain_attn[None], projected_grad, attended, branch_grad)
    relayed, kept_sums, given_sums, in_summed, out_summed = lax.optimization_barrier(
        (relayed, kept_sums, given_sums, in_summed, out_summed)
    )
    sums_half = kept_sums + exchange(given_sums, "expert", 1).astype(wide)
    sums = exchange_halves(sums_half.astype(low), (2, 4))
    input_pieces = scatter_parts(input_parts, jnp.concatenate([relayed, mixture_relayed]))
    residual, in_arrived, out_arrived, sums = lax.optimization_barrier(
        (residual, in_arrived, out_arrived, sums)
    )
    w_in_grad = (in_summed[: in_rows // 2] + in_arrived.astype(wide)).reshape(w_in.shape)
    w_out_grad = (out_summed[: out_rows // 2] + out_arrived.astype(wide)).reshape(w_out.shape)
    block = pl.pallas_call(
        finish_kernel,
        out_shape=shaped((2 * span, model_width), low),
        in_specs=in_vmem(7),
        out_specs=in_vmem(1)[0],
        compiler_params=pltpu.CompilerParams(vmem_limit_bytes=6 * mib),
        name="finish",
    )(
        *input_pieces,
        token_block(layer_in),
        gain_attn[None],
        residual_grad,
        residual,
    )
    far = exchange(block, "tensor", 2)
    near = exchange(block, "tensor", 1)
    small = jnp.concatenate([router_part, gain_ffn_part])
    sums, small, _ = lax.optimization_barrier((sums, small, block))
    small = sum_over_experts(small)
    summed = join_cores(exchange_halves(sums, (4, 2)))
    qkv_summed = summed[:model_width].reshape(w_qkv.shape)
    output_summed = jnp.concatenate(split_blocks(summed[model_width:], 0, 2), 1)

    gain_part = jnp.sum(
        qkv_flat.astype(wide) * summed[:model_width], 1
    ) / gain_attn
    small = jnp.concatenate([small, gain_part[None]])
    far, near, small, summed = lax.optimization_barrier((far, near, small, summed))
    for bit in (1, 2):
        small = small + exchange(small, "tensor", bit)
    blocks = [block, near, far, exchange(far, "tensor", 1)]
    layer_here = in_order([block[:span] for block in blocks])
    in_here = in_order([block[span:] for block in blocks])
    return (
        layer_here,
        in_here,
        small[experts_all + 1],
        qkv_summed,
        output_summed,
        small[experts_all],
        jnp.transpose(small[:experts_all]),
        w_in_grad,
        w_out_grad,
    )


def solution(mesh):
    fits = mesh.shape["tensor"] == 4 and mesh.shape["expert"] == 8
    placed = (
        P("expert", None),
        P("expert", None),
        P("expert", None),
        P(),
        P(None, "tensor", None),
        P("tensor", None),
        P(),
        P(),
        P("expert", None, "tensor", None),
        P("expert", "tensor", None),
        P("expert", None),
    )
    return jax.shard_map(
        on_device if fits else on_device_general,
        mesh=mesh,
        in_specs=placed,
        out_specs=(
            P("expert", None),
            P("expert", None),
            P(),
            P(None, "tensor", None),
            P("tensor", None),
            P(),
            P(),
            P("expert", None, "tensor", None),
            P("expert", "tensor", None),
        ),
        check_vma=False,
    )
```

```python
import functools
import math

import jax
import jax.numpy as jnp
import numpy as np
from jax import lax
from jax.experimental import pallas as pl
from jax.experimental.pallas import tpu as pltpu
from jax.sharding import PartitionSpec as P

HEADS = 16
KV_HEADS = 8
HEAD_DIM = 64


epsilon = 1e-06
rope_base = 10000.0
masked_out = -1e30


def rms_forward(values, gain_vec):
    inverse = lax.rsqrt(jnp.mean(values * values, axis=-1, keepdims=True) + epsilon)
    return (values * inverse * gain_vec, inverse)


def rms_backward(values, inverse, gain_vec, upstream):
    normal = values * inverse
    scaled = upstream * gain_vec
    inner_mean = jnp.mean(scaled * normal, axis=-1, keepdims=True)
    return inverse * (scaled - normal * inner_mean)


def positions(lengths, token_count):
    seq_ends = jnp.cumsum(lengths, dtype=jnp.int32)
    row_index = jnp.arange(token_count, dtype=jnp.int32)
    segment = jnp.sum(
        (row_index[:, None] >= seq_ends[None, :]).astype(jnp.int32), axis=1, dtype=jnp.int32
    )
    seq_ids = jnp.arange(lengths.shape[0], dtype=jnp.int32)
    seq_start = jnp.sum(
        jnp.where(segment[:, None] == seq_ids[None, :], (seq_ends - lengths)[None, :], 0),
        axis=1,
        dtype=jnp.int32,
    )
    return (segment, row_index - seq_start)


def rope_tables(position, head_dim):
    half_dim = head_dim // 2
    inverse_freq = jnp.exp(
        jnp.arange(half_dim, dtype=jnp.float32) * (-2.0 * math.log(rope_base) / head_dim)
    )
    angles = position.astype(jnp.float32)[:, None] * inverse_freq[None, :]
    cosine = jnp.cos(angles)
    sine_tab = jnp.sin(angles)
    return (jnp.concatenate([cosine, cosine], 1), jnp.concatenate([sine_tab, sine_tab], 1))


def rotate(values, cosine, sine_tab):
    half_dim = values.shape[-1] // 2
    turned = jnp.concatenate([-values[..., half_dim:], values[..., :half_dim]], -1)
    return values * cosine + turned * sine_tab


def split_blocks(array_in, axis_at, block_count):
    dims_now = array_in.shape
    regrouped = array_in.reshape(
        dims_now[:axis_at]
        + (block_count, dims_now[axis_at] // block_count)
        + dims_now[axis_at + 1 :]
    )
    return jnp.moveaxis(regrouped, axis_at, 0)


def join_blocks(array_in, axis_at):
    regrouped = jnp.moveaxis(array_in, 0, axis_at)
    dims_now = regrouped.shape
    return regrouped.reshape(
        dims_now[:axis_at] + (dims_now[axis_at] * dims_now[axis_at + 1],) + dims_now[axis_at + 2 :]
    )


def block_scores(query_block, key_rows, segment_rows, row_start, segment, scaling):
    block_rows = query_block.shape[2]
    scores_raw = (
        jnp.einsum("kgbd,ksd->kgbs", query_block, key_rows, preferred_element_type=jnp.float32)
        * scaling
    )
    query_index = row_start + jnp.arange(block_rows, dtype=jnp.int32)
    key_index = jnp.arange(key_rows.shape[1], dtype=jnp.int32)
    allowed = (segment_rows[:, None] == segment[None, :]) & (
        key_index[None, :] <= query_index[:, None]
    )
    return jnp.where(allowed[None, None], scores_raw, masked_out)


def attention_forward(queries, key_rows, values, segment, scaling, block_size):
    block_count = queries.shape[2] // block_size
    starts_all = jnp.arange(block_count, dtype=jnp.int32) * block_size

    def one_block(packed):
        query_block, segment_rows, row_start = packed
        scores = block_scores(query_block, key_rows, segment_rows, row_start, segment, scaling)
        top_score = jnp.max(scores, -1)
        exponent = jnp.exp(scores - top_score[..., None])
        row_total = jnp.sum(exponent, -1)
        probs = (exponent / row_total[..., None]).astype(jnp.bfloat16)
        output = jnp.einsum("kgbs,ksd->kgbd", probs, values, preferred_element_type=jnp.float32)
        return (output.astype(jnp.bfloat16), top_score, row_total)

    outputs, top_blocks, total_blocks = lax.map(
        one_block,
        (
            split_blocks(queries, 2, block_count),
            segment.reshape(block_count, block_size),
            starts_all,
        ),
    )
    return (join_blocks(outputs, 2), join_blocks(top_blocks, 2), join_blocks(total_blocks, 2))


def attention_backward(
    queries, key_rows, values, heads_grad, segment, top_kept, total_kept, scaling, block_size
):
    block_count = queries.shape[2] // block_size
    starts_all = jnp.arange(block_count, dtype=jnp.int32) * block_size

    def one_block(running, packed):
        key_acc, value_acc = running
        query_block, grad_block, segment_rows, row_start, top_block, total_block = packed
        scores = block_scores(query_block, key_rows, segment_rows, row_start, segment, scaling)
        probs = jnp.exp(scores - top_block[..., None]) / total_block[..., None]
        probs_low = probs.astype(jnp.bfloat16)
        value_acc = value_acc + jnp.einsum(
            "kgbs,kgbd->ksd", probs_low, grad_block, preferred_element_type=jnp.float32
        )
        prob_grad = jnp.einsum(
            "kgbd,ksd->kgbs", grad_block, values, preferred_element_type=jnp.float32
        )
        inner_sum = jnp.sum(probs * prob_grad, -1, keepdims=True)
        score_grad = (probs * (prob_grad - inner_sum)).astype(jnp.bfloat16)
        query_grad = (
            jnp.einsum("kgbs,ksd->kgbd", score_grad, key_rows, preferred_element_type=jnp.float32)
            * scaling
        )
        key_acc = (
            key_acc
            + jnp.einsum(
                "kgbs,kgbd->ksd", score_grad, query_block, preferred_element_type=jnp.float32
            )
            * scaling
        )
        return ((key_acc, value_acc), query_grad)

    empty = jnp.zeros(key_rows.shape, jnp.float32)
    packed_all = (
        split_blocks(queries, 2, block_count),
        split_blocks(heads_grad, 2, block_count),
        segment.reshape(block_count, block_size),
        starts_all,
        split_blocks(top_kept, 2, block_count),
        split_blocks(total_kept, 2, block_count),
    )
    (key_grad, value_grad), query_blocks = lax.scan(one_block, (empty, empty), packed_all)
    return (join_blocks(query_blocks, 2), key_grad, value_grad)


def on_device_general(
    layer_in,
    seq_lengths,
    routes,
    gain_attn,
    w_qkv,
    w_output,
    gain_ffn,
    w_router,
    w_in,
    w_out,
    out_grad,
):
    token_count, model_width = layer_in.shape
    kv_here = w_qkv.shape[1]
    group_size = HEADS // KV_HEADS
    scaling = 1.0 / math.sqrt(HEAD_DIM)
    block_size = min(512, token_count)
    w_output_all = lax.all_gather(w_output, "tensor", axis=0, tiled=True)
    w_gate_all = lax.all_gather(w_in[0, 0], "expert", axis=0, tiled=True)
    w_up_all = lax.all_gather(w_in[0, 1], "expert", axis=0, tiled=True)
    w_out_all = lax.all_gather(w_out[0], "expert", axis=0, tiled=True)
    segment, position = positions(seq_lengths[0], token_count)
    cosine, sine_tab = rope_tables(position, HEAD_DIM)
    inputs = layer_in.astype(jnp.float32)
    normed_one, inverse_one = rms_forward(inputs, gain_attn)
    normed_one_low = normed_one.astype(jnp.bfloat16)
    qkv_flat = w_qkv.reshape(model_width, -1)
    projected = jnp.dot(normed_one_low, qkv_flat, preferred_element_type=jnp.float32)
    projected = projected.reshape(token_count, kv_here, group_size + 2, HEAD_DIM)
    queries = rotate(
        jnp.transpose(projected[:, :, :group_size], (1, 2, 0, 3)), cosine, sine_tab
    ).astype(jnp.bfloat16)
    key_rows = rotate(
        jnp.transpose(projected[:, :, group_size], (1, 0, 2)), cosine, sine_tab
    ).astype(jnp.bfloat16)
    values = jnp.transpose(projected[:, :, group_size + 1], (1, 0, 2)).astype(jnp.bfloat16)
    attended, top_kept, total_kept = attention_forward(
        queries, key_rows, values, segment, scaling, block_size
    )
    heads_out = jnp.transpose(attended, (2, 0, 1, 3)).reshape(token_count, -1)
    heads_all = lax.all_gather(heads_out, "tensor", axis=1, tiled=True)
    branch_here = jnp.dot(heads_all, w_output_all, preferred_element_type=jnp.float32)
    residual = inputs + branch_here
    normed_two, inverse_two = rms_forward(residual, gain_ffn)
    normed_low = normed_two.astype(jnp.bfloat16)
    experts_all = w_router.shape[1]
    unit_count = w_out.shape[1]
    logits = jnp.dot(normed_low, w_router, preferred_element_type=jnp.float32)
    expert_ids = jnp.arange(experts_all, dtype=jnp.int32)
    picked = jnp.any(routes[:, :, None] == expert_ids[None, None, :], axis=1)
    picked_logits = jnp.where(picked, logits, masked_out)
    top_logit = jnp.max(picked_logits, -1, keepdims=True)
    weight = jnp.where(picked, jnp.exp(picked_logits - top_logit), 0.0)
    gates = weight / jnp.sum(weight, -1, keepdims=True)

    def by_unit(per_expert):
        return jnp.broadcast_to(
            per_expert[:, :, None], (token_count, experts_all, unit_count)
        ).reshape(token_count, -1)

    def over_units(per_unit):
        return jnp.sum(per_unit.reshape(token_count, experts_all, unit_count), -1)

    def times_transposed(left, right):
        return lax.dot_general(
            left, right, (((1,), (1,)), ((), ())), preferred_element_type=jnp.float32
        )

    def transposed_times(left, right):
        return lax.dot_general(
            left, right, (((0,), (0,)), ((), ())), preferred_element_type=jnp.float32
        )

    gates_wide = by_unit(gates)
    gate_vals = times_transposed(normed_low, w_gate_all)
    up_vals = times_transposed(normed_low, w_up_all)
    plain_grad = times_transposed(out_grad, w_out_all)
    sig_vals = jax.nn.sigmoid(gate_vals)
    silu_vals = gate_vals * sig_vals
    active = silu_vals * up_vals
    scaled_active = (active * gates_wide).astype(jnp.bfloat16)
    active_grad = plain_grad * gates_wide
    gate_pre = (
        active_grad * up_vals * (sig_vals * (1.0 + gate_vals * (1.0 - sig_vals)))
    ).astype(jnp.bfloat16)
    up_pre = (active_grad * silu_vals).astype(jnp.bfloat16)
    gate_grad_part = over_units(active * plain_grad)
    logit_part = (
        gates * (gate_grad_part - jnp.sum(gates * gate_grad_part, -1, keepdims=True))
    ).astype(jnp.bfloat16)
    normed_two_part = (
        jnp.dot(gate_pre, w_gate_all, preferred_element_type=jnp.float32)
        + jnp.dot(up_pre, w_up_all, preferred_element_type=jnp.float32)
        + times_transposed(logit_part, w_router)
    )
    normed_two_grad = lax.psum(normed_two_part.astype(jnp.bfloat16), "tensor").astype(jnp.float32)
    mixture_part = jnp.dot(scaled_active, w_out_all, preferred_element_type=jnp.float32)
    mixture = lax.psum(mixture_part.astype(jnp.bfloat16), "tensor").astype(jnp.float32)
    layer_here = (residual + mixture).astype(jnp.bfloat16)

    def to_owner(partial):
        return lax.psum_scatter(
            partial.astype(jnp.bfloat16), "expert", scatter_dimension=0, tiled=True
        ).astype(jnp.float32)

    w_gate_grad = to_owner(transposed_times(gate_pre, normed_low))
    w_up_grad = to_owner(transposed_times(up_pre, normed_low))
    w_in_grad = jnp.stack([w_gate_grad, w_up_grad])[None]
    w_out_grad = to_owner(transposed_times(scaled_active, out_grad))[None]
    router_part = transposed_times(logit_part, normed_low)
    normal_two = residual * inverse_two
    gain_ffn_part = jnp.sum(normed_two_part * normal_two, axis=0)
    upstream = out_grad.astype(jnp.float32)
    residual_part = rms_backward(residual, inverse_two, gain_ffn, normed_two_grad)
    residual_grad = upstream + residual_part
    branch_here_grad = residual_grad.astype(jnp.bfloat16)
    w_output_grad = lax.dot_general(
        heads_out, branch_here_grad, (((0,), (0,)), ((), ())), preferred_element_type=jnp.float32
    )
    heads_flat = lax.dot_general(
        branch_here_grad, w_output, (((1,), (1,)), ((), ())), preferred_element_type=jnp.float32
    ).astype(jnp.bfloat16)
    heads_grad = jnp.transpose(
        heads_flat.reshape(token_count, kv_here, group_size, HEAD_DIM), (1, 2, 0, 3)
    )
    query_grad, key_grad, value_grad = attention_backward(
        queries, key_rows, values, heads_grad, segment, top_kept, total_kept, scaling, block_size
    )
    query_grad = rotate(query_grad, cosine, -sine_tab)
    key_grad = rotate(key_grad, cosine, -sine_tab)
    projected_grad = jnp.concatenate(
        [
            jnp.transpose(query_grad, (2, 0, 1, 3)),
            jnp.transpose(key_grad, (1, 0, 2))[:, :, None],
            jnp.transpose(value_grad, (1, 0, 2))[:, :, None],
        ],
        2,
    )
    projected_grad = projected_grad.reshape(token_count, -1).astype(jnp.bfloat16)
    w_qkv_grad = lax.dot_general(
        normed_one_low, projected_grad, (((0,), (0,)), ((), ())), preferred_element_type=jnp.float32
    ).reshape(w_qkv.shape)
    normed_one_part = lax.dot_general(
        projected_grad, qkv_flat, (((1,), (1,)), ((), ())), preferred_element_type=jnp.float32
    )
    gain_attn_part = jnp.sum(normed_one_part * (inputs * inverse_one), axis=0)
    normed_one_grad = lax.psum(normed_one_part.astype(jnp.bfloat16), "tensor").astype(jnp.float32)
    input_part = rms_backward(inputs, inverse_one, gain_attn, normed_one_grad)
    in_here = (residual_grad + input_part).astype(jnp.bfloat16)
    qkv_summed = lax.psum(w_qkv_grad.astype(jnp.bfloat16), "expert").astype(jnp.float32)
    output_summed = lax.psum(w_output_grad.astype(jnp.bfloat16), "expert").astype(jnp.float32)
    small = jnp.concatenate([router_part, gain_ffn_part[None], gain_attn_part[None]])
    small = lax.psum(small, ("expert", "tensor"))
    return (
        layer_here,
        in_here,
        small[experts_all + 1],
        qkv_summed,
        output_summed,
        small[experts_all],
        jnp.transpose(small[:experts_all]),
        w_in_grad,
        w_out_grad,
    )


LANES = 128
ROWS = 128
IN_ORDER = (0, 2, 4, 6, 1, 3, 5, 7)
OUT_ORDER = (0, 4, 2, 6, 1, 5, 3, 7)


def exchange(array_in, axis_name, bits):
    count = lax.axis_size(axis_name)
    return lax.ppermute(array_in, axis_name, [(i, i ^ bits) for i in range(count)])


def gather_blocks(own):
    far = exchange(own, "tensor", 2)
    near = exchange(own, "tensor", 1)
    far, near = lax.optimization_barrier((far, near))
    return [own, near, far, exchange(far, "tensor", 1)]


def scatter_parts(parts, relayed):
    near, far, relayed = lax.optimization_barrier((parts[1], parts[2], relayed))
    far = (far.astype(jnp.float32) + relayed.astype(jnp.float32)).astype(jnp.bfloat16)
    far = exchange(far, "tensor", 2)
    return parts[0], exchange(near, "tensor", 1), far


def gather_pairs(near, far):
    return [near, far, exchange(near, "expert", 1), exchange(far, "expert", 1)]


def exchange_halves(array_in, bits):
    rows = array_in.shape[0] // 2
    halves = []
    for half, bit in zip((array_in[:rows], array_in[rows:]), bits):
        arrived = exchange(half, "expert", bit)
        halves.append((half.astype(jnp.float32) + arrived.astype(jnp.float32)).astype(jnp.bfloat16))
    return jnp.concatenate(halves)


def join_cores(half):
    core = lax.axis_index("expert") & 1
    other = exchange(half, "expert", 1)
    return jnp.concatenate(
        [jnp.where(core == 0, half, other), jnp.where(core == 0, other, half)]
    ).astype(jnp.float32)


def sum_over_experts(array_in):
    for bit in (1, 2, 4):
        array_in = array_in + exchange(array_in, "expert", bit)
    return array_in


def dot_plain(left, right):
    return jnp.dot(left, right, preferred_element_type=jnp.float32)


def dot_transposed(left, right):
    return lax.dot_general(
        left, right, (((1,), (1,)), ((), ())), preferred_element_type=jnp.float32
    )


def transposed_dot(left, right):
    return lax.dot_general(
        left, right, (((0,), (0,)), ((), ())), preferred_element_type=jnp.float32
    )


def lane_index(shape):
    return lax.broadcasted_iota(jnp.int32, shape, 1)


def turn(values):
    low_half = (lane_index(values.shape) & (HEAD_DIM - 1)) < HEAD_DIM // 2
    return jnp.where(
        low_half,
        -pltpu.roll(values, LANES - HEAD_DIM // 2, 1),
        pltpu.roll(values, HEAD_DIM // 2, 1),
    )


def swap_heads(values):
    return pltpu.roll(values, HEAD_DIM, 1)


def first_head(shape):
    return lane_index(shape) < HEAD_DIM


def angle_tables(token_count):
    half_dim = HEAD_DIM // 2
    inverse_freq = np.exp(np.arange(half_dim) * (-2.0 * math.log(rope_base) / HEAD_DIM))
    angles = np.arange(token_count)[:, None] * inverse_freq[None, :]
    tile = LANES // half_dim
    return (
        np.tile(np.cos(angles), (1, tile)).astype(np.float32),
        np.tile(np.sin(angles), (1, tile)).astype(np.float32),
    )


def attend_kernel(
    lengths,
    layer_in,
    gain,
    w_qkv,
    cosine,
    sine,
    queries_out,
    pairs_out,
    probs_out,
    attended,
    normed,
    queries,
    pairs,
    probs,
    sems,
):
    token_count = layer_in.shape[0]
    kv_here = pairs.shape[0]
    for row in range(0, token_count, ROWS):
        rows = pl.ds(row, ROWS)
        values = layer_in[rows, :].astype(jnp.float32)
        scale = lax.rsqrt(jnp.mean(values * values, axis=-1, keepdims=True) + epsilon)
        normed[rows, :] = (values * scale * gain[...]).astype(jnp.bfloat16)
    is_first = first_head((ROWS, LANES))
    for kv in range(kv_here):
        projected = dot_plain(normed[...], w_qkv[:, 2 * LANES * kv : 2 * LANES * (kv + 1)])
        for block in range(token_count // ROWS):
            rows = pl.ds(block * ROWS, ROWS)
            cos_rows, sin_rows = cosine[rows, :], sine[rows, :]
            query = projected[block * ROWS : (block + 1) * ROWS, :LANES]
            query = (query * cos_rows + turn(query) * sin_rows) * (1.0 / math.sqrt(HEAD_DIM))
            queries[kv, block, :ROWS, :] = jnp.where(is_first, query, 0.0).astype(jnp.bfloat16)
            queries[kv, block, ROWS:, :] = jnp.where(is_first, swap_heads(query), 0.0).astype(
                jnp.bfloat16
            )
            pair = projected[block * ROWS : (block + 1) * ROWS, LANES:]
            pairs[kv, rows, :] = jnp.where(
                is_first, pair * cos_rows + turn(pair) * sin_rows, pair
            ).astype(jnp.bfloat16)
    copies = [
        pltpu.make_async_copy(queries, queries_out, sems.at[0]),
        pltpu.make_async_copy(pairs, pairs_out, sems.at[1]),
    ]
    for copy in copies:
        copy.start()
    for block in range(token_count // ROWS):
        keys = (block + 1) * ROWS
        token = block * ROWS + (
            lax.broadcasted_iota(jnp.int32, (2 * ROWS, keys), 0) & (ROWS - 1)
        )
        start = jnp.zeros_like(token)
        end = 0
        for seq in range(lengths.shape[1] - 1):
            end = end + lengths[0, seq]
            start = jnp.where(token >= end, end, start)
        key = lane_index((2 * ROWS, keys))
        allowed = (key <= token) & (key >= start)
        for kv in range(kv_here):
            scores = dot_transposed(queries[kv, block], pairs[kv, :keys, :])
            scores = jnp.where(allowed, scores, masked_out)
            exponent = jnp.exp(scores - jnp.max(scores, -1, keepdims=True))
            share = (exponent * (1.0 / jnp.sum(exponent, -1, keepdims=True))).astype(jnp.bfloat16)
            probs[kv, block, :, :keys] = share
            output = dot_plain(share, pairs[kv, :keys, :])
            attended[pl.ds(block * ROWS, ROWS), kv * LANES : (kv + 1) * LANES] = jnp.where(
                is_first, swap_heads(output[:ROWS]), output[ROWS:]
            ).astype(jnp.bfloat16)
        copies.append(
            pltpu.make_async_copy(
                probs.at[:, block, :, :keys], probs_out.at[:, block, :, :keys], sems.at[2 + block]
            )
        )
        copies[-1].start()
    for copy in copies:
        copy.wait()


def write_parts(place, total, parts, span):
    for number, part in enumerate(parts):
        row = pl.multiple_of((place[0] ^ number) * span, span)
        part[...] = total[pl.ds(row, span), :].astype(part.dtype)


def branch_kernel(
    place,
    gain,
    router,
    routes,
    layer_in,
    w_mine,
    w_other,
    heads,
    residual,
    inverse,
    normed,
    gates,
    w_output,
):
    token_count, model_width = layer_in.shape
    half = LANES
    mine = (place[1] & 1) * half
    for row in range(0, model_width, 2 * half):
        rows = pl.ds(row // 2, half)
        w_output[pl.ds(pl.multiple_of(row + mine, half), half), :] = w_mine[rows, :]
        w_output[pl.ds(pl.multiple_of(row + half - mine, half), half), :] = w_other[rows, :]

    def branch_step(number, carry):
        columns = pl.ds(pl.multiple_of(number * 2 * LANES, 2 * LANES), 2 * LANES)
        residual[:, columns] = layer_in[:, columns].astype(jnp.float32) + dot_plain(
            heads[...], w_output[:, columns]
        )
        return carry

    lax.fori_loop(0, model_width // (2 * LANES), branch_step, 0)
    for row in range(0, token_count, ROWS):
        rows = pl.ds(row, ROWS)
        values = residual[rows, :]
        scale = lax.rsqrt(jnp.mean(values * values, axis=-1, keepdims=True) + epsilon)
        inverse[rows, :] = scale
        normed[rows, :] = (values * scale * gain[...]).astype(jnp.bfloat16)
    gates[...] = dot_transposed(normed[...], router[...])
    lane = lane_index((ROWS, LANES))
    for row in range(0, token_count, ROWS):
        rows = pl.ds(row, ROWS)
        picked = routes[rows, 0:1] == lane
        for top in range(1, routes.shape[1]):
            picked = picked | (routes[rows, top : top + 1] == lane)
        logits = jnp.where(picked, gates[rows, :], masked_out)
        weight = jnp.where(picked, jnp.exp(logits - jnp.max(logits, -1, keepdims=True)), 0.0)
        gates[rows, :] = weight / jnp.sum(weight, -1, keepdims=True)


def middle_kernel(tensor_count, *refs):
    place, router, out_grad, residual, inverse, normed, gates = refs[:7]
    w_ins, w_outs, refs = refs[7:11], refs[11:15], refs[15:]
    parts, refs = refs[:tensor_count], refs[tensor_count:]
    (residual_block, inverse_block, active_out, pre_out, gain_part, router_part) = refs[:6]
    (gate_wide, product, hidden, plain, total) = refs[6:]
    token_count, model_width = normed.shape
    experts_all = router_part.shape[0]
    units = w_outs[0].shape[0] // 2
    span = token_count // tensor_count
    for pair, weights in enumerate(w_outs):
        plain[:, 2 * pair * units : 2 * (pair + 1) * units] = dot_transposed(
            out_grad[...], weights[...]
        )
    gates_high = gates[...].astype(jnp.bfloat16)
    gates_low = (gates[...] - gates_high.astype(jnp.float32)).astype(jnp.bfloat16)
    total_grad = jnp.zeros((token_count, LANES), jnp.float32)
    for number in range(experts_all):
        name = place[1] ^ IN_ORDER[number]
        in_rows = pl.ds(number % 2 * 2 * units, 2 * units)
        out_number = OUT_ORDER.index(IN_ORDER[number])
        hidden[...] = dot_transposed(normed[...], w_ins[number // 2][in_rows, :])
        out_lanes = pl.ds(out_number * units, units)
        chosen = lax.broadcasted_iota(jnp.int32, (LANES, units), 0) == name
        chosen = jnp.where(chosen, 1.0, 0.0).astype(jnp.bfloat16)
        gate_wide[...] = dot_plain(gates_high, chosen) + dot_plain(gates_low, chosen)
        for row in range(0, token_count, ROWS):
            rows = pl.ds(row, ROWS)
            gate = gate_wide[rows, :]
            gate_vals, up_vals = hidden[rows, :units], hidden[rows, units:]
            sig_vals = 0.5 + 0.5 * jnp.tanh(0.5 * gate_vals)
            silu_vals = gate_vals * sig_vals
            active = silu_vals * up_vals
            grad = plain[rows, out_lanes]
            product[rows, :] = (active * grad).astype(jnp.bfloat16)
            active_grad = grad * gate
            active_out[rows, out_number * units : (out_number + 1) * units] = (
                active * gate
            ).astype(jnp.bfloat16)
            pre_out[rows, 2 * number * units : (2 * number + 1) * units] = (
                active_grad * up_vals * (sig_vals * (1.0 + gate_vals * (1.0 - sig_vals)))
            ).astype(jnp.bfloat16)
            pre_out[rows, (2 * number + 1) * units : (2 * number + 2) * units] = (
                active_grad * silu_vals
            ).astype(jnp.bfloat16)
        total_grad = total_grad + dot_transposed(product[...], chosen)
    gate_all, grad_all = gates[...], total_grad
    logit_part = (
        gate_all * (grad_all - jnp.sum(gate_all * grad_all, -1, keepdims=True))
    ).astype(jnp.bfloat16)
    router_part[...] = transposed_dot(logit_part, normed[...])[:experts_all]

    def column_step(number, carry):
        columns = pl.ds(pl.multiple_of(number * 2 * LANES, 2 * LANES), 2 * LANES)
        summed = dot_plain(logit_part, router[:, columns])
        for pair, weights in enumerate(w_ins):
            pre = pre_out[:, 4 * pair * units : 4 * (pair + 1) * units]
            summed = summed + dot_plain(pre, weights[:, columns])
        total[:, columns] = summed
        return carry

    lax.fori_loop(0, model_width // (2 * LANES), column_step, 0)
    write_parts(place, total, parts, span)
    row = pl.ds(pl.multiple_of(place[0] * span, span), span)
    residual_block[...] = residual[row, :]
    inverse_block[...] = inverse[row, :]
    gain_sum = jnp.zeros((1, model_width), jnp.float32)
    for row in range(0, token_count, ROWS):
        rows = pl.ds(row, ROWS)
        gain_sum = gain_sum + jnp.sum(
            total[rows, :] * (residual[rows, :] * inverse[rows, :]), 0, keepdims=True
        )
    gain_part[...] = gain_sum


def weight_grad_kernel(tensor_count, *refs):
    place, normed, out_grad, active, pre_grad = refs[:5]
    w_outs, parts = refs[5:9], refs[9 : 9 + tensor_count]
    kept, given, total = refs[9 + tensor_count :]
    token_count, model_width = normed.shape
    units = w_outs[0].shape[0] // 2
    experts_all = 2 * kept.shape[0] // (3 * units)

    def column_step(number, carry):
        columns = pl.ds(pl.multiple_of(number * 2 * LANES, 2 * LANES), 2 * LANES)
        summed = jnp.zeros((token_count, 2 * LANES), jnp.float32)
        for pair, weights in enumerate(w_outs):
            summed = summed + dot_plain(
                active[:, 2 * pair * units : 2 * (pair + 1) * units], weights[:, columns]
            )
        total[:, columns] = summed
        return carry

    lax.fori_loop(0, model_width // (2 * LANES), column_step, 0)
    write_parts(place, total, parts, token_count // tensor_count)
    for number in range(experts_all):
        out_number = OUT_ORDER.index(IN_ORDER[number])
        grads = kept if number < experts_all // 2 else given
        in_row = number % (experts_all // 2) * 2 * units
        out_row = experts_all * units + out_number % (experts_all // 2) * units
        grads[pl.ds(in_row, 2 * units), :] = transposed_dot(
            pre_grad[:, 2 * number * units : 2 * (number + 1) * units], normed[...]
        ).astype(jnp.bfloat16)
        grads[pl.ds(out_row, units), :] = transposed_dot(
            active[:, out_number * units : (out_number + 1) * units], out_grad[...]
        ).astype(jnp.bfloat16)


def add_grads_kernel(kept, given, in_kept, in_given, out_kept, out_given):
    row = 0
    for target in (in_kept, in_given, out_kept, out_given):
        rows = pl.ds(row, target.shape[0])
        summed = kept[rows, :].astype(jnp.float32) + given[rows, :].astype(jnp.float32)
        target[...] = summed.astype(target.dtype)
        row += target.shape[0]


def attend_back_kernel(tensor_count, *refs):
    place, far_refs, refs = refs[0], refs[1:8], refs[8:]
    blocks, refs = refs[:tensor_count], refs[tensor_count:]
    mixtures, refs = refs[: tensor_count - 1], refs[tensor_count - 1 :]
    parts, refs = refs[:tensor_count], refs[tensor_count:]
    branch_grad, projected_grad, heads_grad, pair_grad, total = refs[:5]
    near_refs, sems = refs[5:12], refs[12]
    w_output, queries, pairs, probs, cosine, sine, w_qkv = near_refs
    copies, prob_copies = [], []
    for number, (source, target) in enumerate(zip(far_refs, near_refs)):
        if target is probs:
            for block in range(probs.shape[1]):
                part = (slice(None), block, slice(None), slice((block + 1) * ROWS))
                prob_copies.append(
                    pltpu.make_async_copy(
                        source.at[part], target.at[part], sems.at[len(near_refs) + block]
                    )
                )
        else:
            copies.append(pltpu.make_async_copy(source, target, sems.at[number]))
    more = len(near_refs) + len(prob_copies)
    token_count, model_width = branch_grad.shape
    span = token_count // tensor_count
    mixture_copies = [
        pltpu.make_async_copy(mixture, part.at[pl.ds(span, span)], sems.at[more + number])
        for number, (mixture, part) in enumerate(zip(mixtures, parts[:-1]))
    ]
    block_copies = []
    for number, block in enumerate(blocks):
        row = pl.multiple_of((place[0] ^ number) * span, span)
        block_copies.append(
            pltpu.make_async_copy(
                block,
                branch_grad.at[pl.ds(row, span)],
                sems.at[more + tensor_count + number],
            )
        )
    for copy in block_copies + copies[:5] + prob_copies + copies[5:] + mixture_copies:
        copy.start()
    for copy in copies[:1] + block_copies:
        copy.wait()
    heads_grad[...] = dot_transposed(branch_grad[...], w_output[...])
    for copy in copies[1:5]:
        copy.wait()
    is_first = first_head((ROWS, LANES))
    for kv in range(pairs.shape[0]):
        pair_grad[...] = jnp.zeros_like(pair_grad)
        for block in range(token_count // ROWS):
            keys = (block + 1) * ROWS
            rows = pl.ds(block * ROWS, ROWS)
            upper = heads_grad[rows, kv * LANES : (kv + 1) * LANES]
            upper = jnp.concatenate(
                [
                    jnp.where(is_first, 0.0, swap_heads(upper)),
                    jnp.where(is_first, 0.0, upper),
                ]
            ).astype(jnp.bfloat16)
            if kv == 0:
                prob_copies[block].wait()
            share_low = probs[kv, block, :, :keys]
            share = share_low.astype(jnp.float32)
            prob_grad = dot_transposed(upper, pairs[kv, :keys, :])
            inner = jnp.sum(share * prob_grad, -1, keepdims=True)
            score_grad = (share * (prob_grad - inner)).astype(jnp.bfloat16)
            query_grad = dot_plain(score_grad, pairs[kv, :keys, :])
            query_grad = jnp.where(
                is_first, query_grad[:ROWS], swap_heads(query_grad[ROWS:])
            ) * (1.0 / math.sqrt(HEAD_DIM))
            projected_grad[rows, 2 * kv * LANES : (2 * kv + 1) * LANES] = (
                query_grad * cosine[rows, :] - turn(query_grad) * sine[rows, :]
            ).astype(jnp.bfloat16)
            pair_grad[:keys, :] = (
                pair_grad[:keys, :]
                + transposed_dot(score_grad, queries[kv, block])
                + transposed_dot(share_low, upper)
            )
        for block in range(token_count // ROWS):
            rows = pl.ds(block * ROWS, ROWS)
            grad = pair_grad[rows, :]
            projected_grad[rows, (2 * kv + 1) * LANES : (2 * kv + 2) * LANES] = jnp.where(
                is_first, grad * cosine[rows, :] - turn(grad) * sine[rows, :], grad
            ).astype(jnp.bfloat16)

    for copy in copies[5:]:
        copy.wait()

    def column_step(number, carry):
        columns = pl.ds(pl.multiple_of(number * 2 * LANES, 2 * LANES), 2 * LANES)
        total[:, columns] = dot_transposed(projected_grad[...], w_qkv[columns, :])
        return carry

    lax.fori_loop(0, model_width // (2 * LANES), column_step, 0)
    write_parts(place, total, [part.at[:span] for part in parts[:-1]] + [parts[-1]], span)
    for copy in mixture_copies:
        copy.wait()


def attend_grad_kernel(
    place, layer_in, gain, projected_grad, attended, branch_grad, kept, given, normed
):
    token_count, model_width = layer_in.shape
    for row in range(0, token_count, ROWS):
        rows = pl.ds(row, ROWS)
        values = layer_in[rows, :].astype(jnp.float32)
        scale = lax.rsqrt(jnp.mean(values * values, axis=-1, keepdims=True) + epsilon)
        normed[rows, :] = (values * scale * gain[...]).astype(jnp.bfloat16)
    width = projected_grad.shape[1]
    blocks = []
    for row in range(0, model_width, attended.shape[1]):
        lanes = pl.ds(row, attended.shape[1])
        blocks.append((normed, lanes, projected_grad, pl.ds(0, width)))
    for lane in range(0, model_width, width):
        blocks.append((attended, pl.ds(0, attended.shape[1]), branch_grad, pl.ds(lane, width)))
    half = len(blocks) // 2
    for number, (left, left_lanes, right, right_lanes) in enumerate(blocks):
        rows = pl.ds(number % half * attended.shape[1], attended.shape[1])
        grad = transposed_dot(left[:, left_lanes], right[:, right_lanes])
        mine = (place[1] & 1) == number // half

        @pl.when(mine)
        def _():
            kept[rows, :] = grad

        @pl.when(jnp.logical_not(mine))
        def _():
            given[rows, :] = grad.astype(jnp.bfloat16)


def norm_back_kernel(own, near, far, residual, inverse, gain, out_grad, residual_grad, low_grad):
    summed = own[...] + near[...].astype(jnp.float32) + far[...].astype(jnp.float32)
    total = out_grad[...].astype(jnp.float32) + rms_backward(
        residual[...], inverse[...], gain[...], summed
    )
    residual_grad[...] = total
    low_grad[...] = total.astype(jnp.bfloat16)


def finish_kernel(own, near, far, layer_in, gain, residual_grad, residual, block):
    span = layer_in.shape[0]
    summed = own[...] + near[...].astype(jnp.float32) + far[...].astype(jnp.float32)
    values = layer_in[...].astype(jnp.float32)
    inverse = lax.rsqrt(jnp.mean(values * values, axis=-1, keepdims=True) + epsilon)
    block[:span, :] = (residual[...] + summed[span:]).astype(jnp.bfloat16)
    block[span : 2 * span, :] = (
        residual_grad[...] + rms_backward(values, inverse, gain[...], summed[:span])
    ).astype(jnp.bfloat16)


def in_vmem(count):
    return [pl.BlockSpec(memory_space=pltpu.VMEM)] * count


def in_hbm(count):
    return [pl.BlockSpec(memory_space=pltpu.HBM)] * count


def in_smem(count):
    return [pl.BlockSpec(memory_space=pltpu.SMEM)] * count


def shaped(shape, dtype):
    return jax.ShapeDtypeStruct(shape, dtype)


def on_device(
    layer_in,
    seq_lengths,
    routes,
    gain_attn,
    w_qkv,
    w_output,
    gain_ffn,
    w_router,
    w_in,
    w_out,
    out_grad,
):
    low, wide = jnp.bfloat16, jnp.float32
    token_count, model_width = layer_in.shape
    kv_here = w_qkv.shape[1]
    experts_all = w_router.shape[1]
    units = w_out.shape[1]
    head_width = kv_here * LANES
    block_count = token_count // ROWS
    tensor_count = lax.axis_size("tensor")
    span = token_count // tensor_count
    tensor_here = lax.axis_index("tensor")
    place = jnp.stack([tensor_here, lax.axis_index("expert")]).astype(jnp.int32)
    mib = 1 << 20

    def token_block(array_in):
        return lax.dynamic_slice_in_dim(array_in, tensor_here * span, span, 0)

    def in_order(blocks):
        joined = jnp.zeros((token_count,) + blocks[0].shape[1:], blocks[0].dtype)
        for number, block in enumerate(blocks):
            joined = lax.dynamic_update_slice_in_dim(
                joined, block, (tensor_here ^ number) * span, 0
            )
        return joined

    core = lax.axis_index("expert") & 1
    half = w_output.shape[0] // 2
    output_own = jnp.where(core == 0, w_output[:half], w_output[half:])
    output_far = exchange(output_own, "tensor", 2)
    output_near = exchange(output_own, "tensor", 1)
    w_in_own, w_out_own = w_in.reshape(2 * units, model_width), w_out[0]
    w_in_near = exchange(w_in_own, "expert", 2)
    w_out_near = exchange(w_out_own, "expert", 4)

    cosine, sine = angle_tables(token_count)
    qkv_flat = w_qkv.reshape(model_width, -1)
    kept = (
        shaped((kv_here, block_count, 2 * ROWS, LANES), low),
        shaped((kv_here, token_count, LANES), low),
        shaped((kv_here, block_count, 2 * ROWS, token_count), low),
    )
    queries, pairs, probs, attended = pl.pallas_call(
        attend_kernel,
        out_shape=kept + (shaped((token_count, head_width), low),),
        in_specs=in_smem(1) + in_vmem(5),
        out_specs=tuple(in_hbm(3) + in_vmem(1)),
        scratch_shapes=[pltpu.VMEM((token_count, model_width), low)]
        + [pltpu.VMEM(each.shape, low) for each in kept]
        + [pltpu.SemaphoreType.DMA((2 + block_count,))],
        compiler_params=pltpu.CompilerParams(vmem_limit_bytes=46 * mib),
        name="attend",
    )(seq_lengths, layer_in, gain_attn[None], qkv_flat, cosine, sine)

    w_in_near, w_out_near, output_far, output_near, attended = lax.optimization_barrier(
        (w_in_near, w_out_near, output_far, output_near, attended)
    )
    w_in_near = jnp.concatenate([w_in_own, w_in_near])
    w_out_near = jnp.concatenate([w_out_own, w_out_near])
    w_in_far = exchange(w_in_near, "expert", 4)
    w_out_far = exchange(w_out_near, "expert", 2)
    heads_far = exchange(attended, "tensor", 2)
    heads_near = exchange(attended, "tensor", 1)
    output_both = exchange(output_far, "tensor", 1)
    heads_far, heads_near, w_in_near, w_out_near, output_both = lax.optimization_barrier(
        (heads_far, heads_near, w_in_near, w_out_near, output_both)
    )
    heads_both = exchange(heads_far, "tensor", 1)
    heads_both, w_in_far, w_out_far = lax.optimization_barrier((heads_both, w_in_far, w_out_far))
    w_in_all = gather_pairs(w_in_near, w_in_far)
    w_out_all = gather_pairs(w_out_near, w_out_far)
    heads_all = [attended, heads_near, heads_far, heads_both]
    output_mine = jnp.concatenate([output_own, output_near, output_far, output_both])
    output_other = exchange(output_mine, "expert", 1)
    router_rows = jnp.pad(jnp.transpose(w_router), ((0, LANES - experts_all), (0, 0)))
    part_shapes = (shaped((span, model_width), wide),) + (
        shaped((span, model_width), low),
    ) * (tensor_count - 1)
    residual_all, inverse_all, normed_two, gates = pl.pallas_call(
        branch_kernel,
        out_shape=(
            shaped((token_count, model_width), wide),
            shaped((token_count, 1), wide),
            shaped((token_count, model_width), low),
            shaped((token_count, LANES), wide),
        ),
        in_specs=in_smem(1) + in_vmem(7),
        out_specs=tuple(in_vmem(4)),
        scratch_shapes=[pltpu.VMEM((model_width, model_width), low)],
        compiler_params=pltpu.CompilerParams(vmem_limit_bytes=12 * mib),
        name="branch",
    )(
        place,
        gain_ffn[None],
        router_rows,
        routes,
        layer_in,
        output_mine,
        output_other,
        jnp.concatenate(heads_all, 1),
    )
    middle = pl.pallas_call(
        functools.partial(middle_kernel, tensor_count),
        out_shape=part_shapes
        + (
            shaped((span, model_width), wide),
            shaped((span, 1), wide),
            shaped((token_count, experts_all * units), low),
            shaped((token_count, experts_all * 2 * units), low),
            shaped((1, model_width), wide),
            shaped((experts_all, model_width), wide),
        ),
        in_specs=in_smem(1) + in_vmem(14),
        out_specs=tuple(in_vmem(tensor_count + 6)),
        scratch_shapes=[
            pltpu.VMEM((token_count, units), wide),
            pltpu.VMEM((token_count, units), low),
            pltpu.VMEM((token_count, 2 * units), wide),
            pltpu.VMEM((token_count, experts_all * units), wide),
            pltpu.VMEM((token_count, model_width), wide),
        ],
        compiler_params=pltpu.CompilerParams(vmem_limit_bytes=24 * mib),
        name="middle",
    )(
        place,
        router_rows,
        out_grad,
        residual_all,
        inverse_all,
        normed_two,
        gates,
        *w_in_all,
        *w_out_all,
    )
    normed_parts, middle = middle[:tensor_count], middle[tensor_count:]
    residual, inverse_two, active, pre_grad, gain_ffn_part, router_part = middle

    relayed = exchange(normed_parts[3], "tensor", 1)
    half_grads = shaped((experts_all // 2 * 3 * units, model_width), low)
    late = pl.pallas_call(
        functools.partial(weight_grad_kernel, tensor_count),
        out_shape=part_shapes + (half_grads,) * 2,
        in_specs=in_smem(1) + in_vmem(8),
        out_specs=tuple(in_vmem(tensor_count + 2)),
        scratch_shapes=[pltpu.VMEM((token_count, model_width), wide)],
        compiler_params=pltpu.CompilerParams(vmem_limit_bytes=16 * mib),
        name="weight_grad",
    )(place, normed_two, out_grad, active, pre_grad, *w_out_all)
    late, relayed = lax.optimization_barrier((late, relayed))
    normed_pieces = scatter_parts(normed_parts, relayed)
    mixture_parts, kept_grads, given_grads = late[:tensor_count], late[-2], late[-1]
    given_grads = exchange(given_grads, "expert", 1)

    in_rows, out_rows = experts_all * units // 2, experts_all * units // 4
    in_kept, in_given, out_kept, out_given = pl.pallas_call(
        add_grads_kernel,
        out_shape=(
            shaped((in_rows, model_width), wide),
            shaped((in_rows, model_width), low),
            shaped((out_rows, model_width), wide),
            shaped((out_rows, model_width), low),
        ),
        in_specs=in_vmem(2),
        out_specs=tuple(in_vmem(4)),
        compiler_params=pltpu.CompilerParams(vmem_limit_bytes=16 * mib),
        name="add_grads",
    )(kept_grads, given_grads)
    residual, in_kept, in_given, out_kept, out_given = lax.optimization_barrier(
        (residual, in_kept, in_given, out_kept, out_given)
    )
    residual_grad, low_grad = pl.pallas_call(
        norm_back_kernel,
        out_shape=(shaped((span, model_width), wide), shaped((span, model_width), low)),
        in_specs=in_vmem(7),
        out_specs=tuple(in_vmem(2)),
        compiler_params=pltpu.CompilerParams(vmem_limit_bytes=6 * mib),
        name="norm_back",
    )(
        *normed_pieces,
        residual,
        inverse_two,
        gain_ffn[None],
        token_block(out_grad),
    )
    grad_blocks = gather_blocks(low_grad)

    in_arrived = exchange(in_given, "expert", 4)
    out_arrived = exchange(out_given, "expert", 2)
    mixture_last, *grad_blocks = lax.optimization_barrier((mixture_parts[3], *grad_blocks))
    mixture_relayed = exchange(mixture_last, "tensor", 1)
    fetched = (w_output, queries, pairs, probs, cosine, sine, qkv_flat)
    back = pl.pallas_call(
        functools.partial(attend_back_kernel, tensor_count),
        out_shape=(shaped((2 * span, model_width), wide),)
        + (shaped((2 * span, model_width), low),) * (tensor_count - 2)
        + (shaped((span, model_width), low),)
        + (
            shaped((token_count, model_width), low),
            shaped((token_count, 2 * head_width), low),
        ),
        in_specs=in_smem(1) + in_hbm(6 + 2 * tensor_count),
        out_specs=tuple(in_vmem(tensor_count + 2)),
        scratch_shapes=[
            pltpu.VMEM((token_count, head_width), wide),
            pltpu.VMEM((token_count, LANES), wide),
            pltpu.VMEM((token_count, model_width), wide),
        ]
        + [pltpu.VMEM(each.shape, each.dtype) for each in fetched]
        + [pltpu.SemaphoreType.DMA((len(fetched) + block_count + 2 * tensor_count,))],
        compiler_params=pltpu.CompilerParams(vmem_limit_bytes=58 * mib),
        name="attend_back",
    )(
        place,
        *fetched,
        *grad_blocks,
        *mixture_parts[:-1],
    )
    input_parts, (branch_grad, projected_grad) = (
        back[:tensor_count],
        back[tensor_count:],
    )
    *input_parts, projected_grad, in_arrived, out_arrived, mixture_relayed = (
        lax.optimization_barrier(
            (*input_parts, projected_grad, in_arrived, out_arrived, mixture_relayed)
        )
    )
    in_summed = in_kept + in_arrived.astype(wide)
    out_summed = out_kept + out_arrived.astype(wide)
    in_arrived = exchange(in_summed[in_rows // 2 :].astype(low), "expert", 2)
    out_arrived = exchange(out_summed[out_rows // 2 :].astype(low), "expert", 4)

    relayed = exchange(input_parts[3], "tensor", 1)
    row_count = (model_width + w_output.shape[0] * model_width // (2 * head_width)) // 2
    kept_sums, given_sums = pl.pallas_call(
        attend_grad_kernel,
        out_shape=(
            shaped((row_count, 2 * head_width), wide),
            shaped((row_count, 2 * head_width), low),
        ),
        in_specs=in_smem(1) + in_vmem(5),
        out_specs=tuple(in_vmem(2)),
        scratch_shapes=[pltpu.VMEM((token_count, model_width), low)],
        compiler_params=pltpu.CompilerParams(vmem_limit_bytes=12 * mib),
        name="attend_grad",
    )(place, layer_in, gain_attn[None], projected_grad, attended, branch_grad)
    relayed, kept_sums, given_sums, in_summed, out_summed = lax.optimization_barrier(
        (relayed, kept_sums, given_sums, in_summed, out_summed)
    )
    sums_half = kept_sums + exchange(given_sums, "expert", 1).astype(wide)
    sums = exchange_halves(sums_half.astype(low), (2, 4))
    input_pieces = scatter_parts(input_parts, jnp.concatenate([relayed, mixture_relayed]))
    residual, in_arrived, out_arrived, sums = lax.optimization_barrier(
        (residual, in_arrived, out_arrived, sums)
    )
    w_in_grad = (in_summed[: in_rows // 2] + in_arrived.astype(wide)).reshape(w_in.shape)
    w_out_grad = (out_summed[: out_rows // 2] + out_arrived.astype(wide)).reshape(w_out.shape)
    block = pl.pallas_call(
        finish_kernel,
        out_shape=shaped((2 * span, model_width), low),
        in_specs=in_vmem(7),
        out_specs=in_vmem(1)[0],
        compiler_params=pltpu.CompilerParams(vmem_limit_bytes=6 * mib),
        name="finish",
    )(
        *input_pieces,
        token_block(layer_in),
        gain_attn[None],
        residual_grad,
        residual,
    )
    far = exchange(block, "tensor", 2)
    near = exchange(block, "tensor", 1)
    small = jnp.concatenate([router_part, gain_ffn_part])
    sums, small, _ = lax.optimization_barrier((sums, small, block))
    small = sum_over_experts(small)
    summed = join_cores(exchange_halves(sums, (4, 2)))
    qkv_summed = summed[:model_width].reshape(w_qkv.shape)
    output_summed = jnp.concatenate(split_blocks(summed[model_width:], 0, 2), 1)

    gain_part = jnp.sum(
        qkv_flat.astype(wide) * summed[:model_width], 1
    ) / gain_attn
    small = jnp.concatenate([small, gain_part[None]])
    far, near = lax.optimization_barrier((far, near))
    for bit in (1, 2):
        small = small + exchange(small, "tensor", bit)
    both, qkv_summed, output_summed = lax.optimization_barrier(
        (exchange(far, "tensor", 1), qkv_summed, output_summed)
    )
    blocks = [block, near, far, both]
    layer_here = in_order([block[:span] for block in blocks])
    in_here = in_order([block[span:] for block in blocks])
    return (
        layer_here,
        in_here,
        small[experts_all + 1],
        qkv_summed,
        output_summed,
        small[experts_all],
        jnp.transpose(small[:experts_all]),
        w_in_grad,
        w_out_grad,
    )


def solution(mesh):
    fits = mesh.shape["tensor"] == 4 and mesh.shape["expert"] == 8
    placed = (
        P("expert", None),
        P("expert", None),
        P("expert", None),
        P(),
        P(None, "tensor", None),
        P("tensor", None),
        P(),
        P(),
        P("expert", None, "tensor", None),
        P("expert", "tensor", None),
        P("expert", None),
    )
    return jax.shard_map(
        on_device if fits else on_device_general,
        mesh=mesh,
        in_specs=placed,
        out_specs=(
            P("expert", None),
            P("expert", None),
            P(),
            P(None, "tensor", None),
            P("tensor", None),
            P(),
            P(),
            P("expert", None, "tensor", None),
            P("expert", "tensor", None),
        ),
        check_vma=False,
    )
```
